32 devices in a mesh: seq: 8 (over z, y), head: 4 (over x, core).
Axes of the slice: x: 2, y: 2, z: 4, core: 2. Of those that a mesh axis runs over, the one named last changes fastest.
Arguments:
- block_input: bfloat16 [4096, 2048], P('seq'), may hold values from -6 to 6
- cotangent: bfloat16 [4096, 2048], P('seq'), may hold values from -6 to 6
- lengths: int32 [2], replicated, may hold values from 1536 to 2560, as said below
- proj_master: float32 [4, 2048, 2048], P(None, 'seq', 'head'), may hold values from -0.125 to 0.125
- proj_first: float32 [4, 2048, 2048], P(None, 'seq', 'head'), as said below
- proj_second: float32 [4, 2048, 2048], P(None, 'seq', 'head'), as said below
- beta_master: float32 [2048, 16], P('seq', 'head'), may hold values from -0.125 to 0.125
- beta_first: float32 [2048, 16], P('seq', 'head'), may hold values from -224 to 224
- beta_second: float32 [2048, 16], P('seq', 'head'), may hold values from 5386.24 to 21544.96
- conv_master: float32 [3, 4, 2048], P(None, None, ('head', 'seq')), may hold values from -3 to 3
- conv_first: float32 [3, 4, 2048], P(None, None, ('head', 'seq')), as said below
- conv_second: float32 [3, 4, 2048], P(None, None, ('head', 'seq')), as said below
- out_master: float32 [2048, 2048], P('head', 'seq'), may hold values from -0.125 to 0.125
- out_first: float32 [2048, 2048], P('head', 'seq'), may hold values from -28 to 28
- out_second: float32 [2048, 2048], P('head', 'seq'), may hold values from 105.6768 to 421.888
- mlp_master: float32 [2, 2048, 5632], P(None, 'seq', 'head'), may hold values from -0.125 to 0.125
- mlp_first: float32 [2, 2048, 5632], P(None, 'seq', 'head'), may hold values from -12 to 12
- mlp_second: float32 [2, 2048, 5632], P(None, 'seq', 'head'), may hold values from 19.37408 to 77.4144
- down_master: float32 [5632, 2048], P('head', 'seq'), may hold values from -0.078125 to 0.078125
- down_first: float32 [5632, 2048], P('head', 'seq'), may hold values from -24 to 24
- down_second: float32 [5632, 2048], P('head', 'seq'), may hold values from 77.4144 to 310.0672
- gains_master: float32 [4224], P('seq'), may hold values from 0.5 to 1.5
- gains_first: float32 [4224], P('seq'), as said below
- gains_second: float32 [4224], P('seq'), as said below
Outputs:
- result: float32 [4096, 2048], P('seq')
- input_grad: float32 [4096, 2048], P('seq')
- proj_new: float32 [4, 2048, 2048], P(None, 'seq', 'head')
- proj_first_new: float32 [4, 2048, 2048], P(None, 'seq', 'head')
- proj_second_new: float32 [4, 2048, 2048], P(None, 'seq', 'head')
- proj_copy: bfloat16 [4, 2048, 2048], P(None, 'seq', 'head')
- beta_new: float32 [2048, 16], P('seq', 'head')
- beta_first_new: float32 [2048, 16], P('seq', 'head')
- beta_second_new: float32 [2048, 16], P('seq', 'head')
- beta_copy: bfloat16 [2048, 16], P('seq', 'head')
- conv_new: float32 [3, 4, 2048], P(None, None, ('head', 'seq'))
- conv_first_new: float32 [3, 4, 2048], P(None, None, ('head', 'seq'))
- conv_second_new: float32 [3, 4, 2048], P(None, None, ('head', 'seq'))
- conv_copy: bfloat16 [3, 4, 2048], P(None, None, ('head', 'seq'))
- out_new: float32 [2048, 2048], P('head', 'seq')
- out_first_new: float32 [2048, 2048], P('head', 'seq')
- out_second_new: float32 [2048, 2048], P('head', 'seq')
- out_copy: bfloat16 [2048, 2048], P('head', 'seq')
- mlp_new: float32 [2, 2048, 5632], P(None, 'seq', 'head')
- mlp_first_new: float32 [2, 2048, 5632], P(None, 'seq', 'head')
- mlp_second_new: float32 [2, 2048, 5632], P(None, 'seq', 'head')
- mlp_copy: bfloat16 [2, 2048, 5632], P(None, 'seq', 'head')
- down_new: float32 [5632, 2048], P('head', 'seq')
- down_first_new: float32 [5632, 2048], P('head', 'seq')
- down_second_new: float32 [5632, 2048], P('head', 'seq')
- down_copy: bfloat16 [5632, 2048], P('head', 'seq')
- gains_new: float32 [4224], P('seq')
- gains_first_new: float32 [4224], P('seq')
- gains_second_new: float32 [4224], P('seq')
The draws below stay inside these ranges and needn't reach their ends.
Inputs may be any that keep to these rules, and one draw needn't show every extreme that they name: lengths of sequence 0 and sequence 1 in order; both are multiples of 64 and they sum to 4096. `proj_first`: an optimizer state of both signs. `proj_second`: an optimizer state, positive. `conv_first`: an optimizer state of both signs. `conv_second`: an optimizer state, positive. `gains_first`: an optimizer state of both signs. `gains_second`: an optimizer state, positive.
All inputs are finite; a program needn't handle non-finite values.
Results may differ from the reference program's by a relative error of at most 0.024.
Values may be sent and summed in bfloat16 or wider, within the bound.
No kernel may reach another device: no remote copies, remote signals or barrier semaphores. Data moves between devices by JAX's collectives and lax.ppermute only.
A program may use at most 320 MiB of HBM per device.

```python
import math
from functools import partial
import jax
import jax.numpy as jnp
from jax import lax

D = 2048
NH = 16
DK = 128
FF = 5632
CONV = 4
SPAN = 64
STEP = 10
TOKENS = 4096


def draw_lengths(key, part):
    key = jax.random.fold_in(key, 11)
    lowest = 3 * TOKENS // (8 * SPAN)
    highest = 5 * TOKENS // (8 * SPAN)
    first_len = jax.random.randint(key, (), lowest, highest + 1, dtype=jnp.int32) * SPAN
    return jnp.stack([first_len, TOKENS - first_len]).astype(jnp.int32)


def first_state(key, shape, sizes):
    noise = jax.random.truncated_normal(key, -4.0, 4.0, shape, jnp.float32)
    return noise * (sizes / 9.0) * jnp.float32(TOKENS) ** 0.5


def second_state(key, shape, sizes):
    spread = jax.random.uniform(key, shape, jnp.float32)
    return 0.0526 * sizes * sizes * jnp.float32(TOKENS) * jnp.exp(spread * jnp.log(4.0))


def proj_sizes():
    return jnp.array([0.07, 0.1, 0.75, 0.6], jnp.float32)[:, None, None]


def conv_sizes():
    return jnp.array([0.07, 0.1, 0.75], jnp.float32)[:, None, None]


def gains_sizes():
    index = jnp.arange(2 * D + DK, dtype=jnp.int32)
    return jnp.where(index < D, 1.1, jnp.where(index < 2 * D, 0.6, 2.9)).astype(jnp.float32)


def draw_proj_first(key, part):
    key = jax.random.fold_in(key, 21)
    return first_state(key, (4, D, D), proj_sizes())


def draw_proj_second(key, part):
    key = jax.random.fold_in(key, 22)
    return second_state(key, (4, D, D), proj_sizes())


def draw_conv_first(key, part):
    key = jax.random.fold_in(key, 23)
    return first_state(key, (3, CONV, D), conv_sizes())


def draw_conv_second(key, part):
    key = jax.random.fold_in(key, 24)
    return second_state(key, (3, CONV, D), conv_sizes())


def draw_gains_first(key, part):
    key = jax.random.fold_in(key, 25)
    return first_state(key, (2 * D + DK,), gains_sizes())


def draw_gains_second(key, part):
    key = jax.random.fold_in(key, 26)
    return second_state(key, (2 * D + DK,), gains_sizes())


def block_levels(rng, extent, cuts, low, high):
    def one(axis_at, parts):
        heights = jax.random.uniform(jax.random.fold_in(jax.random.fold_in(rng, 6), axis_at), (parts,), jnp.float32, low / len(cuts), high / len(cuts))
        return jnp.repeat(jnp.exp(heights), extent[axis_at] // parts).reshape((-1,) + (1,) * (len(extent) - axis_at - 1))

    factor_of = one(*cuts[0])
    for cut in cuts[1:]:
        factor_of = factor_of * one(*cut)
    return factor_of


def centred(own_key, shape, scale, limit, pieces=(), kind=jnp.bfloat16):
    drawn = scale * jax.random.normal(own_key, shape, jnp.float32)
    if pieces:
        drawn = drawn * block_levels(own_key, shape, pieces, -0.22, 0.18)
    return jnp.clip(drawn, -limit, limit).astype(kind)


def setup_inputs(seed: int = 0) -> dict:
    keys = jax.random.split(jax.random.key(seed), 25)
    block_input = centred(keys[0], (TOKENS, D), 1.0, 6.0, ((0, 8),))
    cotangent = centred(keys[1], (TOKENS, D), 1.0, 6.0, ((0, 8),))
    lengths = draw_lengths(jax.random.fold_in(keys[24], 71), 0)
    proj_master = centred(keys[3], (4, D, D), D ** -0.5, 0.125, ((1, 8), (2, 4)), jnp.float32)
    proj_first = draw_proj_first(jax.random.fold_in(keys[24], 71), 0)
    proj_second = draw_proj_second(jax.random.fold_in(keys[24], 71), 0)
    beta_master = centred(keys[6], (D, NH), D ** -0.5, 0.125, ((0, 8), (1, 4)), jnp.float32)
    beta_first = centred(keys[7], (D, NH), (0.55 * TOKENS ** 0.5), 224.0, ((0, 8), (1, 4)), jnp.float32)
    beta_second = jnp.clip(jnp.exp(math.log(21544.96) - 1.3862944 * jax.random.uniform(keys[8], (D, NH), jnp.float32) ** block_levels(keys[8], (D, NH), ((0, 8), (1, 4)), -0.2, 0.2)), 5386.24, 21544.96)
    conv_master = centred(keys[9], (3, CONV, D), CONV ** -0.5, 3.0, ((2, 32),), jnp.float32)
    conv_first = draw_conv_first(jax.random.fold_in(keys[24], 71), 0)
    conv_second = draw_conv_second(jax.random.fold_in(keys[24], 71), 0)
    out_master = centred(keys[12], (D, D), D ** -0.5, 0.125, ((0, 4), (1, 8)), jnp.float32)
    out_first = centred(keys[13], (D, D), (0.075 * TOKENS ** 0.5), 28.0, ((0, 4), (1, 8)), jnp.float32)
    out_second = jnp.clip(jnp.exp(math.log(421.888) - 1.3843545 * jax.random.uniform(keys[14], (D, D), jnp.float32) ** block_levels(keys[14], (D, D), ((0, 4), (1, 8)), -0.2, 0.2)), 105.6768, 421.888)
    mlp_master = centred(keys[15], (2, D, FF), D ** -0.5, 0.125, ((1, 8), (2, 4)), jnp.float32)
    mlp_first = centred(keys[16], (2, D, FF), (0.033 * TOKENS ** 0.5), 12.0, ((1, 8), (2, 4)), jnp.float32)
    mlp_second = jnp.clip(jnp.exp(math.log(77.4144) - 1.38523666 * jax.random.uniform(keys[17], (2, D, FF), jnp.float32) ** block_levels(keys[17], (2, D, FF), ((1, 8), (2, 4)), -0.2, 0.2)), 19.37408, 77.4144)
    down_master = centred(keys[18], (FF, D), FF ** -0.5, 0.078125, ((0, 4), (1, 8)), jnp.float32)
    down_first = centred(keys[19], (FF, D), (0.066 * TOKENS ** 0.5), 24.0, ((0, 4), (1, 8)), jnp.float32)
    down_second = jnp.clip(jnp.exp(math.log(310.0672) - 1.3876163 * jax.random.uniform(keys[20], (FF, D), jnp.float32) ** block_levels(keys[20], (FF, D), ((0, 4), (1, 8)), -0.2, 0.2)), 77.4144, 310.0672)
    gains_master = jnp.clip(1.0 + 0.1 * jax.random.normal(keys[21], (2 * D + DK,), jnp.float32), 0.5, 1.5)
    gains_first = draw_gains_first(jax.random.fold_in(keys[24], 71), 0)
    gains_second = draw_gains_second(jax.random.fold_in(keys[24], 71), 0)
    return {"block_input": block_input, "cotangent": cotangent, "lengths": lengths, "proj_master": proj_master, "proj_first": proj_first, "proj_second": proj_second, "beta_master": beta_master, "beta_first": beta_first, "beta_second": beta_second, "conv_master": conv_master, "conv_first": conv_first, "conv_second": conv_second, "out_master": out_master, "out_first": out_first, "out_second": out_second, "mlp_master": mlp_master, "mlp_first": mlp_first, "mlp_second": mlp_second, "down_master": down_master, "down_first": down_first, "down_second": down_second, "gains_master": gains_master, "gains_first": gains_first, "gains_second": gains_second}


HIGHEST_PREC = lax.Precision.HIGHEST
eps_norm = 1e-05
eps_unit = 1e-06
beta_one = 0.9
beta_two = 0.95
eps_adam = 1e-08
rate_matrix = 0.04
rate_beta = 0.12
rate_down = 0.03
rate_conv = 0.3
rate_gains = 0.4
decay_matrix = 0.1

@jax.custom_vjp
def low(v):
    return lax.optimization_barrier(v.astype(jnp.bfloat16)).astype(jnp.float32)

@jax.custom_vjp
def low_back(v):
    return v

def low_keep(v):
    return (low(v), None)

def low_pass(kept, grad):
    return (grad,)

def back_keep(v):
    return (v, None)

def back_low(kept, grad):
    return (low(grad),)
low.defvjp(low_keep, low_pass)
low_back.defvjp(back_keep, back_low)

def rms_norm(tensor, scale_gain):
    return tensor * lax.rsqrt(lax.optimization_barrier(jnp.mean(tensor * tensor, axis=-1, keepdims=True)) + eps_norm) * scale_gain

def gated(out_rows, gate_rows, gain_o):
    row_count, width_all = out_rows.shape
    per_head = out_rows.reshape(row_count, width_all // DK, DK)
    scaled = per_head * lax.rsqrt(lax.optimization_barrier(jnp.mean(per_head * per_head, axis=-1, keepdims=True)) + eps_norm)
    gating = jax.nn.silu(gate_rows.reshape(row_count, width_all // DK, DK))
    return (scaled * gain_o * gating).reshape(row_count, width_all)

def unit_heads(tensor):
    row_count, width_all = tensor.shape
    per_head = tensor.reshape(row_count, width_all // DK, DK)
    return per_head * lax.rsqrt(lax.optimization_barrier(jnp.sum(per_head * per_head, axis=-1, keepdims=True)) + eps_unit)

def mixing(valid, extended, conv_taps, logits):
    row_count = logits.shape[0]
    summed = jnp.zeros((3, row_count, extended.shape[2]), jnp.float32)
    for offset in range(CONV):
        summed = summed + conv_taps[:, offset][:, None, :] * extended[:, offset:offset + row_count] * valid[None, :, offset:offset + 1]
    activated = jax.nn.silu(summed)
    return (unit_heads(activated[0]), unit_heads(activated[1]), activated[2].reshape(row_count, -1, DK), jax.nn.sigmoid(logits))

def delta_rule(query_rows, key_rows, value_rows, beta_rows, reset_rows):
    token_count = query_rows.shape[0]
    seg_rows = math.gcd(token_count, 256)

    def advance(memory, element):
        q_row, k_row, v_row, b_row, r_row = element
        memory = memory * (1.0 - r_row)
        predicted = jnp.einsum('hvk,hk->hv', memory, k_row, precision=HIGHEST_PREC)
        change = b_row[:, None] * (v_row - predicted)
        memory = memory + change[:, :, None] * k_row[:, None, :]
        return (memory, jnp.einsum('hvk,hk->hv', memory, q_row, precision=HIGHEST_PREC))

    @jax.checkpoint
    def segment(memory, elements):
        return lax.scan(advance, memory, elements)

    def by_segment(tensor):
        return tensor.reshape((token_count // seg_rows, seg_rows) + tensor.shape[1:])
    initial = jnp.zeros((NH, DK, DK), jnp.float32)
    _, outputs = lax.scan(segment, initial, (by_segment(query_rows), by_segment(key_rows), by_segment(value_rows), by_segment(beta_rows), by_segment(reset_rows)))
    return outputs.reshape(token_count, NH * DK)

def project(x_rows, w_proj, w_beta, gain_a):
    hidden = low(rms_norm(x_rows, gain_a))
    projected = jnp.einsum('td,cde->cte', hidden, w_proj, precision=HIGHEST_PREC)
    pre_conv = low(low_back(projected[:3]))
    gate_rows = low_back(projected[3])
    logits = low_back(jnp.dot(hidden, w_beta, precision=HIGHEST_PREC))
    return (pre_conv, gate_rows, logits)

def finish(elements, w_out, w_mlp, w_down, gain_m, gain_o):
    x_rows, o_rows, g_rows = elements
    normed = low(gated(o_rows, g_rows, gain_o))
    x_one = x_rows + low_back(jnp.dot(normed, w_out, precision=HIGHEST_PREC))
    h_two = low(rms_norm(x_one, gain_m))
    gate_up = low_back(jnp.einsum('td,cdf->ctf', h_two, w_mlp, precision=HIGHEST_PREC))
    activated = low(jax.nn.silu(gate_up[0]) * gate_up[1])
    return x_one + jnp.dot(activated, w_down, precision=HIGHEST_PREC)

def forward(valid, reset_rows, x_full, proj_w, beta_w, conv_w, out_w, mlp_w, down_w, gains_w):
    w_proj = low(proj_w)
    w_beta = low(beta_w)
    w_conv = low(conv_w)
    w_out = low(out_w)
    w_mlp = low(mlp_w)
    w_down = low(down_w)
    gain_all = low(gains_w)
    gain_a = gain_all[:D]
    gain_m = gain_all[D:2 * D]
    gain_o = gain_all[2 * D:]
    token_count = x_full.shape[0]
    block_rows = math.gcd(token_count, 4096)
    blocks = token_count // block_rows
    x_blocks = x_full.reshape(blocks, block_rows, D)

    @jax.checkpoint
    def project_block(x_rows):
        return project(x_rows, w_proj, w_beta, gain_a)
    pre_conv, gate_rows, logits = lax.map(project_block, x_blocks)
    pre_conv = jnp.transpose(pre_conv, (1, 0, 2, 3)).reshape(3, token_count, D)
    extended = jnp.pad(pre_conv, ((0, 0), (CONV - 1, 0), (0, 0)))
    query_rows, key_rows, value_rows, beta_rows = jax.checkpoint(partial(mixing, valid))(extended, w_conv, logits.reshape(token_count, NH))
    mixed_rows = delta_rule(query_rows, key_rows, value_rows, beta_rows, reset_rows)

    @jax.checkpoint
    def finish_block(elements):
        return finish(elements, w_out, w_mlp, w_down, gain_m, gain_o)
    outputs = lax.map(finish_block, (x_blocks, mixed_rows.reshape(blocks, block_rows, D), gate_rows))
    return outputs.reshape(token_count, D)

def adam_update(master, first_m, second_m, gradient, step_rate, decay_rate):
    first_new = beta_one * first_m + (1.0 - beta_one) * gradient
    second_new = beta_two * second_m + (1.0 - beta_two) * gradient * gradient
    first_hat = first_new / (1.0 - beta_one ** STEP)
    second_hat = second_new / (1.0 - beta_two ** STEP)
    master_new = master - step_rate * (first_hat / (jnp.sqrt(second_hat) + eps_adam) + decay_rate * master)
    return (master_new, first_new, second_new)

def reference(block_input, cotangent, lengths, proj_master, proj_first, proj_second, beta_master, beta_first, beta_second, conv_master, conv_first, conv_second, out_master, out_first, out_second, mlp_master, mlp_first, mlp_second, down_master, down_first, down_second, gains_master, gains_first, gains_second):
    token_count = block_input.shape[0]
    token_pos = jnp.arange(token_count, dtype=jnp.int32)
    first_len = lengths[0].astype(jnp.int32)
    position = token_pos - first_len * (token_pos >= first_len).astype(jnp.int32)
    reach = CONV - 1 - jnp.arange(CONV, dtype=jnp.int32)
    valid = (position[:, None] >= reach[None, :]).astype(jnp.float32)
    reset_rows = ((token_pos == 0) | (token_pos == first_len)).astype(jnp.float32)
    result, pullback = jax.vjp(partial(forward, valid, reset_rows), block_input.astype(jnp.float32), proj_master, beta_master, conv_master, out_master, mlp_master, down_master, gains_master)
    grads = pullback(cotangent.astype(jnp.float32))
    input_grad = grads[0]
    proj_new, proj_first_new, proj_second_new = adam_update(proj_master, proj_first, proj_second, grads[1], rate_matrix, decay_matrix)
    beta_new, beta_first_new, beta_second_new = adam_update(beta_master, beta_first, beta_second, grads[2], rate_beta, decay_matrix)
    conv_new, conv_first_new, conv_second_new = adam_update(conv_master, conv_first, conv_second, grads[3], rate_conv, decay_matrix)
    out_new, out_first_new, out_second_new = adam_update(out_master, out_first, out_second, grads[4], rate_matrix, decay_matrix)
    mlp_new, mlp_first_new, mlp_second_new = adam_update(mlp_master, mlp_first, mlp_second, grads[5], rate_matrix, decay_matrix)
    down_new, down_first_new, down_second_new = adam_update(down_master, down_first, down_second, grads[6], rate_down, decay_matrix)
    gains_new, gains_first_new, gains_second_new = adam_update(gains_master, gains_first, gains_second, grads[7], rate_gains, 0.0)
    return (result, input_grad, proj_new, proj_first_new, proj_second_new, proj_new.astype(jnp.bfloat16), beta_new, beta_first_new, beta_second_new, beta_new.astype(jnp.bfloat16), conv_new, conv_first_new, conv_second_new, conv_new.astype(jnp.bfloat16), out_new, out_first_new, out_second_new, out_new.astype(jnp.bfloat16), mlp_new, mlp_first_new, mlp_second_new, mlp_new.astype(jnp.bfloat16), down_new, down_first_new, down_second_new, down_new.astype(jnp.bfloat16), gains_new, gains_first_new, gains_second_new)
```

```python
from functools import partial

import jax
import jax.numpy as jnp
from jax import lax
from jax.experimental import pallas as pl
from jax.experimental.pallas import tpu as pltpu
from jax.sharding import PartitionSpec as P

D = 2048
DK = 128
CONV = 4
SPAN = 64
STEP = 10

eps_norm = 1e-05
eps_unit = 1e-06
beta_one = 0.9
beta_two = 0.95
eps_adam = 1e-08
rate_matrix = 0.04
rate_beta = 0.12
rate_down = 0.03
rate_conv = 0.3
rate_gains = 0.4
decay_matrix = 0.1


SPANROWS = 128


def _mm(a, b):
    return jnp.dot(
        a.astype(jnp.bfloat16), b.astype(jnp.bfloat16), preferred_element_type=jnp.float32
    )


def _mm_nt(a, b):
    return lax.dot_general(
        a.astype(jnp.bfloat16),
        b.astype(jnp.bfloat16),
        (((1,), (1,)), ((), ())),
        preferred_element_type=jnp.float32,
    )


def _mm_tn(a, b):
    return lax.dot_general(
        a.astype(jnp.bfloat16),
        b.astype(jnp.bfloat16),
        (((0,), (0,)), ((), ())),
        preferred_element_type=jnp.float32,
    )


def _pair_masks():
    row = lax.broadcasted_iota(jnp.int32, (SPANROWS, SPANROWS), 0)
    col = lax.broadcasted_iota(jnp.int32, (SPANROWS, SPANROWS), 1)
    same = (row // SPAN) == (col // SPAN)
    return row, col, same


def _tap_masks(scal_ref, rows):
    edge, base = scal_ref[0], scal_ref[1]
    token = lax.broadcasted_iota(jnp.int32, (rows, DK), 0)
    after = token >= edge
    masks = [None]
    for shift in range(1, CONV):
        good = jnp.where(after, token - edge, token + base) >= shift
        masks.append(good.astype(jnp.float32))
    return masks


def _keep(scal_ref, span):
    edge, base = scal_ref[0], scal_ref[1]
    start = span * SPAN
    hit = (edge == start) | ((base + start) == 0)
    return jnp.where(hit, 0.0, 1.0).astype(jnp.float32)


def _convolved(ext_ref, pre, halo, taps, masks):
    rows = pre.shape[0]
    ext_ref[0:8] = halo[8:16].astype(jnp.float32)
    ext_ref[8 : 8 + rows] = pre.astype(jnp.float32)
    total = taps[CONV - 1 : CONV] * ext_ref[8 : 8 + rows]
    for shift in range(1, CONV):
        total = (
            total
            + taps[CONV - 1 - shift : CONV - shift]
            * ext_ref[8 - shift : 8 - shift + rows]
            * masks[shift]
        )
    return total


def _unit(act):
    return act * lax.rsqrt(jnp.sum(act * act, axis=-1, keepdims=True) + eps_unit)


def _column(table, index):
    lane = lax.broadcasted_iota(jnp.int32, table.shape, 1)
    return jnp.sum(jnp.where(lane == index, table, 0.0), axis=1, keepdims=True)


def _local_kernel(
    heads, scal_ref, pre_ref, halo_ref, taps_ref, logit_ref, q_ref, k_ref, w_ref, uv_ref, t_ref,
    bt_ref, pt_ref, ext_ref,
):
    rows = pre_ref.shape[1]
    pairs = rows // SPANROWS
    masks = _tap_masks(scal_ref, rows)
    row, col, same = _pair_masks()
    strict = same & (row > col)
    eye = (row == col).astype(jnp.float32)
    levels = []
    for bit in range(6):
        inside = ((row >> (bit + 1)) == (col >> (bit + 1))) & same
        levels.append(
            (inside & (((row >> bit) & 1) == 1) & (((col >> bit) & 1) == 0)).astype(jnp.float32)
        )
    logit = logit_ref[...]
    first_head = pl.program_id(0) * heads
    keys, lowers, sides = [], [], []
    for head in range(heads):
        lanes = slice(head * DK, (head + 1) * DK)
        beta = jax.nn.sigmoid(_column(logit, first_head + head))
        acts = []
        for part in range(3):
            mixed = _convolved(
                ext_ref.at[head * 3 + part], pre_ref[part, :, lanes], halo_ref[part, :, lanes],
                taps_ref[part, :, lanes], masks,
            )
            acts.append(mixed * jax.nn.sigmoid(mixed))
        query = _unit(acts[0])
        key = _unit(acts[1])
        q_ref[:, lanes] = query.astype(jnp.bfloat16)
        key_low = key.astype(jnp.bfloat16)
        k_ref[:, lanes] = key_low
        side = jnp.concatenate([beta * key, beta * acts[2]], axis=1).astype(jnp.bfloat16)
        for pair in range(pairs):
            part = slice(pair * SPANROWS, (pair + 1) * SPANROWS)
            gram = _mm_nt(key_low[part], key_low[part])
            lowers.append(jnp.where(strict, gram * beta[part], 0.0))
            sides.append(side[part])
        keys.append(key_low)
    inverses = [eye - low * levels[0] for low in lowers]
    for bit in range(1, 6):
        middle = [_mm(low * levels[bit], inv) for low, inv in zip(lowers, inverses)]
        inverses = [inv - _mm(inv, mid) for mid, inv in zip(middle, inverses)]
    carried = []
    w_all, uv_all = [], []
    for head in range(heads):
        lanes = slice(head * DK, (head + 1) * DK)
        w_rows, uv_rows = [], []
        for pair in range(pairs):
            part = slice(pair * SPANROWS, (pair + 1) * SPANROWS)
            inv = inverses[head * pairs + pair].astype(jnp.bfloat16)
            t_ref[part, lanes] = inv
            both = _mm(inv, sides[head * pairs + pair])
            w_part = both[:, :DK].astype(jnp.bfloat16)
            w_ref[part, lanes] = w_part
            uv_ref[part, lanes] = both[:, DK:]
            w_rows.append(w_part)
            uv_rows.append(both[:, DK:])
        w_all.append(w_rows)
        uv_all.append(uv_rows)
        carried.append(jnp.concatenate([jnp.zeros((DK, DK), jnp.float32), eye], axis=1))
    for span in range(rows // SPAN):
        keep = _keep(scal_ref, span)
        pair, half = divmod(span, SPANROWS // SPAN)
        part = slice(half * SPAN, (half + 1) * SPAN)
        for head in range(heads):
            state = carried[head] * keep
            w_part = w_all[head][pair][part]
            source = jnp.concatenate(
                [uv_all[head][pair][part], jnp.zeros((SPAN, DK), jnp.float32)], axis=1
            )
            change = source - _mm(w_part, state)
            carried[head] = state + _mm_tn(
                keys[head][span * SPAN : (span + 1) * SPAN], change
            )
    for head in range(heads):
        bt_ref[head] = carried[head][:, :DK]
        pt_ref[head] = carried[head][:, DK:].astype(jnp.bfloat16)


def _apply_kernel(
    heads, scal_ref, q_ref, k_ref, w_ref, uv_ref, state_ref, gate_ref, gain_ref, n_ref, o_ref,
    u_ref, s_ref,
):
    rows = q_ref.shape[0]
    pairs = rows // SPANROWS
    row, col, same = _pair_masks()
    lower = same & (row >= col)
    states = [state_ref[head].astype(jnp.float32) for head in range(heads)]
    moved = [[] for _ in range(heads)]
    crossed = [[] for _ in range(heads)]
    for span in range(rows // SPAN):
        keep = _keep(scal_ref, span)
        part = slice(span * SPAN, (span + 1) * SPAN)
        for head in range(heads):
            lanes = slice(head * DK, (head + 1) * DK)
            state = states[head] * keep
            state_low = state.astype(jnp.bfloat16)
            s_ref[head, span] = state_low
            both = _mm(
                jnp.concatenate([w_ref[part, lanes], q_ref[part, lanes]], axis=0), state_low
            )
            change = (uv_ref[part, lanes] - both[:SPAN]).astype(jnp.bfloat16)
            crossed[head].append(both[SPAN:])
            moved[head].append(change)
            states[head] = state + _mm_tn(k_ref[part, lanes], change)
    for head in range(heads):
        lanes = slice(head * DK, (head + 1) * DK)
        for pair in range(pairs):
            part = slice(pair * SPANROWS, (pair + 1) * SPANROWS)
            change = jnp.concatenate([moved[head][2 * pair], moved[head][2 * pair + 1]], axis=0)
            cross = jnp.concatenate([crossed[head][2 * pair], crossed[head][2 * pair + 1]], axis=0)
            u_ref[part, lanes] = change
            scores = jnp.where(lower, _mm_nt(q_ref[part, lanes], k_ref[part, lanes]), 0.0)
            out = cross + _mm(scores, change)
            o_ref[part, lanes] = out
            scaled = out * lax.rsqrt(jnp.mean(out * out, axis=-1, keepdims=True) + eps_norm)
            gate = gate_ref[part, lanes]
            n_ref[part, lanes] = (
                scaled * gain_ref[...] * (gate * jax.nn.sigmoid(gate))
            ).astype(jnp.bfloat16)


def _back_local_kernel(
    heads, scal_ref, dn_ref, gate_ref, gain_ref, o_ref, q_ref, k_ref, w_ref, dg_ref, dgo_ref,
    do_ref, p_ref, carry_ref,
):
    rows = q_ref.shape[0]
    pairs = rows // SPANROWS
    row, col, same = _pair_masks()
    lower = same & (row >= col)
    gain = gain_ref[...]
    grad_outs = [[] for _ in range(heads)]
    passed = [[] for _ in range(heads)]
    for head in range(heads):
        lanes = slice(head * DK, (head + 1) * DK)
        gain_sum = jnp.zeros((1, DK), jnp.float32)
        for pair in range(pairs):
            part = slice(pair * SPANROWS, (pair + 1) * SPANROWS)
            out = o_ref[part, lanes]
            gate = gate_ref[part, lanes]
            grad_n = dn_ref[part, lanes]
            inv = lax.rsqrt(jnp.mean(out * out, axis=-1, keepdims=True) + eps_norm)
            sig = jax.nn.sigmoid(gate)
            act = gate * sig
            scaled = out * inv
            with_gain = grad_n * gain
            dg_ref[part, lanes] = (
                with_gain * scaled * (sig * (1.0 + gate * (1.0 - sig)))
            ).astype(jnp.bfloat16)
            gain_sum = gain_sum + jnp.sum(grad_n * scaled * act, axis=0, keepdims=True)
            inner = with_gain * act
            grad_out = (
                inv * inner
                - out * (inv * inv * inv) * jnp.mean(inner * out, axis=-1, keepdims=True)
            ).astype(jnp.bfloat16)
            do_ref[part, lanes] = grad_out
            scores = jnp.where(lower, _mm_nt(q_ref[part, lanes], k_ref[part, lanes]), 0.0)
            through = _mm_tn(scores, grad_out)
            p_ref[part, lanes] = through
            grad_outs[head].append(grad_out)
            passed[head].append(through)
        dgo_ref[head] = jnp.broadcast_to(gain_sum, (8, DK))
    carried = [jnp.zeros((DK, DK), jnp.float32) for _ in range(heads)]
    for span in reversed(range(rows // SPAN)):
        keep = _keep(scal_ref, span)
        rows_in = slice(span * SPAN, (span + 1) * SPAN)
        pair, half = divmod(span, SPANROWS // SPAN)
        part = slice(half * SPAN, (half + 1) * SPAN)
        for head in range(heads):
            lanes = slice(head * DK, (head + 1) * DK)
            change = passed[head][pair][part] + _mm(k_ref[rows_in, lanes], carried[head])
            carried[head] = keep * (
                carried[head]
                + _mm_tn(q_ref[rows_in, lanes], grad_outs[head][pair][part])
                - _mm_tn(w_ref[rows_in, lanes], change)
            )
    for head in range(heads):
        carry_ref[head] = carried[head]


def _back_kernel(
    heads, scal_ref, pre_ref, halo_ref, taps_ref, logit_ref, q_ref, k_ref, w_ref, t_ref, u_ref,
    s_ref, do_ref, p_ref, above_ref, dpre_ref, tail_ref, dhalo_ref, dtaps_ref, dlogit_ref,
    ext_ref, pad_ref,
):
    rows = q_ref.shape[0]
    pairs = rows // SPANROWS
    masks = _tap_masks(scal_ref, rows)
    row, col, same = _pair_masks()
    lower = same & (row >= col)
    strict = same & (row > col)
    edge, base = scal_ref[0], scal_ref[1]
    token = lax.broadcasted_iota(jnp.int32, (rows + 8, DK), 0) - 8
    back_masks = []
    for shift in range(CONV):
        good = jnp.where(token + shift >= edge, token - edge, token + base) >= 0
        back_masks.append(good.astype(jnp.float32))
    logit = logit_ref[...]
    first_head = pl.program_id(0) * heads
    carried = [above_ref[head].astype(jnp.float32) for head in range(heads)]
    changes = [[None] * (rows // SPAN) for _ in range(heads)]
    crossed = [[None] * (rows // SPAN) for _ in range(heads)]
    for span in reversed(range(rows // SPAN)):
        keep = _keep(scal_ref, span)
        part = slice(span * SPAN, (span + 1) * SPAN)
        for head in range(heads):
            lanes = slice(head * DK, (head + 1) * DK)
            above = carried[head].astype(jnp.bfloat16)
            change = (p_ref[part, lanes] + _mm(k_ref[part, lanes], above)).astype(jnp.bfloat16)
            changes[head][span] = change
            crossed[head][span] = _mm_nt(u_ref[part, lanes], above)
            carried[head] = keep * (
                carried[head]
                + _mm_tn(q_ref[part, lanes], do_ref[part, lanes])
                - _mm_tn(w_ref[part, lanes], change)
            )
    lane_index = lax.broadcasted_iota(jnp.int32, logit.shape, 1)
    grad_logit = jnp.zeros(logit.shape, jnp.float32)
    for head in range(heads):
        lanes = slice(head * DK, (head + 1) * DK)
        taps = taps_ref[:, :, lanes]
        beta = jax.nn.sigmoid(_column(logit, first_head + head))
        acts, slopes = [], []
        for which in range(3):
            mixed = _convolved(
                ext_ref.at[head * 3 + which], pre_ref[which, :, lanes], halo_ref[which, :, lanes],
                taps[which], masks,
            )
            sig = jax.nn.sigmoid(mixed)
            acts.append(mixed * sig)
            slopes.append(sig * (1.0 + mixed * (1.0 - sig)))
        query_inv = lax.rsqrt(jnp.sum(acts[0] * acts[0], axis=-1, keepdims=True) + eps_unit)
        key_inv = lax.rsqrt(jnp.sum(acts[1] * acts[1], axis=-1, keepdims=True) + eps_unit)
        query = acts[0] * query_inv
        key = acts[1] * key_inv
        value = acts[2]
        grad_q, grad_k, grad_v, grad_b = [], [], [], []
        for pair in range(pairs):
            part = slice(pair * SPANROWS, (pair + 1) * SPANROWS)
            spans = (2 * pair, 2 * pair + 1)
            q_low, k_low = q_ref[part, lanes], k_ref[part, lanes]
            u_low, do_low = u_ref[part, lanes], do_ref[part, lanes]
            change = jnp.concatenate([changes[head][span] for span in spans], axis=0)
            solved = _mm_tn(t_ref[part, lanes], change)
            solved_low = solved.astype(jnp.bfloat16)
            both = [
                _mm_nt(
                    jnp.concatenate(
                        [
                            do_low[half * SPAN : (half + 1) * SPAN],
                            solved_low[half * SPAN : (half + 1) * SPAN],
                        ],
                        axis=0,
                    ),
                    s_ref[head, span],
                )
                for half, span in enumerate(spans)
            ]
            out_state = jnp.concatenate([both[0][:SPAN], both[1][:SPAN]], axis=0)
            solved_state = jnp.concatenate([both[0][SPAN:], both[1][SPAN:]], axis=0)
            weights = jnp.where(lower, _mm_nt(do_low, u_low), 0.0).astype(jnp.bfloat16)
            grad_q.append(out_state + _mm(weights, k_low))
            grad_low = jnp.where(strict, -_mm_nt(solved_low, u_low), 0.0)
            gram = _mm_nt(k_low, k_low)
            beta_part = beta[part]
            grad_gram = (grad_low * beta_part).astype(jnp.bfloat16)
            grad_k.append(
                _mm_tn(weights, q_low)
                + jnp.concatenate([crossed[head][span] for span in spans], axis=0)
                - beta_part * solved_state
                + _mm(grad_gram, k_low)
                + _mm_tn(grad_gram, k_low)
            )
            grad_v.append(beta_part * solved)
            grad_b.append(
                jnp.sum(grad_low * gram, axis=1, keepdims=True)
                + jnp.sum(solved * value[part] - solved_state * key[part], axis=1, keepdims=True)
            )
        grad_query = jnp.concatenate(grad_q, axis=0)
        grad_key = jnp.concatenate(grad_k, axis=0)
        grad_beta = jnp.concatenate(grad_b, axis=0)
        grad_logit = grad_logit + jnp.where(
            lane_index == first_head + head, grad_beta * beta * (1.0 - beta), 0.0
        )
        grad_acts = [
            (grad_query - query * jnp.sum(query * grad_query, axis=-1, keepdims=True)) * query_inv,
            (grad_key - key * jnp.sum(key * grad_key, axis=-1, keepdims=True)) * key_inv,
            jnp.concatenate(grad_v, axis=0),
        ]
        for which in range(3):
            grad_mixed = grad_acts[which] * slopes[which]
            pad = pad_ref.at[head * 3 + which]
            ext = ext_ref.at[head * 3 + which]
            pad[0:8] = jnp.zeros((8, DK), jnp.float32)
            pad[8 : 8 + rows] = grad_mixed
            pad[8 + rows : 16 + rows] = jnp.zeros((8, DK), jnp.float32)
            total = jnp.zeros((rows + 8, DK), jnp.float32)
            for shift in range(CONV):
                tap = CONV - 1 - shift
                shifted = pad[shift : shift + rows + 8] * back_masks[shift]
                total = total + taps[which, tap : tap + 1] * shifted
                dtaps_ref[which, tap : tap + 1, lanes] = jnp.sum(
                    shifted * ext[0 : rows + 8], axis=0, keepdims=True
                )
            dhalo_ref[which, :, lanes] = total[:8]
            dpre_ref[which, :, lanes] = total[8:].astype(jnp.bfloat16)
            tail_ref[which, :, lanes] = total[rows:]

    @pl.when(pl.program_id(0) == 0)
    def _():
        dlogit_ref[...] = grad_logit

    @pl.when(pl.program_id(0) > 0)
    def _():
        dlogit_ref[...] += grad_logit


HEADS_AT_ONCE = 2


def _specs(heads, rows):
    wide = heads * DK
    return dict(
        scal=pl.BlockSpec(memory_space=pltpu.SMEM),
        flat=pl.BlockSpec((rows, wide), lambda h: (0, h)),
        three=pl.BlockSpec((3, rows, wide), lambda h: (0, 0, h)),
        halo=pl.BlockSpec((3, 16, wide), lambda h: (0, 0, h)),
        edge=pl.BlockSpec((3, 8, wide), lambda h: (0, 0, h)),
        taps=pl.BlockSpec((3, CONV, wide), lambda h: (0, 0, h)),
        square=pl.BlockSpec((heads, DK, DK), lambda h: (h, 0, 0)),
        spans=pl.BlockSpec((heads, rows // SPAN, DK, DK), lambda h: (h, 0, 0, 0)),
        gain=pl.BlockSpec((1, DK), lambda h: (0, 0)),
        small=pl.BlockSpec((heads, 8, DK), lambda h: (h, 0, 0)),
    )


def _params():
    return pltpu.CompilerParams(
        dimension_semantics=("arbitrary",), vmem_limit_bytes=48 * 1024 * 1024
    )


def delta_local(scal, pre, halo, taps, logits):
    _, rows, width = pre.shape
    total = width // DK
    heads = min(HEADS_AT_ONCE, total)
    sp = _specs(heads, rows)
    table = pl.BlockSpec((rows, total), lambda h: (0, 0))
    low = jax.ShapeDtypeStruct((rows, width), jnp.bfloat16)
    return pl.pallas_call(
        partial(_local_kernel, heads),
        grid=(total // heads,),
        in_specs=[sp["scal"], sp["three"], sp["halo"], sp["taps"], table],
        out_specs=[sp["flat"]] * 5 + [sp["square"]] * 2,
        out_shape=[
            low,
            low,
            low,
            jax.ShapeDtypeStruct((rows, width), jnp.float32),
            low,
            jax.ShapeDtypeStruct((total, DK, DK), jnp.float32),
            jax.ShapeDtypeStruct((total, DK, DK), jnp.bfloat16),
        ],
        scratch_shapes=[pltpu.VMEM((3 * heads, rows + 8, DK), jnp.float32)],
        compiler_params=_params(),
        cost_estimate=pl.CostEstimate(flops=2 * 10**9, bytes_accessed=8 * 10**6, transcendentals=0),
        name="delta_local",
    )(scal, pre, halo, taps, logits)


def delta_apply(scal, q, k, w, uv, state_in, gate, gain):
    rows, width = q.shape
    total = width // DK
    heads = min(HEADS_AT_ONCE, total)
    sp = _specs(heads, rows)
    low = jax.ShapeDtypeStruct((rows, width), jnp.bfloat16)
    return pl.pallas_call(
        partial(_apply_kernel, heads),
        grid=(total // heads,),
        in_specs=[sp["scal"]] + [sp["flat"]] * 4 + [sp["square"], sp["flat"], sp["gain"]],
        out_specs=[sp["flat"]] * 3 + [sp["spans"]],
        out_shape=[
            low,
            jax.ShapeDtypeStruct((rows, width), jnp.float32),
            low,
            jax.ShapeDtypeStruct((total, rows // SPAN, DK, DK), jnp.bfloat16),
        ],
        compiler_params=_params(),
        cost_estimate=pl.CostEstimate(flops=2 * 10**9, bytes_accessed=8 * 10**6, transcendentals=0),
        name="delta_apply",
    )(scal, q, k, w, uv, state_in, gate, gain)


def delta_back_local(scal, dn, gate, gain, o, q, k, w):
    rows, width = q.shape
    total = width // DK
    heads = min(HEADS_AT_ONCE, total)
    sp = _specs(heads, rows)
    low = jax.ShapeDtypeStruct((rows, width), jnp.bfloat16)
    return pl.pallas_call(
        partial(_back_local_kernel, heads),
        grid=(total // heads,),
        in_specs=[sp["scal"], sp["flat"], sp["flat"], sp["gain"]] + [sp["flat"]] * 4,
        out_specs=[sp["flat"], sp["small"], sp["flat"], sp["flat"], sp["square"]],
        out_shape=[
            low,
            jax.ShapeDtypeStruct((total, 8, DK), jnp.float32),
            low,
            jax.ShapeDtypeStruct((rows, width), jnp.float32),
            jax.ShapeDtypeStruct((total, DK, DK), jnp.float32),
        ],
        compiler_params=_params(),
        cost_estimate=pl.CostEstimate(flops=2 * 10**9, bytes_accessed=8 * 10**6, transcendentals=0),
        name="delta_back_local",
    )(scal, dn, gate, gain, o, q, k, w)


def delta_back(scal, pre, halo, taps, logits, q, k, w, t, u, s, do, p, above):
    _, rows, width = pre.shape
    total = width // DK
    heads = min(HEADS_AT_ONCE, total)
    sp = _specs(heads, rows)
    table = pl.BlockSpec((rows, total), lambda h: (0, 0))
    edge = jax.ShapeDtypeStruct((3, 8, width), jnp.float32)
    return pl.pallas_call(
        partial(_back_kernel, heads),
        grid=(total // heads,),
        in_specs=[sp["scal"], sp["three"], sp["halo"], sp["taps"], table]
        + [sp["flat"]] * 5
        + [sp["spans"], sp["flat"], sp["flat"], sp["square"]],
        out_specs=[sp["three"], sp["edge"], sp["edge"], sp["taps"], table],
        out_shape=[
            jax.ShapeDtypeStruct((3, rows, width), jnp.bfloat16),
            edge,
            edge,
            jax.ShapeDtypeStruct((3, CONV, width), jnp.float32),
            jax.ShapeDtypeStruct((rows, total), jnp.float32),
        ],
        scratch_shapes=[
            pltpu.VMEM((3 * heads, rows + 8, DK), jnp.float32),
            pltpu.VMEM((3 * heads, rows + 16, DK), jnp.float32),
        ],
        compiler_params=_params(),
        cost_estimate=pl.CostEstimate(
            flops=4 * 10**9, bytes_accessed=12 * 10**6, transcendentals=0
        ),
        name="delta_back",
    )(scal, pre, halo, taps, logits, q, k, w, t, u, s, do, p, above)


def ring_order(count):
    return list(range(0, count, 2)) + list(range(count - 1, 0, -2))


def ring_pairs(count):
    order = ring_order(count)
    return [(order[place], order[(place + 1) % count]) for place in range(count)]


def send_up(value):
    return lax.ppermute(value, "seq", ring_pairs(lax.axis_size("seq")))


def send_down(value):
    return lax.ppermute(value, "seq", [(b, a) for a, b in ring_pairs(lax.axis_size("seq"))])


def ring_place():
    count = lax.axis_size("seq")
    index = lax.axis_index("seq")
    return jnp.where(index % 2 == 0, index // 2, count - (index + 1) // 2)


def to_ring(value):
    count = lax.axis_size("seq")
    piece = value.shape[-1] // count
    parts = [value[..., one * piece : (one + 1) * piece] for one in ring_order(count)]
    doubled = jnp.concatenate(parts + parts[:-1], axis=-1)
    return lax.dynamic_slice_in_dim(doubled, ring_place() * piece, count * piece, value.ndim - 1)


def from_ring(value):
    count = lax.axis_size("seq")
    piece = value.shape[-1] // count
    doubled = jnp.concatenate([value, value[..., : (count - 1) * piece]], axis=-1)
    start = lax.rem(count - ring_place(), count) * piece
    placed = lax.dynamic_slice_in_dim(doubled, start, count * piece, value.ndim - 1)
    order = ring_order(count)
    parts = []
    for one in range(count):
        place = order.index(one)
        parts.append(placed[..., place * piece : (place + 1) * piece])
    return jnp.concatenate(parts, axis=-1)


def ring_gather(first, second):
    count = lax.axis_size("seq")
    half = count // 2
    one = {0: first}
    two = {0: second}
    for step in range(1, half + 1):
        one[count - step] = send_up(one[(count - step + 1) % count])
        two[step] = send_down(two[step - 1])
        if step < half:
            one[step] = send_down(one[step - 1])
            two[count - step] = send_up(two[(count - step + 1) % count])
    late = (one[count - half + 1], two[half - 1])
    return [one[key] for key in range(count)], [two[key] for key in range(count)], late


def ring_scatter(first, second):
    count = lax.axis_size("seq")
    half = count // 2

    def low(value):
        return value.astype(jnp.bfloat16)

    one_up, one_down = low(first(half)), low(first(half + 1))
    two_up, two_down = low(second(half - 1)), low(second(half))
    for step in range(1, half):
        one_up = low(first(half - step) + send_up(one_up).astype(jnp.float32))
        two_down = low(second(half + step) + send_down(two_down).astype(jnp.float32))
        if step < half - 1:
            one_down = low(first(half + 1 + step) + send_down(one_down).astype(jnp.float32))
            two_up = low(second(half - 1 - step) + send_up(two_up).astype(jnp.float32))
    one = first(0) + send_up(one_up).astype(jnp.float32) + send_down(one_down).astype(jnp.float32)
    two = second(0) + send_up(two_up).astype(jnp.float32) + send_down(two_down).astype(jnp.float32)
    return one, two


def swap(value, axis, bit):
    count = lax.axis_size(axis)
    return lax.ppermute(value, axis, [(one, one ^ bit) for one in range(count)])


def gather_small(value):
    index = lax.axis_index("seq")
    held = value[None]
    bit = 1
    while bit < lax.axis_size("seq"):
        other = swap(held, "seq", bit)
        mine_first = (index & bit) == 0
        held = jnp.where(
            mine_first,
            jnp.concatenate([held, other], axis=0),
            jnp.concatenate([other, held], axis=0),
        )
        bit *= 2
    return held


def scatter_small(value):
    index = lax.axis_index("seq")
    held = value
    bit = lax.axis_size("seq") // 2
    while bit >= 1:
        low, high = held[: held.shape[0] // 2], held[held.shape[0] // 2 :]
        upper = (index & bit) != 0
        got = swap(jnp.where(upper, low, high), "seq", bit)
        held = jnp.where(upper, high, low) + got
        bit //= 2
    return held[0]


def own_half(value):
    rows = value.shape[0] // 2
    return lax.dynamic_slice_in_dim(value, (lax.axis_index("head") & 1) * rows, rows, 0)


def other_half(value):
    rows = value.shape[0] // 2
    return lax.dynamic_slice_in_dim(value, (1 - (lax.axis_index("head") & 1)) * rows, rows, 0)


def both_halves(value):
    other = swap(value, "head", 1)
    return jnp.where(
        (lax.axis_index("head") & 1) == 0,
        jnp.concatenate([value, other], axis=0),
        jnp.concatenate([other, value], axis=0),
    )


def summed_half(partial_rows):
    low = partial_rows.astype(jnp.bfloat16)
    pair = own_half(partial_rows) + swap(other_half(low), "head", 1).astype(jnp.float32)
    total = pair
    bit = 2
    while bit < lax.axis_size("head"):
        total = total + swap(total.astype(jnp.bfloat16), "head", bit).astype(jnp.float32)
        bit *= 2
    return total


def chunk_of(value, index):
    piece = value.shape[-1] // lax.axis_size("seq")
    return value[..., index * piece : (index + 1) * piece]


def dot(a, b):
    return jnp.dot(a, b, preferred_element_type=jnp.float32)


def dot_tn(a, b):
    return lax.dot_general(a, b, (((0,), (0,)), ((), ())), preferred_element_type=jnp.float32)


def dot_nt(a, b):
    return lax.dot_general(a, b, (((1,), (1,)), ((), ())), preferred_element_type=jnp.float32)


def after(values, others):
    return lax.optimization_barrier((values, others))[0]


def passed_along(value, steps):
    count = lax.axis_size("seq")
    leading, last = (max(0, -steps), min(count, count - steps))
    return lax.ppermute(
        value, "seq", [(source, source + steps) for source in range(leading, last)]
    )


def adam_update(master, first_m, second_m, gradient, step_rate, decay_rate):
    first_new = beta_one * first_m + (1.0 - beta_one) * gradient
    second_new = beta_two * second_m + (1.0 - beta_two) * gradient * gradient
    first_hat = first_new / (1.0 - beta_one**STEP)
    second_hat = second_new / (1.0 - beta_two**STEP)
    master_new = master - step_rate * (
        first_hat / (jnp.sqrt(second_hat) + eps_adam) + decay_rate * master
    )
    return (master_new, first_new, second_new)


def norm_back(rows, inv, gain, grad):
    weighted = grad * gain
    mean = jnp.mean(weighted * rows, axis=-1, keepdims=True)
    return inv * weighted - rows * (inv * inv * inv) * mean


def inverse_size(rows):
    return lax.rsqrt(jnp.mean(rows * rows, axis=-1, keepdims=True) + eps_norm)


def per_device(
    block_input, cotangent, lengths,
    proj_master, proj_first, proj_second,
    beta_master, beta_first, beta_second,
    conv_master, conv_first, conv_second,
    out_master, out_first, out_second,
    mlp_master, mlp_first, mlp_second,
    down_master, down_first, down_second,
    gains_master, gains_first, gains_second,
):
    bf16, f32 = jnp.bfloat16, jnp.float32
    count = lax.axis_size("seq")
    seq_index = lax.axis_index("seq")
    rows = block_input.shape[0]
    width = proj_master.shape[2]
    units = mlp_master.shape[2]
    shard = proj_master.shape[1]
    heads = width // DK
    scal = jnp.stack([lengths[0] - seq_index * rows, seq_index * rows]).astype(jnp.int32)
    qkv = jnp.transpose(proj_master[:3], (1, 0, 2)).reshape(shard, 3 * width).astype(bf16)
    wide = 3 * width // 2
    w_qkv_a, w_qkv_b, late = ring_gather(qkv[:, :wide], qkv[:, wide:])
    w_gate, w_out, late = ring_gather(
        *after((proj_master[3].astype(bf16), out_master.astype(bf16)), late)
    )
    cut = (units // 2 + DK - 1) // DK * DK
    down_low = down_master.astype(bf16)
    w_down_a, w_down_b, late = ring_gather(*after((down_low[:cut], down_low[cut:]), late))
    mlp_low = mlp_master.astype(bf16)
    w_mlp_g, w_mlp_u, late = ring_gather(*after((mlp_low[0], mlp_low[1]), late))
    sizes = [conv_master.size, beta_master.size, gains_master.size]
    packed = jnp.concatenate(
        [conv_master.reshape(-1), beta_master.reshape(-1), gains_master.reshape(-1)]
    ).astype(bf16)
    packed = jnp.pad(packed, (0, -packed.size % 2048))
    small = gather_small(packed)
    conv_all = small[:, : sizes[0]].reshape(count, 3, CONV, -1)
    taps = jnp.transpose(conv_all, (1, 2, 0, 3)).reshape(3, CONV, width).astype(f32)
    beta_all = small[:, sizes[0] : sizes[0] + sizes[1]].reshape(D, heads)
    gains_all = small[:, sizes[0] + sizes[1] : sum(sizes)].reshape(-1)
    columns = to_ring(
        jnp.concatenate([gains_all[: 2 * D].reshape(2, D), jnp.transpose(beta_all)], axis=0)
    )
    gain_a = columns[0:1].astype(f32)
    gain_m = columns[1:2].astype(f32)
    w_beta = columns[2:]
    gain_o = gains_all[2 * D :].astype(f32)[None]
    x_ring = to_ring(block_input)
    dy_ring = to_ring(cotangent)
    x_rows = x_ring.astype(f32)
    x_inv = inverse_size(x_rows)
    hidden = (x_rows * x_inv * gain_a).astype(bf16)
    logits = dot_nt(hidden, w_beta)

    def over_chunks(value, weights, order):
        total = None
        for one in order:
            term = dot(chunk_of(value, one), weights[one])
            total = term if total is None else total + term
        return total

    order = [0]
    for step in range(1, count // 2):
        order += [count - step, step]
    order.append(count // 2)
    pre = jnp.concatenate(
        [over_chunks(hidden, w_qkv_a, order), over_chunks(hidden, w_qkv_b, order)], axis=1
    ).astype(bf16)
    pre = jnp.transpose(pre.reshape(rows, 3, width), (1, 0, 2))
    halo = passed_along(pre[:, rows - 16 :], 1)
    q, k, w, uv, t, state_add, state_map = delta_local(scal, pre, halo, taps, logits)
    gate = over_chunks(hidden, w_gate, order)
    hops = -(-5 * count // 8) - 1
    state_in = passed_along(state_add.astype(bf16), 1)
    for _ in range(hops - 1):
        moved = jnp.einsum("hij,hjk->hik", state_map, state_in, preferred_element_type=f32)
        state_in = passed_along((moved + state_add).astype(bf16), 1)
    normed, out_rows, change, states = delta_apply(scal, q, k, w, uv, state_in, gate, gain_o)
    attn_part = jnp.concatenate([dot(normed, w_out[one]) for one in range(count)], axis=1)
    x_one = own_half(x_rows) + summed_half(attn_part)
    one_inv = inverse_size(x_one)
    h_two = both_halves((x_one * one_inv * gain_m).astype(bf16))
    grad_act_a = None
    grad_act_b = None
    for one in order:
        term_a = dot_nt(chunk_of(dy_ring, one), w_down_a[one])
        term_b = dot_nt(chunk_of(dy_ring, one), w_down_b[one])
        grad_act_a = term_a if grad_act_a is None else grad_act_a + term_a
        grad_act_b = term_b if grad_act_b is None else grad_act_b + term_b
    grad_act = jnp.concatenate([grad_act_a, grad_act_b], axis=1)
    gate_u = over_chunks(h_two, w_mlp_g, order)
    up_u = over_chunks(h_two, w_mlp_u, order)
    sig = jax.nn.sigmoid(gate_u)
    act = gate_u * sig
    act_low = (act * up_u).astype(bf16)
    grad_gate_u = (grad_act * up_u * (sig * (1.0 + gate_u * (1.0 - sig)))).astype(bf16)
    grad_up_u = (grad_act * act).astype(bf16)
    grad_h_part = jnp.concatenate(
        [
            dot_nt(grad_gate_u, w_mlp_g[one]) + dot_nt(grad_up_u, w_mlp_u[one])
            for one in range(count)
        ],
        axis=1,
    )
    grad_h_two = summed_half(grad_h_part)
    x_half_grad = norm_back(x_one, one_inv, gain_m, grad_h_two)
    grad_gain_m = 0.5 * jnp.sum(grad_h_two * x_one * one_inv, axis=0, keepdims=True)
    grad_x_one = own_half(dy_ring).astype(f32) + x_half_grad
    grad_attn = both_halves(grad_x_one.astype(bf16))
    down_a_sum, down_b_sum = ring_scatter(
        lambda one: dot_tn(act_low[:, :cut], chunk_of(dy_ring, one)),
        lambda one: dot_tn(act_low[:, cut:], chunk_of(dy_ring, one)),
    )
    mlp_g_sum, mlp_u_sum = ring_scatter(
        lambda one: dot_tn(chunk_of(h_two, one), grad_gate_u),
        lambda one: dot_tn(chunk_of(h_two, one), grad_up_u),
    )
    mlp_part = jnp.concatenate(
        [
            dot(act_low[:, :cut], w_down_a[one]) + dot(act_low[:, cut:], w_down_b[one])
            for one in range(count)
        ],
        axis=1,
    )
    result = from_ring(both_halves(x_one + summed_half(mlp_part)))
    grad_normed = sum(dot_nt(chunk_of(grad_attn, one), w_out[one]) for one in range(count))
    grad_gate, grad_gain_o, grad_out, through, carry = delta_back_local(
        scal, grad_normed, gate, gain_o, out_rows, q, k, w
    )
    gate_sum, out_sum = ring_scatter(
        lambda one: dot_tn(chunk_of(hidden, one), grad_gate),
        lambda one: dot_tn(normed, chunk_of(grad_attn, one)),
    )
    above = passed_along(carry.astype(bf16), -1)
    for _ in range(hops - 1):
        moved = jnp.einsum("hji,hjk->hik", state_map, above, preferred_element_type=f32)
        above = passed_along((moved + carry).astype(bf16), -1)
    grad_pre, tail, back_halo, grad_taps, grad_logits = delta_back(
        scal, pre, halo, taps, logits, q, k, w, t, change, states, grad_out, through, above
    )
    fixed = (tail + passed_along(back_halo, -1)).astype(bf16)
    grad_pre = lax.dynamic_update_slice_in_dim(grad_pre, fixed, rows - 8, 1)
    grad_qkv = jnp.transpose(grad_pre, (1, 0, 2)).reshape(rows, 3 * width)
    grad_logits = grad_logits.astype(bf16)
    qkv_a_sum, qkv_b_sum = ring_scatter(
        lambda one: dot_tn(chunk_of(hidden, one), grad_qkv[:, :wide]),
        lambda one: dot_tn(chunk_of(hidden, one), grad_qkv[:, wide:]),
    )
    grad_hidden = jnp.concatenate(
        [
            dot_nt(grad_qkv[:, :wide], w_qkv_a[one])
            + dot_nt(grad_qkv[:, wide:], w_qkv_b[one])
            + dot_nt(grad_gate, w_gate[one])
            for one in range(count)
        ],
        axis=1,
    ) + dot(grad_logits, w_beta)
    grad_gain_a = jnp.sum(grad_hidden * x_rows * x_inv, axis=0, keepdims=True)
    grad_hidden_half = summed_half(grad_hidden)
    grad_x_rest = norm_back(own_half(x_rows), own_half(x_inv), gain_a, grad_hidden_half)
    input_grad = from_ring(both_halves(grad_x_one + grad_x_rest))
    grad_beta = dot_tn(grad_logits, hidden)
    stacked = from_ring(jnp.concatenate([grad_gain_a, grad_gain_m, grad_beta], axis=0))
    grad_gains = jnp.concatenate(
        [stacked[:2].reshape(-1), jnp.sum(grad_gain_o[:, 0], axis=0)]
    ).reshape(count, -1)
    grad_conv = jnp.transpose(
        grad_taps.reshape(3, CONV, count, width // count), (2, 0, 1, 3)
    ).reshape(count, -1)
    grad_beta = jnp.transpose(stacked[2:]).reshape(count, -1)
    small_sum = scatter_small(jnp.concatenate([grad_conv, grad_beta, grad_gains], axis=1))
    gains_sum = small_sum[sizes[0] + sizes[1] :]
    bit = 1
    while bit < lax.axis_size("head"):
        gains_sum = gains_sum + swap(gains_sum, "head", bit)
        bit *= 2
    summed_conv = small_sum[: sizes[0]].reshape(conv_master.shape)
    summed_beta = small_sum[sizes[0] : sizes[0] + sizes[1]].reshape(beta_master.shape)
    qkv_sum = jnp.concatenate([qkv_a_sum, qkv_b_sum], axis=1).reshape(shard, 3, width)
    summed_proj = jnp.concatenate([jnp.transpose(qkv_sum, (1, 0, 2)), gate_sum[None]], axis=0)
    summed_mlp = jnp.stack([mlp_g_sum, mlp_u_sum])
    summed_down = jnp.concatenate([down_a_sum, down_b_sum], axis=0)
    proj_new, proj_first_new, proj_second_new = adam_update(
        proj_master, proj_first, proj_second, summed_proj, rate_matrix, decay_matrix
    )
    beta_new, beta_first_new, beta_second_new = adam_update(
        beta_master, beta_first, beta_second, summed_beta, rate_beta, decay_matrix
    )
    conv_new, conv_first_new, conv_second_new = adam_update(
        conv_master, conv_first, conv_second, summed_conv, rate_conv, decay_matrix
    )
    out_new, out_first_new, out_second_new = adam_update(
        out_master, out_first, out_second, out_sum, rate_matrix, decay_matrix
    )
    mlp_new, mlp_first_new, mlp_second_new = adam_update(
        mlp_master, mlp_first, mlp_second, summed_mlp, rate_matrix, decay_matrix
    )
    down_new, down_first_new, down_second_new = adam_update(
        down_master, down_first, down_second, summed_down, rate_down, decay_matrix
    )
    gains_new, gains_first_new, gains_second_new = adam_update(
        gains_master, gains_first, gains_second, gains_sum, rate_gains, 0.0
    )
    return (
        result,
        input_grad,
        proj_new, proj_first_new, proj_second_new, proj_new.astype(bf16),
        beta_new, beta_first_new, beta_second_new, beta_new.astype(bf16),
        conv_new, conv_first_new, conv_second_new, conv_new.astype(bf16),
        out_new, out_first_new, out_second_new, out_new.astype(bf16),
        mlp_new, mlp_first_new, mlp_second_new, mlp_new.astype(bf16),
        down_new, down_first_new, down_second_new, down_new.astype(bf16),
        gains_new, gains_first_new, gains_second_new,
    )


def solution(mesh):
    rows = P("seq", None)
    proj = P(None, "seq", "head")
    tall = P("seq", "head")
    conv = P(None, None, ("head", "seq"))
    flat = P("head", "seq")
    gains = P("seq")
    return jax.shard_map(
        per_device,
        mesh=mesh,
        in_specs=(rows, rows, P())
        + (proj,) * 3
        + (tall,) * 3
        + (conv,) * 3
        + (flat,) * 3
        + (proj,) * 3
        + (flat,) * 3
        + (gains,) * 3,
        out_specs=(rows, rows)
        + (proj,) * 4
        + (tall,) * 4
        + (conv,) * 4
        + (flat,) * 4
        + (proj,) * 4
        + (flat,) * 4
        + (gains,) * 3,
        check_vma=False,
    )
```

```python
from functools import partial

import jax
import jax.numpy as jnp
from jax import lax
from jax.experimental import pallas as pl
from jax.experimental.pallas import tpu as pltpu
from jax.sharding import PartitionSpec as P

D = 2048
DK = 128
CONV = 4
SPAN = 64
STEP = 10

eps_norm = 1e-05
eps_unit = 1e-06
beta_one = 0.9
beta_two = 0.95
eps_adam = 1e-08
rate_matrix = 0.04
rate_beta = 0.12
rate_down = 0.03
rate_conv = 0.3
rate_gains = 0.4
decay_matrix = 0.1


SPANROWS = 128


def _mm(a, b):
    return jnp.dot(
        a.astype(jnp.bfloat16), b.astype(jnp.bfloat16), preferred_element_type=jnp.float32
    )


def _mm_nt(a, b):
    return lax.dot_general(
        a.astype(jnp.bfloat16),
        b.astype(jnp.bfloat16),
        (((1,), (1,)), ((), ())),
        preferred_element_type=jnp.float32,
    )


def _mm_tn(a, b):
    return lax.dot_general(
        a.astype(jnp.bfloat16),
        b.astype(jnp.bfloat16),
        (((0,), (0,)), ((), ())),
        preferred_element_type=jnp.float32,
    )


def _pair_masks():
    row = lax.broadcasted_iota(jnp.int32, (SPANROWS, SPANROWS), 0)
    col = lax.broadcasted_iota(jnp.int32, (SPANROWS, SPANROWS), 1)
    same = (row // SPAN) == (col // SPAN)
    return row, col, same


def _tap_masks(scal_ref, rows):
    edge, base = scal_ref[0], scal_ref[1]
    token = lax.broadcasted_iota(jnp.int32, (rows, DK), 0)
    after = token >= edge
    masks = [None]
    for shift in range(1, CONV):
        good = jnp.where(after, token - edge, token + base) >= shift
        masks.append(good.astype(jnp.float32))
    return masks


def _keep(scal_ref, span):
    edge, base = scal_ref[0], scal_ref[1]
    start = span * SPAN
    hit = (edge == start) | ((base + start) == 0)
    return jnp.where(hit, 0.0, 1.0).astype(jnp.float32)


def _convolved(ext_ref, pre, halo, taps, masks):
    rows = pre.shape[0]
    ext_ref[0:8] = halo[8:16].astype(jnp.float32)
    ext_ref[8 : 8 + rows] = pre.astype(jnp.float32)
    total = taps[CONV - 1 : CONV] * ext_ref[8 : 8 + rows]
    for shift in range(1, CONV):
        total = (
            total
            + taps[CONV - 1 - shift : CONV - shift]
            * ext_ref[8 - shift : 8 - shift + rows]
            * masks[shift]
        )
    return total


def _unit(act):
    return act * lax.rsqrt(jnp.sum(act * act, axis=-1, keepdims=True) + eps_unit)


def _column(table, index):
    lane = lax.broadcasted_iota(jnp.int32, table.shape, 1)
    return jnp.sum(jnp.where(lane == index, table, 0.0), axis=1, keepdims=True)


def _local_kernel(
    heads, scal_ref, pre_q, pre_k, pre_v, halo_q, halo_k, halo_v, taps_ref, logit_ref, q_ref, k_ref,
    w_ref, uv_ref, t_ref, bt_ref, pt_ref, ext_ref,
):
    pre_refs, halo_refs = (pre_q, pre_k, pre_v), (halo_q, halo_k, halo_v)
    rows = pre_q.shape[0]
    pairs = rows // SPANROWS
    masks = _tap_masks(scal_ref, rows)
    row, col, same = _pair_masks()
    strict = same & (row > col)
    eye = (row == col).astype(jnp.float32)
    levels = []
    for bit in range(6):
        inside = ((row >> (bit + 1)) == (col >> (bit + 1))) & same
        levels.append(
            (inside & (((row >> bit) & 1) == 1) & (((col >> bit) & 1) == 0)).astype(jnp.float32)
        )
    logit = logit_ref[...]
    first_head = pl.program_id(0) * heads
    keys, lowers, sides = [], [], []
    for head in range(heads):
        lanes = slice(head * DK, (head + 1) * DK)
        beta = jax.nn.sigmoid(_column(logit, first_head + head))
        acts = []
        for part in range(3):
            mixed = _convolved(
                ext_ref.at[head * 3 + part], pre_refs[part][:, lanes], halo_refs[part][:, lanes],
                taps_ref[part, :, lanes], masks,
            )
            acts.append(mixed * jax.nn.sigmoid(mixed))
        query = _unit(acts[0])
        key = _unit(acts[1])
        q_ref[:, lanes] = query.astype(jnp.bfloat16)
        key_low = key.astype(jnp.bfloat16)
        k_ref[:, lanes] = key_low
        side = jnp.concatenate([beta * key, beta * acts[2]], axis=1).astype(jnp.bfloat16)
        for pair in range(pairs):
            part = slice(pair * SPANROWS, (pair + 1) * SPANROWS)
            gram = _mm_nt(key_low[part], key_low[part])
            lowers.append(jnp.where(strict, gram * beta[part], 0.0))
            sides.append(side[part])
        keys.append(key_low)
    inverses = [eye - low * levels[0] for low in lowers]
    for bit in range(1, 6):
        middle = [_mm(low * levels[bit], inv) for low, inv in zip(lowers, inverses)]
        inverses = [inv - _mm(inv, mid) for mid, inv in zip(middle, inverses)]
    carried = []
    w_all, uv_all = [], []
    for head in range(heads):
        lanes = slice(head * DK, (head + 1) * DK)
        w_rows, uv_rows = [], []
        for pair in range(pairs):
            part = slice(pair * SPANROWS, (pair + 1) * SPANROWS)
            inv = inverses[head * pairs + pair].astype(jnp.bfloat16)
            t_ref[part, lanes] = inv
            both = _mm(inv, sides[head * pairs + pair])
            w_part = both[:, :DK].astype(jnp.bfloat16)
            w_ref[part, lanes] = w_part
            uv_ref[part, lanes] = both[:, DK:]
            w_rows.append(w_part)
            uv_rows.append(both[:, DK:])
        w_all.append(w_rows)
        uv_all.append(uv_rows)
        carried.append(jnp.concatenate([jnp.zeros((DK, DK), jnp.float32), eye], axis=1))
    for span in range(rows // SPAN):
        keep = _keep(scal_ref, span)
        pair, half = divmod(span, SPANROWS // SPAN)
        part = slice(half * SPAN, (half + 1) * SPAN)
        for head in range(heads):
            state = carried[head] * keep
            w_part = w_all[head][pair][part]
            source = jnp.concatenate(
                [uv_all[head][pair][part], jnp.zeros((SPAN, DK), jnp.float32)], axis=1
            )
            change = source - _mm(w_part, state)
            carried[head] = state + _mm_tn(
                keys[head][span * SPAN : (span + 1) * SPAN], change
            )
    for head in range(heads):
        bt_ref[head] = carried[head][:, :DK]
        pt_ref[head] = carried[head][:, DK:].astype(jnp.bfloat16)


def _apply_kernel(
    heads, scal_ref, q_ref, k_ref, w_ref, uv_ref, state_ref, gate_ref, gain_ref, n_ref, o_ref,
    u_ref, s_ref,
):
    rows = q_ref.shape[0]
    pairs = rows // SPANROWS
    row, col, same = _pair_masks()
    lower = same & (row >= col)
    states = [state_ref[head].astype(jnp.float32) for head in range(heads)]
    moved = [[] for _ in range(heads)]
    crossed = [[] for _ in range(heads)]
    for span in range(rows // SPAN):
        keep = _keep(scal_ref, span)
        part = slice(span * SPAN, (span + 1) * SPAN)
        for head in range(heads):
            lanes = slice(head * DK, (head + 1) * DK)
            state = states[head] * keep
            state_low = state.astype(jnp.bfloat16)
            s_ref[head, span] = state_low
            both = _mm(
                jnp.concatenate([w_ref[part, lanes], q_ref[part, lanes]], axis=0), state_low
            )
            change = (uv_ref[part, lanes] - both[:SPAN]).astype(jnp.bfloat16)
            crossed[head].append(both[SPAN:])
            moved[head].append(change)
            states[head] = state + _mm_tn(k_ref[part, lanes], change)
    for head in range(heads):
        lanes = slice(head * DK, (head + 1) * DK)
        for pair in range(pairs):
            part = slice(pair * SPANROWS, (pair + 1) * SPANROWS)
            change = jnp.concatenate([moved[head][2 * pair], moved[head][2 * pair + 1]], axis=0)
            cross = jnp.concatenate([crossed[head][2 * pair], crossed[head][2 * pair + 1]], axis=0)
            u_ref[part, lanes] = change
            scores = jnp.where(lower, _mm_nt(q_ref[part, lanes], k_ref[part, lanes]), 0.0)
            out = cross + _mm(scores, change)
            o_ref[part, lanes] = out
            scaled = out * lax.rsqrt(jnp.mean(out * out, axis=-1, keepdims=True) + eps_norm)
            gate = gate_ref[part, lanes]
            n_ref[part, lanes] = (
                scaled * gain_ref[...] * (gate * jax.nn.sigmoid(gate))
            ).astype(jnp.bfloat16)


def _back_local_kernel(
    heads, scal_ref, dn_ref, gate_ref, gain_ref, o_ref, q_ref, k_ref, w_ref, dg_ref, dgo_ref,
    do_ref, p_ref, carry_ref,
):
    rows = q_ref.shape[0]
    pairs = rows // SPANROWS
    row, col, same = _pair_masks()
    lower = same & (row >= col)
    gain = gain_ref[...]
    grad_outs = [[] for _ in range(heads)]
    passed = [[] for _ in range(heads)]
    for head in range(heads):
        lanes = slice(head * DK, (head + 1) * DK)
        gain_sum = jnp.zeros((1, DK), jnp.float32)
        for pair in range(pairs):
            part = slice(pair * SPANROWS, (pair + 1) * SPANROWS)
            out = o_ref[part, lanes]
            gate = gate_ref[part, lanes]
            grad_n = dn_ref[part, lanes]
            inv = lax.rsqrt(jnp.mean(out * out, axis=-1, keepdims=True) + eps_norm)
            sig = jax.nn.sigmoid(gate)
            act = gate * sig
            scaled = out * inv
            with_gain = grad_n * gain
            dg_ref[part, lanes] = (
                with_gain * scaled * (sig * (1.0 + gate * (1.0 - sig)))
            ).astype(jnp.bfloat16)
            gain_sum = gain_sum + jnp.sum(grad_n * scaled * act, axis=0, keepdims=True)
            inner = with_gain * act
            grad_out = (
                inv * inner
                - out * (inv * inv * inv) * jnp.mean(inner * out, axis=-1, keepdims=True)
            ).astype(jnp.bfloat16)
            do_ref[part, lanes] = grad_out
            scores = jnp.where(lower, _mm_nt(q_ref[part, lanes], k_ref[part, lanes]), 0.0)
            through = _mm_tn(scores, grad_out)
            p_ref[part, lanes] = through
            grad_outs[head].append(grad_out)
            passed[head].append(through)
        dgo_ref[head] = jnp.broadcast_to(gain_sum, (8, DK))
    carried = [jnp.zeros((DK, DK), jnp.float32) for _ in range(heads)]
    for span in reversed(range(rows // SPAN)):
        keep = _keep(scal_ref, span)
        rows_in = slice(span * SPAN, (span + 1) * SPAN)
        pair, half = divmod(span, SPANROWS // SPAN)
        part = slice(half * SPAN, (half + 1) * SPAN)
        for head in range(heads):
            lanes = slice(head * DK, (head + 1) * DK)
            change = passed[head][pair][part] + _mm(k_ref[rows_in, lanes], carried[head])
            carried[head] = keep * (
                carried[head]
                + _mm_tn(q_ref[rows_in, lanes], grad_outs[head][pair][part])
                - _mm_tn(w_ref[rows_in, lanes], change)
            )
    for head in range(heads):
        carry_ref[head] = carried[head]


def _back_kernel(
    heads, scal_ref, pre_q, pre_k, pre_v, halo_q, halo_k, halo_v, taps_ref, logit_ref, q_ref, k_ref,
    w_ref, t_ref, u_ref, s_ref, do_ref, p_ref, above_ref, dpre_ref, tail_ref, dhalo_ref, dtaps_ref,
    dlogit_ref, ext_ref, pad_ref,
):
    pre_refs, halo_refs = (pre_q, pre_k, pre_v), (halo_q, halo_k, halo_v)
    rows = q_ref.shape[0]
    pairs = rows // SPANROWS
    masks = _tap_masks(scal_ref, rows)
    row, col, same = _pair_masks()
    lower = same & (row >= col)
    strict = same & (row > col)
    edge, base = scal_ref[0], scal_ref[1]
    token = lax.broadcasted_iota(jnp.int32, (rows + 8, DK), 0) - 8
    back_masks = []
    for shift in range(CONV):
        good = jnp.where(token + shift >= edge, token - edge, token + base) >= 0
        back_masks.append(good.astype(jnp.float32))
    logit = logit_ref[...]
    first_head = pl.program_id(0) * heads
    carried = [above_ref[head].astype(jnp.float32) for head in range(heads)]
    changes = [[None] * (rows // SPAN) for _ in range(heads)]
    crossed = [[None] * (rows // SPAN) for _ in range(heads)]
    for span in reversed(range(rows // SPAN)):
        keep = _keep(scal_ref, span)
        part = slice(span * SPAN, (span + 1) * SPAN)
        for head in range(heads):
            lanes = slice(head * DK, (head + 1) * DK)
            above = carried[head].astype(jnp.bfloat16)
            change = (p_ref[part, lanes] + _mm(k_ref[part, lanes], above)).astype(jnp.bfloat16)
            changes[head][span] = change
            crossed[head][span] = _mm_nt(u_ref[part, lanes], above)
            carried[head] = keep * (
                carried[head]
                + _mm_tn(q_ref[part, lanes], do_ref[part, lanes])
                - _mm_tn(w_ref[part, lanes], change)
            )
    lane_index = lax.broadcasted_iota(jnp.int32, logit.shape, 1)
    grad_logit = jnp.zeros(logit.shape, jnp.float32)
    for head in range(heads):
        lanes = slice(head * DK, (head + 1) * DK)
        taps = taps_ref[:, :, lanes]
        beta = jax.nn.sigmoid(_column(logit, first_head + head))
        acts, slopes = [], []
        for which in range(3):
            mixed = _convolved(
                ext_ref.at[head * 3 + which], pre_refs[which][:, lanes], halo_refs[which][:, lanes],
                taps[which], masks,
            )
            sig = jax.nn.sigmoid(mixed)
            acts.append(mixed * sig)
            slopes.append(sig * (1.0 + mixed * (1.0 - sig)))
        query_inv = lax.rsqrt(jnp.sum(acts[0] * acts[0], axis=-1, keepdims=True) + eps_unit)
        key_inv = lax.rsqrt(jnp.sum(acts[1] * acts[1], axis=-1, keepdims=True) + eps_unit)
        query = acts[0] * query_inv
        key = acts[1] * key_inv
        value = acts[2]
        grad_q, grad_k, grad_v, grad_b = [], [], [], []
        for pair in range(pairs):
            part = slice(pair * SPANROWS, (pair + 1) * SPANROWS)
            spans = (2 * pair, 2 * pair + 1)
            q_low, k_low = q_ref[part, lanes], k_ref[part, lanes]
            u_low, do_low = u_ref[part, lanes], do_ref[part, lanes]
            change = jnp.concatenate([changes[head][span] for span in spans], axis=0)
            solved = _mm_tn(t_ref[part, lanes], change)
            solved_low = solved.astype(jnp.bfloat16)
            both = [
                _mm_nt(
                    jnp.concatenate(
                        [
                            do_low[half * SPAN : (half + 1) * SPAN],
                            solved_low[half * SPAN : (half + 1) * SPAN],
                        ],
                        axis=0,
                    ),
                    s_ref[head, span],
                )
                for half, span in enumerate(spans)
            ]
            out_state = jnp.concatenate([both[0][:SPAN], both[1][:SPAN]], axis=0)
            solved_state = jnp.concatenate([both[0][SPAN:], both[1][SPAN:]], axis=0)
            weights = jnp.where(lower, _mm_nt(do_low, u_low), 0.0).astype(jnp.bfloat16)
            grad_q.append(out_state + _mm(weights, k_low))
            grad_low = jnp.where(strict, -_mm_nt(solved_low, u_low), 0.0)
            gram = _mm_nt(k_low, k_low)
            beta_part = beta[part]
            grad_gram = (grad_low * beta_part).astype(jnp.bfloat16)
            grad_k.append(
                _mm_tn(weights, q_low)
                + jnp.concatenate([crossed[head][span] for span in spans], axis=0)
                - beta_part * solved_state
                + _mm(grad_gram, k_low)
                + _mm_tn(grad_gram, k_low)
            )
            grad_v.append(beta_part * solved)
            grad_b.append(
                jnp.sum(grad_low * gram, axis=1, keepdims=True)
                + jnp.sum(solved * value[part] - solved_state * key[part], axis=1, keepdims=True)
            )
        grad_query = jnp.concatenate(grad_q, axis=0)
        grad_key = jnp.concatenate(grad_k, axis=0)
        grad_beta = jnp.concatenate(grad_b, axis=0)
        grad_logit = grad_logit + jnp.where(
            lane_index == first_head + head, grad_beta * beta * (1.0 - beta), 0.0
        )
        grad_acts = [
            (grad_query - query * jnp.sum(query * grad_query, axis=-1, keepdims=True)) * query_inv,
            (grad_key - key * jnp.sum(key * grad_key, axis=-1, keepdims=True)) * key_inv,
            jnp.concatenate(grad_v, axis=0),
        ]
        for which in range(3):
            grad_mixed = grad_acts[which] * slopes[which]
            pad = pad_ref.at[head * 3 + which]
            ext = ext_ref.at[head * 3 + which]
            pad[0:8] = jnp.zeros((8, DK), jnp.float32)
            pad[8 : 8 + rows] = grad_mixed
            pad[8 + rows : 16 + rows] = jnp.zeros((8, DK), jnp.float32)
            total = jnp.zeros((rows + 8, DK), jnp.float32)
            for shift in range(CONV):
                tap = CONV - 1 - shift
                shifted = pad[shift : shift + rows + 8] * back_masks[shift]
                total = total + taps[which, tap : tap + 1] * shifted
                dtaps_ref[which, tap : tap + 1, lanes] = jnp.sum(
                    shifted * ext[0 : rows + 8], axis=0, keepdims=True
                )
            dhalo_ref[which, :, lanes] = total[:8]
            dpre_ref[which, :, lanes] = total[8:].astype(jnp.bfloat16)
            tail_ref[which, :, lanes] = total[rows:]

    @pl.when(pl.program_id(0) == 0)
    def _():
        dlogit_ref[...] = grad_logit

    @pl.when(pl.program_id(0) > 0)
    def _():
        dlogit_ref[...] += grad_logit


HEADS_AT_ONCE = 2


def _specs(heads, rows):
    wide = heads * DK
    return dict(
        scal=pl.BlockSpec(memory_space=pltpu.SMEM),
        flat=pl.BlockSpec((rows, wide), lambda h: (0, h)),
        three=pl.BlockSpec((3, rows, wide), lambda h: (0, 0, h)),
        edge=pl.BlockSpec((3, 8, wide), lambda h: (0, 0, h)),
        taps=pl.BlockSpec((3, CONV, wide), lambda h: (0, 0, h)),
        square=pl.BlockSpec((heads, DK, DK), lambda h: (h, 0, 0)),
        spans=pl.BlockSpec((heads, rows // SPAN, DK, DK), lambda h: (h, 0, 0, 0)),
        gain=pl.BlockSpec((1, DK), lambda h: (0, 0)),
        small=pl.BlockSpec((heads, 8, DK), lambda h: (h, 0, 0)),
    )


def _three_specs(heads, rows, total):
    def one(tall, part):
        return pl.BlockSpec((tall, heads * DK), lambda h: (0, part * (total // heads) + h))

    return [one(rows, 0)] * 3 + [one(16, part) for part in range(3)]


def _cost(microseconds):
    return pl.CostEstimate(
        flops=microseconds * 11 * 10**8,
        bytes_accessed=microseconds * 36 * 10**5,
        transcendentals=0,
    )


def _params():
    return pltpu.CompilerParams(
        dimension_semantics=("arbitrary",), vmem_limit_bytes=48 * 1024 * 1024
    )


def delta_local(scal, pre, halo, taps, logits):
    rows, width = pre[0].shape
    total = width // DK
    heads = min(HEADS_AT_ONCE, total)
    sp = _specs(heads, rows)
    table = pl.BlockSpec((rows, total), lambda h: (0, 0))
    low = jax.ShapeDtypeStruct((rows, width), jnp.bfloat16)
    return pl.pallas_call(
        partial(_local_kernel, heads),
        grid=(total // heads,),
        in_specs=[sp["scal"]] + _three_specs(heads, rows, total) + [sp["taps"], table],
        out_specs=[sp["flat"]] * 5 + [sp["square"]] * 2,
        out_shape=[
            low,
            low,
            low,
            jax.ShapeDtypeStruct((rows, width), jnp.float32),
            low,
            jax.ShapeDtypeStruct((total, DK, DK), jnp.float32),
            jax.ShapeDtypeStruct((total, DK, DK), jnp.bfloat16),
        ],
        scratch_shapes=[pltpu.VMEM((3 * heads, rows + 8, DK), jnp.float32)],
        compiler_params=_params(),
        cost_estimate=_cost(11),
        name="delta_local",
    )(scal, *pre, halo, halo, halo, taps, logits)


def delta_apply(scal, q, k, w, uv, state_in, gate, gain):
    rows, width = q.shape
    total = width // DK
    heads = min(HEADS_AT_ONCE, total)
    sp = _specs(heads, rows)
    low = jax.ShapeDtypeStruct((rows, width), jnp.bfloat16)
    return pl.pallas_call(
        partial(_apply_kernel, heads),
        grid=(total // heads,),
        in_specs=[sp["scal"]] + [sp["flat"]] * 4 + [sp["square"], sp["flat"], sp["gain"]],
        out_specs=[sp["flat"]] * 3 + [sp["spans"]],
        out_shape=[
            low,
            jax.ShapeDtypeStruct((rows, width), jnp.float32),
            low,
            jax.ShapeDtypeStruct((total, rows // SPAN, DK, DK), jnp.bfloat16),
        ],
        compiler_params=_params(),
        cost_estimate=_cost(7),
        name="delta_apply",
    )(scal, q, k, w, uv, state_in, gate, gain)


def delta_back_local(scal, dn, gate, gain, o, q, k, w):
    rows, width = q.shape
    total = width // DK
    heads = min(HEADS_AT_ONCE, total)
    sp = _specs(heads, rows)
    low = jax.ShapeDtypeStruct((rows, width), jnp.bfloat16)
    return pl.pallas_call(
        partial(_back_local_kernel, heads),
        grid=(total // heads,),
        in_specs=[sp["scal"], sp["flat"], sp["flat"], sp["gain"]] + [sp["flat"]] * 4,
        out_specs=[sp["flat"], sp["small"], sp["flat"], sp["flat"], sp["square"]],
        out_shape=[
            low,
            jax.ShapeDtypeStruct((total, 8, DK), jnp.float32),
            low,
            jax.ShapeDtypeStruct((rows, width), jnp.float32),
            jax.ShapeDtypeStruct((total, DK, DK), jnp.float32),
        ],
        compiler_params=_params(),
        cost_estimate=_cost(9),
        name="delta_back_local",
    )(scal, dn, gate, gain, o, q, k, w)


def delta_back(scal, pre, halo, taps, logits, q, k, w, t, u, s, do, p, above):
    rows, width = pre[0].shape
    total = width // DK
    heads = min(HEADS_AT_ONCE, total)
    sp = _specs(heads, rows)
    table = pl.BlockSpec((rows, total), lambda h: (0, 0))
    edge = jax.ShapeDtypeStruct((3, 8, width), jnp.float32)
    return pl.pallas_call(
        partial(_back_kernel, heads),
        grid=(total // heads,),
        in_specs=[sp["scal"]]
        + _three_specs(heads, rows, total)
        + [sp["taps"], table]
        + [sp["flat"]] * 5
        + [sp["spans"], sp["flat"], sp["flat"], sp["square"]],
        out_specs=[sp["three"], sp["edge"], sp["edge"], sp["taps"], table],
        out_shape=[
            jax.ShapeDtypeStruct((3, rows, width), jnp.bfloat16),
            edge,
            edge,
            jax.ShapeDtypeStruct((3, CONV, width), jnp.float32),
            jax.ShapeDtypeStruct((rows, total), jnp.float32),
        ],
        scratch_shapes=[
            pltpu.VMEM((3 * heads, rows + 8, DK), jnp.float32),
            pltpu.VMEM((3 * heads, rows + 16, DK), jnp.float32),
        ],
        compiler_params=_params(),
        cost_estimate=_cost(17),
        name="delta_back",
    )(
        scal, *pre, halo, halo, halo, taps, logits, q, k, w, t, u, s, do, p, above
    )


def ring_order(count):
    return list(range(0, count, 2)) + list(range(count - 1, 0, -2))


def ring_pairs(count):
    order = ring_order(count)
    return [(order[place], order[(place + 1) % count]) for place in range(count)]


def send_up(value):
    return lax.ppermute(value, "seq", ring_pairs(lax.axis_size("seq")))


def send_down(value):
    return lax.ppermute(value, "seq", [(b, a) for a, b in ring_pairs(lax.axis_size("seq"))])


def ring_place():
    count = lax.axis_size("seq")
    index = lax.axis_index("seq")
    return jnp.where(index % 2 == 0, index // 2, count - (index + 1) // 2)


def ring_sources():
    count = lax.axis_size("seq")
    order = jnp.asarray(ring_order(count), jnp.int32)
    return jnp.take(order, (ring_place() + jnp.arange(count, dtype=jnp.int32)) % count)


def ring_targets():
    count = lax.axis_size("seq")
    order = ring_order(count)
    places = jnp.asarray([order.index(one) for one in range(count)], jnp.int32)
    return (places + count - ring_place()) % count


def _pick_kernel(pieces, index_ref, value_ref, out_ref):
    piece = out_ref.shape[1] // pieces
    for one in range(pieces):
        start = pl.multiple_of(index_ref[one] * piece, DK)
        out_ref[:, one * piece : (one + 1) * piece] = value_ref[:, pl.ds(start, piece)]


def _join_kernel(pieces, index_ref, own_ref, other_ref, out_ref):
    piece = out_ref.shape[1] // pieces
    own = (pl.program_id(0) >= pl.num_programs(0) // 2) == (index_ref[pieces] == 1)
    for one in range(pieces):
        start = pl.multiple_of(index_ref[one] * piece, DK)
        out_ref[:, one * piece : (one + 1) * piece] = jnp.where(
            own, own_ref[:, pl.ds(start, piece)], other_ref[:, pl.ds(start, piece)]
        )


def pick_columns(value, index):
    count = index.shape[0]
    rows, wide = value.shape
    piece = wide // count
    if piece % DK:
        return jnp.take(value.reshape(rows, count, piece), index, axis=1).reshape(rows, wide)
    tall = rows // 4
    return pl.pallas_call(
        partial(_pick_kernel, count),
        grid=(4,),
        in_specs=[
            pl.BlockSpec(memory_space=pltpu.SMEM),
            pl.BlockSpec((tall, wide), lambda i: (i, 0)),
        ],
        out_specs=pl.BlockSpec((tall, wide), lambda i: (i, 0)),
        out_shape=jax.ShapeDtypeStruct(value.shape, value.dtype),
        compiler_params=_params(),
        cost_estimate=_cost(3),
        name="pick_columns",
    )(index, value)


def join_columns(own, index):
    other = swap(own, "head", 1)
    bit = lax.axis_index("head") & 1
    count = index.shape[0]
    rows, wide = own.shape
    if (wide // count) % DK:
        both = jnp.where(
            bit == 0,
            jnp.concatenate([own, other], axis=0),
            jnp.concatenate([other, own], axis=0),
        )
        return pick_columns(both, index)
    tall = rows // 2
    half = pl.BlockSpec((tall, wide), lambda i: (i % 2, 0))
    return pl.pallas_call(
        partial(_join_kernel, count),
        grid=(4,),
        in_specs=[pl.BlockSpec(memory_space=pltpu.SMEM), half, half],
        out_specs=pl.BlockSpec((tall, wide), lambda i: (i, 0)),
        out_shape=jax.ShapeDtypeStruct((2 * rows, wide), own.dtype),
        compiler_params=_params(),
        cost_estimate=_cost(4),
        name="join_columns",
    )(jnp.concatenate([index, bit[None].astype(jnp.int32)]), own, other)


def low(value):
    return value.astype(jnp.bfloat16)


class Gather:
    def __init__(self, first, second):
        self.count = lax.axis_size("seq")
        self.half = self.count // 2
        self.held = ({0: first}, {0: second})

    def fresh(self, slot):
        return [self.held[slot]] if slot < 2 else []

    def send(self, slot):
        step, second = slot // 2 + 1, slot % 2
        held = self.held[second]
        back, forth = (self.count - step) % self.count, step
        keys = []
        if step < self.half or not second:
            held[back] = send_up(held[(back + 1) % self.count])
            keys.append((held, back))
        if step < self.half or second:
            held[forth] = send_down(held[forth - 1])
            keys.append((held, forth))
        return keys


class Scatter:
    def __init__(self, first, second):
        self.count = lax.axis_size("seq")
        self.half = self.count // 2
        self.terms = (first, second)
        self.got = ({}, {})

    def places(self, slot):
        step, second = slot // 2, slot % 2
        up = self.half - step - (1 if second else 0)
        down = self.half + step + (0 if second else 1)
        return up, down

    def fresh(self, slot):
        if slot > 1:
            return []
        self.first = {0: dict(zip(("up", "down"), map(self.terms[slot], self.places(slot))))}
        return [self.first]

    def send(self, slot):
        got = self.got[slot % 2]
        keys = []
        for way, send, place in zip(("up", "down"), (send_up, send_down), self.places(slot)):
            if 0 < place < self.count:
                if way in got:
                    term = self.terms[slot % 2](place)
                    term = low(term.astype(jnp.float32) + got[way].astype(jnp.float32))
                else:
                    term = self.first[0][way]
                got[way] = send(term)
                keys.append((got, way))
        return keys

    def sums(self):
        return [
            terms(0).astype(jnp.float32) + got["up"].astype(jnp.float32) + got["down"].astype(jnp.float32)
            for terms, got in zip(self.terms, self.got)
        ]


class Flow:
    def __init__(self):
        self.flying = []

    def step(self, ring, stage, values=()):
        each = lax.axis_size("seq") // 8
        for slot in range(stage * each, (stage + 1) * each):
            keys = self.flying.pop(0) if len(self.flying) > 1 else []
            arrived = [held[key] for held, key in keys]
            fresh = ring.fresh(slot)
            arrived, first, values = lax.optimization_barrier(
                (arrived, [held[0] for held in fresh], values)
            )
            for held, value in zip(fresh, first):
                held[0] = value
            for (held, key), value in zip(keys, arrived):
                held[key] = value
            self.flying.append(ring.send(slot))
        return values


def _rows_dot_kernel(count, operands, outs, *refs):
    size = len(operands)
    value_ref = refs[0]
    weights = [refs[1 + one * count : 1 + (one + 1) * count] for one in range(size)]
    out_refs = refs[1 + size * count : -1 - size]
    held = refs[-1 - size : -1]
    sems = refs[-1]

    def copy(one, place):
        first, columns = operands[one]
        piece = weights[one][place].shape[0]
        return pltpu.make_async_copy(
            weights[one][place].at[:, pl.ds(first, columns)],
            held[one].at[pl.ds(place * piece, piece)],
            sems.at[one, place],
        )

    for one in range(size):
        for place in range(count):
            copy(one, place).start()
    for one in range(size):
        for place in range(count):
            copy(one, place).wait()
        for source, start, columns, out, at in outs:
            if source == one:
                out_refs[out][:, at : at + columns] = jnp.dot(
                    value_ref[...],
                    held[one][:, start : start + columns],
                    preferred_element_type=jnp.float32,
                ).astype(out_refs[out].dtype)


def rows_dot(value, operands, outs, shapes):
    count = len(operands[0][0])
    vmem = pl.BlockSpec(memory_space=pltpu.VMEM)
    ranges = [(first, columns) for _, first, columns in operands]
    whole = [
        jax.ShapeDtypeStruct((value.shape[1], columns), jnp.bfloat16) for _, columns in ranges
    ]
    results = pl.pallas_call(
        partial(_rows_dot_kernel, count, ranges, outs),
        in_specs=[vmem] + [pl.BlockSpec(memory_space=pl.ANY)] * (len(operands) * count),
        out_specs=[vmem] * (len(shapes) + len(whole)),
        out_shape=list(shapes) + whole,
        scratch_shapes=[pltpu.SemaphoreType.DMA((len(operands), count))],
        compiler_params=pltpu.CompilerParams(vmem_limit_bytes=48 * 1024 * 1024),
        cost_estimate=_cost(12),
        name="rows_dot",
    )(value, *[pieces[place] for pieces, _, _ in operands for place in range(count)])
    return results[: len(shapes)], results[len(shapes) :]


def _glu_early_kernel(count, *refs):
    half = count // 2
    late = (half - 1, half, half + 1)
    value_ref = refs[0]
    weights = (refs[1 : 1 + count], refs[1 + count : 1 + 2 * count])
    outs = refs[1 + 2 * count : 3 + 2 * count]
    held = refs[3 + 2 * count : 5 + 2 * count]
    sems = refs[-1]
    piece = weights[0][0].shape[0]
    places = [place for place in range(count) if place not in late]

    def copy(one, place):
        return pltpu.make_async_copy(
            weights[one][place], held[one].at[pl.ds(place * piece, piece)], sems.at[one, place]
        )

    for one in range(2):
        for place in places:
            copy(one, place).start()
    stop, again = (half - 1) * piece, (half + 2) * piece
    for one in range(2):
        held[one][stop:again] = jnp.zeros((3 * piece, held[one].shape[1]), jnp.bfloat16)
    for one in range(2):
        for place in places:
            copy(one, place).wait()
        outs[one][...] = jnp.dot(
            value_ref[:, :stop], held[one][:stop], preferred_element_type=jnp.float32
        ) + jnp.dot(value_ref[:, again:], held[one][again:], preferred_element_type=jnp.float32)


def glu_early(value, gates, ups):
    count = lax.axis_size("seq")
    vmem = pl.BlockSpec(memory_space=pltpu.VMEM)
    columns = gates[0].shape[1]
    return pl.pallas_call(
        partial(_glu_early_kernel, count),
        in_specs=[vmem] + [pl.BlockSpec(memory_space=pl.ANY)] * (2 * count),
        out_specs=[vmem] * 4,
        out_shape=[jax.ShapeDtypeStruct((value.shape[0], columns), jnp.float32)] * 2
        + [jax.ShapeDtypeStruct((value.shape[1], columns), jnp.bfloat16)] * 2,
        scratch_shapes=[pltpu.SemaphoreType.DMA((2, count))],
        compiler_params=pltpu.CompilerParams(vmem_limit_bytes=52 * 1024 * 1024),
        cost_estimate=_cost(14),
        name="glu_early",
    )(
        value,
        *[gates.get(place, gates[0]) for place in range(count)],
        *[ups.get(place, ups[0]) for place in range(count)],
    )


def _glu_late_kernel(value_ref, *refs):
    gates_refs, ups_refs = refs[:3], refs[3:6]
    gate_ref, up_ref, grad_ref, act_ref, dgate_ref, dup_ref = refs[6:]
    columns = grad_ref.shape[1]
    piece = gates_refs[0].shape[0]
    wide = 256
    for start in range(0, columns, wide):
        part = slice(start, min(start + wide, columns))
        gate, up = gate_ref[:, part], up_ref[:, part]
        for one in range(3):
            value = value_ref[:, one * piece : (one + 1) * piece]
            gate = gate + jnp.dot(
                value, gates_refs[one][:, part], preferred_element_type=jnp.float32
            )
            up = up + jnp.dot(value, ups_refs[one][:, part], preferred_element_type=jnp.float32)
        grad = grad_ref[:, part]
        sig = jax.nn.sigmoid(gate)
        act = gate * sig
        act_ref[:, part] = low(act * up)
        dgate_ref[:, part] = low(grad * up * (sig * (1.0 + gate * (1.0 - sig))))
        dup_ref[:, part] = low(grad * act)


def glu_late(value, gates, ups, sums, grad):
    rows, columns = grad.shape
    tall = rows // 4

    def by_rows(wide):
        return pl.BlockSpec((tall, wide), lambda i: (i, 0))

    whole = pl.BlockSpec(gates[0].shape, lambda i: (0, 0))
    return pl.pallas_call(
        _glu_late_kernel,
        grid=(4,),
        in_specs=[by_rows(value.shape[1])] + [whole] * 6 + [by_rows(columns)] * 3,
        out_specs=[by_rows(columns)] * 3,
        out_shape=[jax.ShapeDtypeStruct(grad.shape, jnp.bfloat16)] * 3,
        compiler_params=_params(),
        cost_estimate=_cost(8),
        name="glu_late",
    )(value, *gates, *ups, *sums, grad)


def swap(value, axis, bit):
    count = lax.axis_size(axis)
    return lax.ppermute(value, axis, [(one, one ^ bit) for one in range(count)])


def gather_round(held, bit):
    other = swap(held, "seq", bit)
    return jnp.where(
        (lax.axis_index("seq") & bit) == 0,
        jnp.concatenate([held, other], axis=0),
        jnp.concatenate([other, held], axis=0),
    )


def scatter_round(held, bit):
    low_rows, high_rows = held[: held.shape[0] // 2], held[held.shape[0] // 2 :]
    upper = (lax.axis_index("seq") & bit) != 0
    got = swap(jnp.where(upper, low_rows, high_rows), "seq", bit)
    return jnp.where(upper, high_rows, low_rows) + got


def bits_of(axis):
    return [1 << bit for bit in range(lax.axis_size(axis).bit_length() - 1)]


def own_half(value):
    rows = value.shape[0] // 2
    return lax.dynamic_slice_in_dim(value, (lax.axis_index("head") & 1) * rows, rows, 0)


def other_half(value):
    rows = value.shape[0] // 2
    return lax.dynamic_slice_in_dim(value, (1 - (lax.axis_index("head") & 1)) * rows, rows, 0)


def both_halves(value):
    other = swap(value, "head", 1)
    return jnp.where(
        (lax.axis_index("head") & 1) == 0,
        jnp.concatenate([value, other], axis=0),
        jnp.concatenate([other, value], axis=0),
    )


def summed_pair(partial_rows):
    pair = own_half(partial_rows).astype(jnp.float32) + swap(
        other_half(low(partial_rows)), "head", 1
    ).astype(jnp.float32)
    return pair


def asked(total):
    bits = bits_of("head")[1:]
    for bit in bits[:-1]:
        total = total + swap(low(total), "head", bit).astype(jnp.float32)
    return total, swap(low(total), "head", bits[-1])


def summed(parts):
    return parts[0] + parts[1].astype(jnp.float32)


def chunk_of(value, index):
    piece = value.shape[-1] // lax.axis_size("seq")
    return value[..., index * piece : (index + 1) * piece]


def dot(a, b):
    return jnp.dot(a, b, preferred_element_type=jnp.float32)


def dot_tn(a, b):
    return lax.dot_general(a, b, (((0,), (0,)), ((), ())), preferred_element_type=jnp.float32)


def dot_nt(a, b):
    return lax.dot_general(a, b, (((1,), (1,)), ((), ())), preferred_element_type=jnp.float32)


def after(values, others):
    return lax.optimization_barrier((values, others))[0]


def passed_along(value, steps):
    count = lax.axis_size("seq")
    leading, last = (max(0, -steps), min(count, count - steps))
    return lax.ppermute(
        value, "seq", [(source, source + steps) for source in range(leading, last)]
    )


def adam_update(master, first_m, second_m, gradient, step_rate, decay_rate):
    first_new = beta_one * first_m + (1.0 - beta_one) * gradient
    second_new = beta_two * second_m + (1.0 - beta_two) * gradient * gradient
    first_hat = first_new / (1.0 - beta_one**STEP)
    second_hat = second_new / (1.0 - beta_two**STEP)
    master_new = master - step_rate * (
        first_hat / (jnp.sqrt(second_hat) + eps_adam) + decay_rate * master
    )
    return (master_new, first_new, second_new)


def norm_back(rows, inv, gain, grad):
    weighted = grad * gain
    mean = jnp.mean(weighted * rows, axis=-1, keepdims=True)
    return inv * weighted - rows * (inv * inv * inv) * mean


def inverse_size(rows):
    return lax.rsqrt(jnp.mean(rows * rows, axis=-1, keepdims=True) + eps_norm)


def per_device(
    block_input, cotangent, lengths,
    proj_master, proj_first, proj_second,
    beta_master, beta_first, beta_second,
    conv_master, conv_first, conv_second,
    out_master, out_first, out_second,
    mlp_master, mlp_first, mlp_second,
    down_master, down_first, down_second,
    gains_master, gains_first, gains_second,
):
    bf16, f32 = jnp.bfloat16, jnp.float32
    count = lax.axis_size("seq")
    seq_index = lax.axis_index("seq")
    rows = block_input.shape[0]
    width = proj_master.shape[2]
    units = mlp_master.shape[2]
    shard = proj_master.shape[1]
    heads = width // DK
    scal = jnp.stack([lengths[0] - seq_index * rows, seq_index * rows]).astype(jnp.int32)
    flow = Flow()
    sizes = [conv_master.size, beta_master.size, gains_master.size]
    packed = low(
        jnp.concatenate(
            [conv_master.reshape(-1), beta_master.reshape(-1), gains_master.reshape(-1)]
        )
    )
    small = jnp.pad(packed, (0, -packed.size % 2048))[None]
    seq_bits = bits_of("seq")
    small = gather_round(small, seq_bits[0])
    proj_low = low(proj_master)
    ring_p = Gather(
        jnp.concatenate([proj_low[0], proj_low[1]], axis=1),
        jnp.concatenate([proj_low[2], proj_low[3]], axis=1),
    )
    flow.step(ring_p, 0)
    flow.step(ring_p, 1)
    cut = (units + width) // 2 // DK * DK
    rest = units - cut
    down_low = jnp.transpose(low(down_master))
    out_low = jnp.transpose(low(out_master))
    mlp_low = low(mlp_master)
    sources, targets = ring_sources(), ring_targets()
    x_ring = pick_columns(block_input, sources)
    dy_ring = pick_columns(cotangent, sources)
    x_rows = x_ring.astype(f32)
    x_inv = inverse_size(x_rows)
    x_ring, dy_ring, x_inv = flow.step(ring_p, 2, (x_ring, dy_ring, x_inv))
    x_rows = x_ring.astype(f32)
    small = flow.step(ring_p, 3, small)
    ring_do = Gather(
        down_low[:, :cut], jnp.concatenate([down_low[:, cut:], out_low], axis=1)
    )
    ring_m = Gather(mlp_low[0], mlp_low[1])
    small = gather_round(small, seq_bits[1])
    flow.step(ring_p, 4)
    ring_do.held[0][0], ring_do.held[1][0], ring_m.held[0][0], ring_m.held[1][0], small = flow.step(
        ring_p,
        5,
        (ring_do.held[0][0], ring_do.held[1][0], ring_m.held[0][0], ring_m.held[1][0], small),
    )
    flow.step(ring_p, 6)
    for bit in seq_bits[2:]:
        small = gather_round(small, bit)
    small = flow.step(ring_p, 7, small)
    conv_all = small[:, : sizes[0]].reshape(count, 3, CONV, -1)
    taps = jnp.transpose(conv_all, (1, 2, 0, 3)).reshape(3, CONV, width).astype(f32)
    beta_all = small[:, sizes[0] : sizes[0] + sizes[1]].reshape(D, heads)
    gains_all = small[:, sizes[0] + sizes[1] : sum(sizes)].reshape(-1)
    columns = jnp.concatenate([gains_all[: 2 * D].reshape(2, D), jnp.transpose(beta_all)], axis=0)
    columns = jnp.take(columns.reshape(2 + heads, count, -1), sources, axis=1).reshape(-1, D)
    gain_a = columns[0:1].astype(f32)
    gain_m = columns[1:2].astype(f32)
    w_beta = columns[2:]
    gain_o = gains_all[2 * D :].astype(f32)[None]
    hidden = (x_rows * x_inv * gain_a).astype(bf16)
    hidden = flow.step(ring_do, 0, hidden)
    logits = dot_nt(hidden, w_beta)
    logits = flow.step(ring_do, 1, logits)
    w_qk, w_vg = ring_p.held
    low_rows = jax.ShapeDtypeStruct((rows, width), bf16)
    (pre_q, pre_k, pre_v, gate), (w_qk, w_vg) = rows_dot(
        hidden,
        [(w_qk, 0, 2 * width), (w_vg, 0, 2 * width)],
        [(0, 0, width, 0, 0), (0, width, width, 1, 0), (1, 0, width, 2, 0), (1, width, width, 3, 0)],
        [low_rows] * 3 + [jax.ShapeDtypeStruct((rows, width), f32)],
    )
    pre = (pre_q, pre_k, pre_v)
    pre, gate = flow.step(ring_do, 2, (pre, gate))
    halo = passed_along(jnp.concatenate([one[rows - 16 :] for one in pre], axis=1), 1)
    halo = flow.step(ring_do, 3, halo)
    q, k, w, uv, t, state_add, state_map = delta_local(scal, pre, halo, taps, logits)
    state_add, state_map = flow.step(ring_do, 4, (state_add, state_map))
    hops = -(-5 * count // 8) - 1
    state_in = passed_along(low(state_add), 1)

    def hop(state):
        moved = jnp.einsum("hij,hjk->hik", state_map, state, preferred_element_type=f32)
        return passed_along(low(moved + state_add), 1)

    state_in = flow.step(ring_do, 5, state_in)
    third = (hops - 1) // 3
    for _ in range(third):
        state_in = hop(state_in)
    state_in = flow.step(ring_do, 6, state_in)
    for _ in range(third):
        state_in = hop(state_in)
    state_in = flow.step(ring_do, 7, state_in)
    for _ in range(hops - 1 - 2 * third):
        state_in = hop(state_in)
    state_in = flow.step(ring_m, 0, state_in)
    normed, out_rows, change, states = delta_apply(scal, q, k, w, uv, state_in, gate, gain_o)
    normed = flow.step(ring_m, 1, normed)
    w_do_a, w_do_b = ring_do.held
    (grad_act,), (w_down_a, w_down_b, w_out) = rows_dot(
        dy_ring,
        [(w_do_a, 0, cut), (w_do_b, 0, rest), (w_do_b, rest, width)],
        [(0, 0, cut, 0, 0), (1, 0, rest, 0, cut)],
        [jax.ShapeDtypeStruct((rows, units), f32)],
    )
    w_out, normed, grad_act = flow.step(ring_m, 2, (w_out, normed, grad_act))
    pair = summed_pair(low(dot_nt(normed, w_out)))
    pair = flow.step(ring_m, 3, pair)
    parts = asked(pair)
    flow.step(ring_m, 4)
    parts = flow.step(ring_m, 5, parts)
    x_one = own_half(x_rows) + summed(parts)
    one_inv = inverse_size(x_one)
    h_two = both_halves(low(x_one * one_inv * gain_m))
    h_two, x_one = flow.step(ring_m, 6, (h_two, x_one))
    gates, ups = ring_m.held
    half = count // 2
    *sums, w_mlp_g, w_mlp_u = glu_early(
        h_two,
        {one: piece for one, piece in gates.items() if abs(one - half) > 1},
        {one: piece for one, piece in ups.items() if abs(one - half) > 1},
    )
    sums, w_mlp_g, w_mlp_u, h_two = flow.step(ring_m, 7, (sums, w_mlp_g, w_mlp_u, h_two))
    late = (half - 1, half, half + 1)
    shard = gates[half].shape[0]
    act_low, grad_gate_u, grad_up_u = glu_late(
        h_two[:, late[0] * shard : (late[-1] + 1) * shard],
        [gates[one] for one in late],
        [ups[one] for one in late],
        sums,
        grad_act,
    )
    for one in late:
        w_mlp_g = lax.dynamic_update_slice_in_dim(w_mlp_g, gates[one], one * shard, 0)
        w_mlp_u = lax.dynamic_update_slice_in_dim(w_mlp_u, ups[one], one * shard, 0)
    def rows_of(value):
        piece = value.shape[0] // count
        return lambda one: value[one * piece : (one + 1) * piece]

    back_m = Scatter(
        rows_of(low(dot_tn(h_two, grad_gate_u))), rows_of(low(dot_tn(h_two, grad_up_u)))
    )
    flow.step(back_m, 0)
    grad_gate_u, grad_up_u, act_low = flow.step(back_m, 1, (grad_gate_u, grad_up_u, act_low))
    part = low(dot_nt(grad_gate_u, w_mlp_g) + dot_nt(grad_up_u, w_mlp_u))
    part = flow.step(back_m, 2, part)
    pair, act_low = flow.step(back_m, 3, (summed_pair(part), act_low))
    parts = asked(pair)
    part = low(dot_nt(act_low[:, :cut], w_down_a) + dot_nt(act_low[:, cut:], w_down_b))
    part = flow.step(back_m, 4, part)
    parts, part = flow.step(back_m, 5, (parts, part))
    mlp_pair = summed_pair(part)
    grad_h_two = summed(parts)
    grad_gain_m = 0.5 * jnp.sum(grad_h_two * x_one * one_inv, axis=0, keepdims=True)
    grad_x_one = own_half(dy_ring).astype(f32) + norm_back(x_one, one_inv, gain_m, grad_h_two)
    grad_attn = both_halves(low(grad_x_one))
    grad_normed = dot(grad_attn, w_out)
    grad_normed, grad_attn, mlp_pair, act_low = flow.step(
        back_m, 6, (grad_normed, grad_attn, mlp_pair, act_low)
    )
    mlp_parts = asked(mlp_pair)
    grad_gate, grad_gain_o, grad_out, through, carry = delta_back_local(
        scal, grad_normed, gate, gain_o, out_rows, q, k, w
    )
    grad_gate, carry, act_low = flow.step(back_m, 7, (grad_gate, carry, act_low))
    above = passed_along(low(carry), -1)
    grad_do_a = low(dot_tn(dy_ring, act_low[:, :cut]))
    grad_do_b = jnp.concatenate(
        [low(dot_tn(dy_ring, act_low[:, cut:])), low(dot_tn(grad_attn, normed))], axis=1
    )
    back_do = Scatter(rows_of(grad_do_a), rows_of(grad_do_b))

    def hop_back(state):
        moved = jnp.einsum("hji,hjk->hik", state_map, state, preferred_element_type=f32)
        return passed_along(low(moved + carry), -1)

    above = flow.step(back_do, 0, above)
    for _ in range(third):
        above = hop_back(above)
    above, mlp_parts = flow.step(back_do, 1, (above, mlp_parts))
    for _ in range(third):
        above = hop_back(above)
    above = flow.step(back_do, 2, above)
    for _ in range(hops - 1 - 2 * third):
        above = hop_back(above)
    above = flow.step(back_do, 3, above)
    grad_pre, tail, back_halo, grad_taps, grad_logits = delta_back(
        scal, pre, halo, taps, logits, q, k, w, t, change, states, grad_out, through, above
    )
    mlp_sum = flow.step(back_do, 4, summed(mlp_parts))
    result = join_columns(x_one + mlp_sum, targets)
    grad_pre, back_halo, tail, grad_logits, result = flow.step(
        back_do, 5, (grad_pre, back_halo, tail, grad_logits, result)
    )
    fixed = low(tail + passed_along(back_halo, -1))
    grad_pre = lax.dynamic_update_slice_in_dim(grad_pre, fixed, rows - 8, 1)
    grad_qk = jnp.concatenate([grad_pre[0], grad_pre[1]], axis=1)
    grad_vg = jnp.concatenate([grad_pre[2], grad_gate], axis=1)
    grad_qk, grad_vg = flow.step(back_do, 6, (grad_qk, grad_vg))
    back_p = Scatter(
        rows_of(low(dot_tn(hidden, grad_qk))), rows_of(low(dot_tn(hidden, grad_vg)))
    )
    flow.step(back_do, 7)
    grad_qk, grad_vg, grad_logits = flow.step(back_p, 0, (grad_qk, grad_vg, grad_logits))
    grad_logits = low(grad_logits)
    grad_hidden = low(
        dot_nt(grad_qk, w_qk) + dot_nt(grad_vg, w_vg) + dot(grad_logits, w_beta)
    )
    grad_beta = dot_tn(grad_logits, hidden)
    grad_hidden, grad_beta = flow.step(back_p, 1, (grad_hidden, grad_beta))
    pair = summed_pair(grad_hidden)
    grad_gain_a = jnp.sum(grad_hidden.astype(f32) * x_rows * x_inv, axis=0, keepdims=True)
    stacked = jnp.concatenate([grad_gain_a, grad_gain_m, grad_beta], axis=0)
    stacked = jnp.take(stacked.reshape(2 + heads, count, -1), targets, axis=1).reshape(-1, D)
    grad_gains = jnp.concatenate(
        [stacked[:2].reshape(-1), jnp.sum(grad_gain_o[:, 0], axis=0)]
    ).reshape(count, -1)
    grad_conv = jnp.transpose(
        grad_taps.reshape(3, CONV, count, width // count), (2, 0, 1, 3)
    ).reshape(count, -1)
    grad_beta = jnp.transpose(stacked[2:]).reshape(count, -1)
    small_sum = jnp.concatenate([grad_conv, grad_beta, grad_gains], axis=1)
    small_sum, pair = flow.step(back_p, 2, (small_sum, pair))
    parts = asked(pair)
    flow.step(back_p, 3)
    small_sum, parts = flow.step(back_p, 4, (small_sum, parts))
    small_sum = scatter_round(small_sum, seq_bits[-1])
    mlp_g_sum, mlp_u_sum = back_m.sums()
    mlp_new, mlp_first_new, mlp_second_new = adam_update(
        mlp_master, mlp_first, mlp_second, jnp.stack([mlp_g_sum, mlp_u_sum]),
        rate_matrix, decay_matrix,
    )
    small_sum, mlp_new, mlp_first_new, mlp_second_new = flow.step(
        back_p, 5, (small_sum, mlp_new, mlp_first_new, mlp_second_new)
    )
    for bit in seq_bits[-2:0:-1]:
        small_sum = scatter_round(small_sum, bit)
    grad_x_rest = norm_back(own_half(x_rows), own_half(x_inv), gain_a, summed(parts))
    input_half = grad_x_one + grad_x_rest
    small_sum, input_half = flow.step(back_p, 6, (small_sum, input_half))
    small_sum = scatter_round(small_sum, seq_bits[0])[0]
    do_a_sum, do_b_sum = back_do.sums()
    summed_down = jnp.transpose(jnp.concatenate([do_a_sum, do_b_sum[:, :rest]], axis=1))
    out_sum = jnp.transpose(do_b_sum[:, rest:])
    down_new, down_first_new, down_second_new = adam_update(
        down_master, down_first, down_second, summed_down, rate_down, decay_matrix
    )
    out_new, out_first_new, out_second_new = adam_update(
        out_master, out_first, out_second, out_sum, rate_matrix, decay_matrix
    )
    input_grad = join_columns(input_half, targets)
    small_sum, input_grad, down_new, down_first_new, down_second_new = flow.step(
        back_p, 7, (small_sum, input_grad, down_new, down_first_new, down_second_new)
    )
    gains_sum = small_sum[sizes[0] + sizes[1] :]
    for bit in bits_of("head"):
        gains_sum = gains_sum + swap(gains_sum, "head", bit)
    summed_conv = small_sum[: sizes[0]].reshape(conv_master.shape)
    summed_beta = small_sum[sizes[0] : sizes[0] + sizes[1]].reshape(beta_master.shape)
    qk_sum, vg_sum = back_p.sums()
    summed_proj = jnp.stack(
        [qk_sum[:, :width], qk_sum[:, width:], vg_sum[:, :width], vg_sum[:, width:]]
    )
    proj_new, proj_first_new, proj_second_new = adam_update(
        proj_master, proj_first, proj_second, summed_proj, rate_matrix, decay_matrix
    )
    beta_new, beta_first_new, beta_second_new = adam_update(
        beta_master, beta_first, beta_second, summed_beta, rate_beta, decay_matrix
    )
    conv_new, conv_first_new, conv_second_new = adam_update(
        conv_master, conv_first, conv_second, summed_conv, rate_conv, decay_matrix
    )
    gains_new, gains_first_new, gains_second_new = adam_update(
        gains_master, gains_first, gains_second, gains_sum, rate_gains, 0.0
    )
    return (
        result,
        input_grad,
        proj_new, proj_first_new, proj_second_new, proj_new.astype(bf16),
        beta_new, beta_first_new, beta_second_new, beta_new.astype(bf16),
        conv_new, conv_first_new, conv_second_new, conv_new.astype(bf16),
        out_new, out_first_new, out_second_new, out_new.astype(bf16),
        mlp_new, mlp_first_new, mlp_second_new, mlp_new.astype(bf16),
        down_new, down_first_new, down_second_new, down_new.astype(bf16),
        gains_new, gains_first_new, gains_second_new,
    )


def solution(mesh):
    rows = P("seq", None)
    proj = P(None, "seq", "head")
    tall = P("seq", "head")
    conv = P(None, None, ("head", "seq"))
    flat = P("head", "seq")
    gains = P("seq")
    return jax.shard_map(
        per_device,
        mesh=mesh,
        in_specs=(rows, rows, P())
        + (proj,) * 3
        + (tall,) * 3
        + (conv,) * 3
        + (flat,) * 3
        + (proj,) * 3
        + (flat,) * 3
        + (gains,) * 3,
        out_specs=(rows, rows)
        + (proj,) * 4
        + (tall,) * 4
        + (conv,) * 4
        + (flat,) * 4
        + (proj,) * 4
        + (flat,) * 4
        + (gains,) * 3,
        check_vma=False,
    )
```

```python
from functools import partial

import jax
import jax.numpy as jnp
from jax import lax
from jax.experimental import pallas as pl
from jax.experimental.pallas import tpu as pltpu
from jax.sharding import PartitionSpec as P

D = 2048
DK = 128
CONV = 4
SPAN = 64
STEP = 10

eps_norm = 1e-05
eps_unit = 1e-06
beta_one = 0.9
beta_two = 0.95
eps_adam = 1e-08
rate_matrix = 0.04
rate_beta = 0.12
rate_down = 0.03
rate_conv = 0.3
rate_gains = 0.4
decay_matrix = 0.1


SPANROWS = 128


def _mm(a, b):
    return jnp.dot(
        a.astype(jnp.bfloat16), b.astype(jnp.bfloat16), preferred_element_type=jnp.float32
    )


def _mm_nt(a, b):
    return lax.dot_general(
        a.astype(jnp.bfloat16),
        b.astype(jnp.bfloat16),
        (((1,), (1,)), ((), ())),
        preferred_element_type=jnp.float32,
    )


def _mm_tn(a, b):
    return lax.dot_general(
        a.astype(jnp.bfloat16),
        b.astype(jnp.bfloat16),
        (((0,), (0,)), ((), ())),
        preferred_element_type=jnp.float32,
    )


def _pair_masks():
    row = lax.broadcasted_iota(jnp.int32, (SPANROWS, SPANROWS), 0)
    col = lax.broadcasted_iota(jnp.int32, (SPANROWS, SPANROWS), 1)
    same = (row // SPAN) == (col // SPAN)
    return row, col, same


def _tap_masks(scal_ref, rows):
    edge, base = scal_ref[0], scal_ref[1]
    token = lax.broadcasted_iota(jnp.int32, (rows, DK), 0)
    after = token >= edge
    masks = [None]
    for shift in range(1, CONV):
        good = jnp.where(after, token - edge, token + base) >= shift
        masks.append(good.astype(jnp.float32))
    return masks


def _keep(scal_ref, span):
    edge, base = scal_ref[0], scal_ref[1]
    start = span * SPAN
    hit = (edge == start) | ((base + start) == 0)
    return jnp.where(hit, 0.0, 1.0).astype(jnp.float32)


def _convolved(ext_ref, pre, halo, taps, masks):
    rows = pre.shape[0]
    ext_ref[0:8] = halo[8:16].astype(jnp.float32)
    ext_ref[8 : 8 + rows] = pre.astype(jnp.float32)
    total = taps[CONV - 1 : CONV] * ext_ref[8 : 8 + rows]
    for shift in range(1, CONV):
        total = (
            total
            + taps[CONV - 1 - shift : CONV - shift]
            * ext_ref[8 - shift : 8 - shift + rows]
            * masks[shift]
        )
    return total


def _unit(act):
    return act * lax.rsqrt(jnp.sum(act * act, axis=-1, keepdims=True) + eps_unit)


def _column(table, index):
    lane = lax.broadcasted_iota(jnp.int32, table.shape, 1)
    return jnp.sum(jnp.where(lane == index, table, 0.0), axis=1, keepdims=True)


def _local_kernel(
    heads, scal_ref, pre_q, pre_k, pre_v, halo_q, halo_k, halo_v, taps_ref, logit_ref, q_ref, k_ref,
    w_ref, uv_ref, t_ref, bt_ref, pt_ref, ext_ref,
):
    pre_refs, halo_refs = (pre_q, pre_k, pre_v), (halo_q, halo_k, halo_v)
    rows = pre_q.shape[0]
    pairs = rows // SPANROWS
    masks = _tap_masks(scal_ref, rows)
    row, col, same = _pair_masks()
    strict = same & (row > col)
    eye = (row == col).astype(jnp.float32)
    levels = []
    for bit in range(6):
        inside = ((row >> (bit + 1)) == (col >> (bit + 1))) & same
        levels.append(
            (inside & (((row >> bit) & 1) == 1) & (((col >> bit) & 1) == 0)).astype(jnp.float32)
        )
    logit = logit_ref[...]
    first_head = pl.program_id(0) * heads
    keys, lowers, sides = [], [], []
    for head in range(heads):
        lanes = slice(head * DK, (head + 1) * DK)
        beta = jax.nn.sigmoid(_column(logit, first_head + head))
        acts = []
        for part in range(3):
            mixed = _convolved(
                ext_ref.at[head * 3 + part], pre_refs[part][:, lanes], halo_refs[part][:, lanes],
                taps_ref[part, :, lanes], masks,
            )
            acts.append(mixed * jax.nn.sigmoid(mixed))
        query = _unit(acts[0])
        key = _unit(acts[1])
        q_ref[:, lanes] = query.astype(jnp.bfloat16)
        key_low = key.astype(jnp.bfloat16)
        k_ref[:, lanes] = key_low
        side = jnp.concatenate([beta * key, beta * acts[2]], axis=1).astype(jnp.bfloat16)
        for pair in range(pairs):
            part = slice(pair * SPANROWS, (pair + 1) * SPANROWS)
            gram = _mm_nt(key_low[part], key_low[part])
            lowers.append(jnp.where(strict, gram * beta[part], 0.0))
            sides.append(side[part])
        keys.append(key_low)
    inverses = [eye - low * levels[0] for low in lowers]
    for bit in range(1, 6):
        middle = [_mm(low * levels[bit], inv) for low, inv in zip(lowers, inverses)]
        inverses = [inv - _mm(inv, mid) for mid, inv in zip(middle, inverses)]
    carried = []
    w_all, uv_all = [], []
    for head in range(heads):
        lanes = slice(head * DK, (head + 1) * DK)
        w_rows, uv_rows = [], []
        for pair in range(pairs):
            part = slice(pair * SPANROWS, (pair + 1) * SPANROWS)
            inv = inverses[head * pairs + pair].astype(jnp.bfloat16)
            t_ref[part, lanes] = inv
            both = _mm(inv, sides[head * pairs + pair])
            w_part = both[:, :DK].astype(jnp.bfloat16)
            w_ref[part, lanes] = w_part
            uv_ref[part, lanes] = both[:, DK:]
            w_rows.append(w_part)
            uv_rows.append(both[:, DK:])
        w_all.append(w_rows)
        uv_all.append(uv_rows)
        carried.append(jnp.concatenate([jnp.zeros((DK, DK), jnp.float32), eye], axis=1))
    for span in range(rows // SPAN):
        keep = _keep(scal_ref, span)
        pair, half = divmod(span, SPANROWS // SPAN)
        part = slice(half * SPAN, (half + 1) * SPAN)
        for head in range(heads):
            state = carried[head] * keep
            w_part = w_all[head][pair][part]
            source = jnp.concatenate(
                [uv_all[head][pair][part], jnp.zeros((SPAN, DK), jnp.float32)], axis=1
            )
            change = source - _mm(w_part, state)
            carried[head] = state + _mm_tn(
                keys[head][span * SPAN : (span + 1) * SPAN], change
            )
    for head in range(heads):
        bt_ref[head] = carried[head][:, :DK]
        pt_ref[head] = carried[head][:, DK:].astype(jnp.bfloat16)


def _apply_kernel(
    heads, scal_ref, q_ref, k_ref, w_ref, uv_ref, state_ref, gate_ref, gain_ref, n_ref, o_ref,
    u_ref, s_ref,
):
    rows = q_ref.shape[0]
    pairs = rows // SPANROWS
    row, col, same = _pair_masks()
    lower = same & (row >= col)
    states = [state_ref[head].astype(jnp.float32) for head in range(heads)]
    moved = [[] for _ in range(heads)]
    crossed = [[] for _ in range(heads)]
    for span in range(rows // SPAN):
        keep = _keep(scal_ref, span)
        part = slice(span * SPAN, (span + 1) * SPAN)
        for head in range(heads):
            lanes = slice(head * DK, (head + 1) * DK)
            state = states[head] * keep
            state_low = state.astype(jnp.bfloat16)
            s_ref[head, span] = state_low
            both = _mm(
                jnp.concatenate([w_ref[part, lanes], q_ref[part, lanes]], axis=0), state_low
            )
            change = (uv_ref[part, lanes] - both[:SPAN]).astype(jnp.bfloat16)
            crossed[head].append(both[SPAN:])
            moved[head].append(change)
            states[head] = state + _mm_tn(k_ref[part, lanes], change)
    for head in range(heads):
        lanes = slice(head * DK, (head + 1) * DK)
        for pair in range(pairs):
            part = slice(pair * SPANROWS, (pair + 1) * SPANROWS)
            change = jnp.concatenate([moved[head][2 * pair], moved[head][2 * pair + 1]], axis=0)
            cross = jnp.concatenate([crossed[head][2 * pair], crossed[head][2 * pair + 1]], axis=0)
            u_ref[part, lanes] = change
            scores = jnp.where(lower, _mm_nt(q_ref[part, lanes], k_ref[part, lanes]), 0.0)
            out = cross + _mm(scores, change)
            o_ref[part, lanes] = out
            scaled = out * lax.rsqrt(jnp.mean(out * out, axis=-1, keepdims=True) + eps_norm)
            gate = gate_ref[part, lanes]
            n_ref[part, lanes] = (
                scaled * gain_ref[...] * (gate * jax.nn.sigmoid(gate))
            ).astype(jnp.bfloat16)


def _back_local_kernel(
    heads, scal_ref, dn_ref, gate_ref, gain_ref, o_ref, q_ref, k_ref, w_ref, dg_ref, dgo_ref,
    do_ref, p_ref, carry_ref,
):
    rows = q_ref.shape[0]
    pairs = rows // SPANROWS
    row, col, same = _pair_masks()
    lower = same & (row >= col)
    gain = gain_ref[...]
    grad_outs = [[] for _ in range(heads)]
    passed = [[] for _ in range(heads)]
    for head in range(heads):
        lanes = slice(head * DK, (head + 1) * DK)
        gain_sum = jnp.zeros((1, DK), jnp.float32)
        for pair in range(pairs):
            part = slice(pair * SPANROWS, (pair + 1) * SPANROWS)
            out = o_ref[part, lanes]
            gate = gate_ref[part, lanes]
            grad_n = dn_ref[part, lanes]
            inv = lax.rsqrt(jnp.mean(out * out, axis=-1, keepdims=True) + eps_norm)
            sig = jax.nn.sigmoid(gate)
            act = gate * sig
            scaled = out * inv
            with_gain = grad_n * gain
            dg_ref[part, lanes] = (
                with_gain * scaled * (sig * (1.0 + gate * (1.0 - sig)))
            ).astype(jnp.bfloat16)
            gain_sum = gain_sum + jnp.sum(grad_n * scaled * act, axis=0, keepdims=True)
            inner = with_gain * act
            grad_out = (
                inv * inner
                - out * (inv * inv * inv) * jnp.mean(inner * out, axis=-1, keepdims=True)
            ).astype(jnp.bfloat16)
            do_ref[part, lanes] = grad_out
            scores = jnp.where(lower, _mm_nt(q_ref[part, lanes], k_ref[part, lanes]), 0.0)
            through = _mm_tn(scores, grad_out)
            p_ref[part, lanes] = through
            grad_outs[head].append(grad_out)
            passed[head].append(through)
        dgo_ref[head] = jnp.broadcast_to(gain_sum, (8, DK))
    carried = [jnp.zeros((DK, DK), jnp.float32) for _ in range(heads)]
    for span in reversed(range(rows // SPAN)):
        keep = _keep(scal_ref, span)
        rows_in = slice(span * SPAN, (span + 1) * SPAN)
        pair, half = divmod(span, SPANROWS // SPAN)
        part = slice(half * SPAN, (half + 1) * SPAN)
        for head in range(heads):
            lanes = slice(head * DK, (head + 1) * DK)
            change = passed[head][pair][part] + _mm(k_ref[rows_in, lanes], carried[head])
            carried[head] = keep * (
                carried[head]
                + _mm_tn(q_ref[rows_in, lanes], grad_outs[head][pair][part])
                - _mm_tn(w_ref[rows_in, lanes], change)
            )
    for head in range(heads):
        carry_ref[head] = carried[head]


def _back_kernel(
    heads, scal_ref, pre_q, pre_k, pre_v, halo_q, halo_k, halo_v, taps_ref, logit_ref, q_ref, k_ref,
    w_ref, t_ref, u_ref, s_ref, do_ref, p_ref, above_ref, dpre_ref, tail_ref, dhalo_ref, dtaps_ref,
    dlogit_ref, ext_ref, pad_ref,
):
    pre_refs, halo_refs = (pre_q, pre_k, pre_v), (halo_q, halo_k, halo_v)
    rows = q_ref.shape[0]
    pairs = rows // SPANROWS
    masks = _tap_masks(scal_ref, rows)
    row, col, same = _pair_masks()
    lower = same & (row >= col)
    strict = same & (row > col)
    edge, base = scal_ref[0], scal_ref[1]
    token = lax.broadcasted_iota(jnp.int32, (rows + 8, DK), 0) - 8
    back_masks = []
    for shift in range(CONV):
        good = jnp.where(token + shift >= edge, token - edge, token + base) >= 0
        back_masks.append(good.astype(jnp.float32))
    logit = logit_ref[...]
    first_head = pl.program_id(0) * heads
    carried = [above_ref[head].astype(jnp.float32) for head in range(heads)]
    changes = [[None] * (rows // SPAN) for _ in range(heads)]
    crossed = [[None] * (rows // SPAN) for _ in range(heads)]
    for span in reversed(range(rows // SPAN)):
        keep = _keep(scal_ref, span)
        part = slice(span * SPAN, (span + 1) * SPAN)
        for head in range(heads):
            lanes = slice(head * DK, (head + 1) * DK)
            above = carried[head].astype(jnp.bfloat16)
            change = (p_ref[part, lanes] + _mm(k_ref[part, lanes], above)).astype(jnp.bfloat16)
            changes[head][span] = change
            crossed[head][span] = _mm_nt(u_ref[part, lanes], above)
            carried[head] = keep * (
                carried[head]
                + _mm_tn(q_ref[part, lanes], do_ref[part, lanes])
                - _mm_tn(w_ref[part, lanes], change)
            )
    lane_index = lax.broadcasted_iota(jnp.int32, logit.shape, 1)
    grad_logit = jnp.zeros(logit.shape, jnp.float32)
    for head in range(heads):
        lanes = slice(head * DK, (head + 1) * DK)
        taps = taps_ref[:, :, lanes]
        beta = jax.nn.sigmoid(_column(logit, first_head + head))
        acts, slopes = [], []
        for which in range(3):
            mixed = _convolved(
                ext_ref.at[head * 3 + which], pre_refs[which][:, lanes], halo_refs[which][:, lanes],
                taps[which], masks,
            )
            sig = jax.nn.sigmoid(mixed)
            acts.append(mixed * sig)
            slopes.append(sig * (1.0 + mixed * (1.0 - sig)))
        query_inv = lax.rsqrt(jnp.sum(acts[0] * acts[0], axis=-1, keepdims=True) + eps_unit)
        key_inv = lax.rsqrt(jnp.sum(acts[1] * acts[1], axis=-1, keepdims=True) + eps_unit)
        query = acts[0] * query_inv
        key = acts[1] * key_inv
        value = acts[2]
        grad_q, grad_k, grad_v, grad_b = [], [], [], []
        for pair in range(pairs):
            part = slice(pair * SPANROWS, (pair + 1) * SPANROWS)
            spans = (2 * pair, 2 * pair + 1)
            q_low, k_low = q_ref[part, lanes], k_ref[part, lanes]
            u_low, do_low = u_ref[part, lanes], do_ref[part, lanes]
            change = jnp.concatenate([changes[head][span] for span in spans], axis=0)
            solved = _mm_tn(t_ref[part, lanes], change)
            solved_low = solved.astype(jnp.bfloat16)
            both = [
                _mm_nt(
                    jnp.concatenate(
                        [
                            do_low[half * SPAN : (half + 1) * SPAN],
                            solved_low[half * SPAN : (half + 1) * SPAN],
                        ],
                        axis=0,
                    ),
                    s_ref[head, span],
                )
                for half, span in enumerate(spans)
            ]
            out_state = jnp.concatenate([both[0][:SPAN], both[1][:SPAN]], axis=0)
            solved_state = jnp.concatenate([both[0][SPAN:], both[1][SPAN:]], axis=0)
            weights = jnp.where(lower, _mm_nt(do_low, u_low), 0.0).astype(jnp.bfloat16)
            grad_q.append(out_state + _mm(weights, k_low))
            grad_low = jnp.where(strict, -_mm_nt(solved_low, u_low), 0.0)
            gram = _mm_nt(k_low, k_low)
            beta_part = beta[part]
            grad_gram = (grad_low * beta_part).astype(jnp.bfloat16)
            grad_k.append(
                _mm_tn(weights, q_low)
                + jnp.concatenate([crossed[head][span] for span in spans], axis=0)
                - beta_part * solved_state
                + _mm(grad_gram, k_low)
                + _mm_tn(grad_gram, k_low)
            )
            grad_v.append(beta_part * solved)
            grad_b.append(
                jnp.sum(grad_low * gram, axis=1, keepdims=True)
                + jnp.sum(solved * value[part] - solved_state * key[part], axis=1, keepdims=True)
            )
        grad_query = jnp.concatenate(grad_q, axis=0)
        grad_key = jnp.concatenate(grad_k, axis=0)
        grad_beta = jnp.concatenate(grad_b, axis=0)
        grad_logit = grad_logit + jnp.where(
            lane_index == first_head + head, grad_beta * beta * (1.0 - beta), 0.0
        )
        grad_acts = [
            (grad_query - query * jnp.sum(query * grad_query, axis=-1, keepdims=True)) * query_inv,
            (grad_key - key * jnp.sum(key * grad_key, axis=-1, keepdims=True)) * key_inv,
            jnp.concatenate(grad_v, axis=0),
        ]
        for which in range(3):
            grad_mixed = grad_acts[which] * slopes[which]
            pad = pad_ref.at[head * 3 + which]
            ext = ext_ref.at[head * 3 + which]
            pad[0:8] = jnp.zeros((8, DK), jnp.float32)
            pad[8 : 8 + rows] = grad_mixed
            pad[8 + rows : 16 + rows] = jnp.zeros((8, DK), jnp.float32)
            total = jnp.zeros((rows + 8, DK), jnp.float32)
            for shift in range(CONV):
                tap = CONV - 1 - shift
                shifted = pad[shift : shift + rows + 8] * back_masks[shift]
                total = total + taps[which, tap : tap + 1] * shifted
                dtaps_ref[which, tap : tap + 1, lanes] = jnp.sum(
                    shifted * ext[0 : rows + 8], axis=0, keepdims=True
                )
            dhalo_ref[which, :, lanes] = total[:8]
            dpre_ref[which, :, lanes] = total[8:].astype(jnp.bfloat16)
            tail_ref[which, :, lanes] = total[rows:]

    @pl.when(pl.program_id(0) == 0)
    def _():
        dlogit_ref[...] = grad_logit

    @pl.when(pl.program_id(0) > 0)
    def _():
        dlogit_ref[...] += grad_logit


HEADS_AT_ONCE = 4


def _specs(heads, rows):
    wide = heads * DK
    return dict(
        scal=pl.BlockSpec(memory_space=pltpu.SMEM),
        flat=pl.BlockSpec((rows, wide), lambda h: (0, h)),
        three=pl.BlockSpec((3, rows, wide), lambda h: (0, 0, h)),
        edge=pl.BlockSpec((3, 8, wide), lambda h: (0, 0, h)),
        taps=pl.BlockSpec((3, CONV, wide), lambda h: (0, 0, h)),
        square=pl.BlockSpec((heads, DK, DK), lambda h: (h, 0, 0)),
        spans=pl.BlockSpec((heads, rows // SPAN, DK, DK), lambda h: (h, 0, 0, 0)),
        gain=pl.BlockSpec((1, DK), lambda h: (0, 0)),
        small=pl.BlockSpec((heads, 8, DK), lambda h: (h, 0, 0)),
    )


def _three_specs(heads, rows, total):
    def one(tall, part):
        return pl.BlockSpec((tall, heads * DK), lambda h: (0, part * (total // heads) + h))

    return [one(rows, 0)] * 3 + [one(16, part) for part in range(3)]


def _cost(microseconds):
    return pl.CostEstimate(
        flops=microseconds * 11 * 10**8,
        bytes_accessed=microseconds * 36 * 10**5,
        transcendentals=0,
    )


def _params(mebibytes=48):
    return pltpu.CompilerParams(
        dimension_semantics=("arbitrary",), vmem_limit_bytes=mebibytes * 1024 * 1024
    )


def delta_local(scal, pre, halo, taps, logits):
    rows, width = pre[0].shape
    total = width // DK
    heads = min(HEADS_AT_ONCE, total)
    sp = _specs(heads, rows)
    table = pl.BlockSpec((rows, total), lambda h: (0, 0))
    low = jax.ShapeDtypeStruct((rows, width), jnp.bfloat16)
    return pl.pallas_call(
        partial(_local_kernel, heads),
        grid=(total // heads,),
        in_specs=[sp["scal"]] + _three_specs(heads, rows, total) + [sp["taps"], table],
        out_specs=[sp["flat"]] * 5 + [sp["square"]] * 2,
        out_shape=[
            low,
            low,
            low,
            jax.ShapeDtypeStruct((rows, width), jnp.float32),
            low,
            jax.ShapeDtypeStruct((total, DK, DK), jnp.float32),
            jax.ShapeDtypeStruct((total, DK, DK), jnp.bfloat16),
        ],
        scratch_shapes=[pltpu.VMEM((3 * heads, rows + 8, DK), jnp.float32)],
        compiler_params=_params(60),
        cost_estimate=_cost(8),
        name="delta_local",
    )(scal, *pre, halo, halo, halo, taps, logits)


def delta_apply(scal, q, k, w, uv, state_in, gate, gain):
    rows, width = q.shape
    total = width // DK
    heads = min(HEADS_AT_ONCE, total)
    sp = _specs(heads, rows)
    low = jax.ShapeDtypeStruct((rows, width), jnp.bfloat16)
    return pl.pallas_call(
        partial(_apply_kernel, heads),
        grid=(total // heads,),
        in_specs=[sp["scal"]] + [sp["flat"]] * 4 + [sp["square"], sp["flat"], sp["gain"]],
        out_specs=[sp["flat"]] * 3 + [sp["spans"]],
        out_shape=[
            low,
            jax.ShapeDtypeStruct((rows, width), jnp.float32),
            low,
            jax.ShapeDtypeStruct((total, rows // SPAN, DK, DK), jnp.bfloat16),
        ],
        compiler_params=_params(60),
        cost_estimate=_cost(5),
        name="delta_apply",
    )(scal, q, k, w, uv, state_in, gate, gain)


def delta_back_local(scal, dn, gate, gain, o, q, k, w):
    rows, width = q.shape
    total = width // DK
    heads = min(HEADS_AT_ONCE, total)
    sp = _specs(heads, rows)
    low = jax.ShapeDtypeStruct((rows, width), jnp.bfloat16)
    return pl.pallas_call(
        partial(_back_local_kernel, heads),
        grid=(total // heads,),
        in_specs=[sp["scal"], sp["flat"], sp["flat"], sp["gain"]] + [sp["flat"]] * 4,
        out_specs=[sp["flat"], sp["small"], sp["flat"], sp["flat"], sp["square"]],
        out_shape=[
            low,
            jax.ShapeDtypeStruct((total, 8, DK), jnp.float32),
            low,
            jax.ShapeDtypeStruct((rows, width), jnp.float32),
            jax.ShapeDtypeStruct((total, DK, DK), jnp.float32),
        ],
        compiler_params=_params(),
        cost_estimate=_cost(8),
        name="delta_back_local",
    )(scal, dn, gate, gain, o, q, k, w)


def delta_back(scal, pre, halo, taps, logits, q, k, w, t, u, s, do, p, above):
    rows, width = pre[0].shape
    total = width // DK
    heads = min(HEADS_AT_ONCE, total)
    sp = _specs(heads, rows)
    table = pl.BlockSpec((rows, total), lambda h: (0, 0))
    edge = jax.ShapeDtypeStruct((3, 8, width), jnp.float32)
    return pl.pallas_call(
        partial(_back_kernel, heads),
        grid=(total // heads,),
        in_specs=[sp["scal"]]
        + _three_specs(heads, rows, total)
        + [sp["taps"], table]
        + [sp["flat"]] * 5
        + [sp["spans"], sp["flat"], sp["flat"], sp["square"]],
        out_specs=[sp["three"], sp["edge"], sp["edge"], sp["taps"], table],
        out_shape=[
            jax.ShapeDtypeStruct((3, rows, width), jnp.bfloat16),
            edge,
            edge,
            jax.ShapeDtypeStruct((3, CONV, width), jnp.float32),
            jax.ShapeDtypeStruct((rows, total), jnp.float32),
        ],
        scratch_shapes=[
            pltpu.VMEM((3 * heads, rows + 8, DK), jnp.float32),
            pltpu.VMEM((3 * heads, rows + 16, DK), jnp.float32),
        ],
        compiler_params=_params(),
        cost_estimate=_cost(15),
        name="delta_back",
    )(
        scal, *pre, halo, halo, halo, taps, logits, q, k, w, t, u, s, do, p, above
    )


def ring_order(count):
    return list(range(0, count, 2)) + list(range(count - 1, 0, -2))


def ring_pairs(count):
    order = ring_order(count)
    return [(order[place], order[(place + 1) % count]) for place in range(count)]


def send_up(value):
    return lax.ppermute(value, "seq", ring_pairs(lax.axis_size("seq")))


def send_down(value):
    return lax.ppermute(value, "seq", [(b, a) for a, b in ring_pairs(lax.axis_size("seq"))])


def ring_place():
    count = lax.axis_size("seq")
    index = lax.axis_index("seq")
    return jnp.where(index % 2 == 0, index // 2, count - (index + 1) // 2)


def ring_sources():
    count = lax.axis_size("seq")
    order = jnp.asarray(ring_order(count), jnp.int32)
    return jnp.take(order, (ring_place() + jnp.arange(count, dtype=jnp.int32)) % count)


def ring_targets():
    count = lax.axis_size("seq")
    order = ring_order(count)
    places = jnp.asarray([order.index(one) for one in range(count)], jnp.int32)
    return (places + count - ring_place()) % count


def _pick_kernel(pieces, index_ref, value_ref, out_ref):
    piece = out_ref.shape[1] // pieces
    for one in range(pieces):
        start = pl.multiple_of(index_ref[one] * piece, DK)
        out_ref[:, one * piece : (one + 1) * piece] = value_ref[:, pl.ds(start, piece)]


def _join_kernel(pieces, index_ref, own_ref, other_ref, out_ref):
    piece = out_ref.shape[1] // pieces
    own = (pl.program_id(0) >= pl.num_programs(0) // 2) == (index_ref[pieces] == 1)
    for one in range(pieces):
        start = pl.multiple_of(index_ref[one] * piece, DK)
        out_ref[:, one * piece : (one + 1) * piece] = jnp.where(
            own, own_ref[:, pl.ds(start, piece)], other_ref[:, pl.ds(start, piece)]
        )


def pick_columns(value, index):
    count = index.shape[0]
    rows, wide = value.shape
    piece = wide // count
    if piece % DK:
        return jnp.take(value.reshape(rows, count, piece), index, axis=1).reshape(rows, wide)
    tall = rows // 4
    return pl.pallas_call(
        partial(_pick_kernel, count),
        grid=(4,),
        in_specs=[
            pl.BlockSpec(memory_space=pltpu.SMEM),
            pl.BlockSpec((tall, wide), lambda i: (i, 0)),
        ],
        out_specs=pl.BlockSpec((tall, wide), lambda i: (i, 0)),
        out_shape=jax.ShapeDtypeStruct(value.shape, value.dtype),
        compiler_params=_params(),
        cost_estimate=_cost(3),
        name="pick_columns",
    )(index, value)


def join_columns(own, index):
    other = swap(own, "head", 1)
    bit = lax.axis_index("head") & 1
    count = index.shape[0]
    rows, wide = own.shape
    if (wide // count) % DK:
        both = jnp.where(
            bit == 0,
            jnp.concatenate([own, other], axis=0),
            jnp.concatenate([other, own], axis=0),
        )
        return pick_columns(both, index)
    tall = rows // 2
    half = pl.BlockSpec((tall, wide), lambda i: (i % 2, 0))
    return pl.pallas_call(
        partial(_join_kernel, count),
        grid=(4,),
        in_specs=[pl.BlockSpec(memory_space=pltpu.SMEM), half, half],
        out_specs=pl.BlockSpec((tall, wide), lambda i: (i, 0)),
        out_shape=jax.ShapeDtypeStruct((2 * rows, wide), own.dtype),
        compiler_params=_params(),
        cost_estimate=_cost(4),
        name="join_columns",
    )(jnp.concatenate([index, bit[None].astype(jnp.int32)]), own, other)


def low(value):
    return value.astype(jnp.bfloat16)


class Gather:
    def __init__(self, first, second):
        self.count = lax.axis_size("seq")
        self.half = self.count // 2
        self.held = ({0: first}, {0: second})

    def fresh(self, slot):
        return [self.held[slot]] if slot < 2 else []

    def send(self, slot):
        step, second = slot // 2 + 1, slot % 2
        held = self.held[second]
        back, forth = (self.count - step) % self.count, step
        keys = []
        if step < self.half or not second:
            held[back] = send_up(held[(back + 1) % self.count])
            keys.append((held, back))
        if step < self.half or second:
            held[forth] = send_down(held[forth - 1])
            keys.append((held, forth))
        return keys


class Scatter:
    def __init__(self, first, second):
        self.count = lax.axis_size("seq")
        self.half = self.count // 2
        self.terms = (first, second)
        self.got = ({}, {})

    def places(self, slot):
        step, second = slot // 2, slot % 2
        up = self.half - step - (1 if second else 0)
        down = self.half + step + (0 if second else 1)
        return up, down

    def fresh(self, slot):
        if slot > 1:
            return []
        self.first = {0: dict(zip(("up", "down"), map(self.terms[slot], self.places(slot))))}
        return [self.first]

    def send(self, slot):
        got = self.got[slot % 2]
        keys = []
        for way, send, place in zip(("up", "down"), (send_up, send_down), self.places(slot)):
            if 0 < place < self.count:
                if way in got:
                    term = self.terms[slot % 2](place)
                    term = low(term.astype(jnp.float32) + got[way].astype(jnp.float32))
                else:
                    term = self.first[0][way]
                got[way] = send(term)
                keys.append((got, way))
        return keys

    def sums(self):
        return [
            terms(0).astype(jnp.float32) + got["up"].astype(jnp.float32) + got["down"].astype(jnp.float32)
            for terms, got in zip(self.terms, self.got)
        ]


class Flow:
    def __init__(self, token):
        self.flying = []
        self.token = token

    def step(self, ring, stage, values=()):
        each = lax.axis_size("seq") // 8
        for slot in range(stage * each, (stage + 1) * each):
            fresh = ring.fresh(slot)
            new = 1 if slot // 2 == ring.half - 1 else 2
            keys = []
            while self.flying and (
                sum(len(sent) for _, _, sent in self.flying) + new > 4
                or any(other is ring and was <= slot - 2 for other, was, _ in self.flying)
            ):
                keys += self.flying.pop(0)[2]
            arrived, first, values, self.token = lax.optimization_barrier(
                (
                    [held[key] for held, key in keys],
                    [held[0] for held in fresh],
                    values,
                    self.token,
                )
            )
            for held, value in zip(fresh, first):
                held[0] = value
            for (held, key), value in zip(keys, arrived):
                held[key] = value
            self.flying.append((ring, slot, ring.send(slot)))
        return values


def _rows_dot_kernel(count, operands, outs, *refs):
    size = len(operands)
    value_ref = refs[0]
    weights = [refs[1 + one * count : 1 + (one + 1) * count] for one in range(size)]
    out_refs = refs[1 + size * count : -1 - size]
    held = refs[-1 - size : -1]
    sems = refs[-1]

    def copy(one, place):
        first, columns = operands[one]
        piece = weights[one][place].shape[0]
        return pltpu.make_async_copy(
            weights[one][place].at[:, pl.ds(first, columns)],
            held[one].at[pl.ds(place * piece, piece)],
            sems.at[one, place],
        )

    for one in range(size):
        for place in range(count):
            copy(one, place).start()
    for one in range(size):
        for place in range(count):
            copy(one, place).wait()
        for source, start, columns, out, at in outs:
            if source == one:
                out_refs[out][:, at : at + columns] = jnp.dot(
                    value_ref[...],
                    held[one][:, start : start + columns],
                    preferred_element_type=jnp.float32,
                ).astype(out_refs[out].dtype)


def rows_dot(value, operands, outs, shapes):
    count = len(operands[0][0])
    vmem = pl.BlockSpec(memory_space=pltpu.VMEM)
    ranges = [(first, columns) for _, first, columns in operands]
    whole = [
        jax.ShapeDtypeStruct((value.shape[1], columns), jnp.bfloat16) for _, columns in ranges
    ]
    results = pl.pallas_call(
        partial(_rows_dot_kernel, count, ranges, outs),
        in_specs=[vmem] + [pl.BlockSpec(memory_space=pl.ANY)] * (len(operands) * count),
        out_specs=[vmem] * (len(shapes) + len(whole)),
        out_shape=list(shapes) + whole,
        scratch_shapes=[pltpu.SemaphoreType.DMA((len(operands), count))],
        compiler_params=pltpu.CompilerParams(vmem_limit_bytes=60 * 1024 * 1024),
        cost_estimate=_cost(12),
        name="rows_dot",
    )(value, *[pieces[place] for pieces, _, _ in operands for place in range(count)])
    return results[: len(shapes)], results[len(shapes) :]


def _glu_early_kernel(count, *refs):
    half = count // 2
    late = (half - 1, half, half + 1)
    value_ref = refs[0]
    weights = (refs[1 : 1 + count], refs[1 + count : 1 + 2 * count])
    outs = refs[1 + 2 * count : 3 + 2 * count]
    held = refs[3 + 2 * count : 5 + 2 * count]
    sems = refs[-1]
    piece = weights[0][0].shape[0]
    places = [place for place in range(count) if place not in late]

    def copy(one, place):
        return pltpu.make_async_copy(
            weights[one][place], held[one].at[pl.ds(place * piece, piece)], sems.at[one, place]
        )

    for one in range(2):
        for place in places:
            copy(one, place).start()
    stop, again = (half - 1) * piece, (half + 2) * piece
    for one in range(2):
        held[one][stop:again] = jnp.zeros((3 * piece, held[one].shape[1]), jnp.bfloat16)
    for one in range(2):
        for place in places:
            copy(one, place).wait()
        outs[one][...] = jnp.dot(
            value_ref[:, :stop], held[one][:stop], preferred_element_type=jnp.float32
        ) + jnp.dot(value_ref[:, again:], held[one][again:], preferred_element_type=jnp.float32)


def glu_early(value, gates, ups):
    count = lax.axis_size("seq")
    vmem = pl.BlockSpec(memory_space=pltpu.VMEM)
    columns = gates[0].shape[1]
    return pl.pallas_call(
        partial(_glu_early_kernel, count),
        in_specs=[vmem] + [pl.BlockSpec(memory_space=pl.ANY)] * (2 * count),
        out_specs=[vmem] * 4,
        out_shape=[jax.ShapeDtypeStruct((value.shape[0], columns), jnp.float32)] * 2
        + [jax.ShapeDtypeStruct((value.shape[1], columns), jnp.bfloat16)] * 2,
        scratch_shapes=[pltpu.SemaphoreType.DMA((2, count))],
        compiler_params=pltpu.CompilerParams(vmem_limit_bytes=60 * 1024 * 1024),
        cost_estimate=_cost(14),
        name="glu_early",
    )(
        value,
        *[gates.get(place, gates[0]) for place in range(count)],
        *[ups.get(place, ups[0]) for place in range(count)],
    )


def _glu_late_kernel(value_ref, *refs):
    gates_refs, ups_refs = refs[:3], refs[3:6]
    gate_ref, up_ref, grad_ref, act_ref, dgate_ref, dup_ref = refs[6:]
    columns = grad_ref.shape[1]
    piece = gates_refs[0].shape[0]
    wide = 256
    for start in range(0, columns, wide):
        part = slice(start, min(start + wide, columns))
        gate, up = gate_ref[:, part], up_ref[:, part]
        for one in range(3):
            value = value_ref[:, one * piece : (one + 1) * piece]
            gate = gate + jnp.dot(
                value, gates_refs[one][:, part], preferred_element_type=jnp.float32
            )
            up = up + jnp.dot(value, ups_refs[one][:, part], preferred_element_type=jnp.float32)
        grad = grad_ref[:, part]
        sig = jax.nn.sigmoid(gate)
        act = gate * sig
        act_ref[:, part] = low(act * up)
        dgate_ref[:, part] = low(grad * up * (sig * (1.0 + gate * (1.0 - sig))))
        dup_ref[:, part] = low(grad * act)


def glu_late(value, gates, ups, sums, grad):
    rows, columns = grad.shape
    tall = rows // 4

    def by_rows(wide):
        return pl.BlockSpec((tall, wide), lambda i: (i, 0))

    whole = pl.BlockSpec(gates[0].shape, lambda i: (0, 0))
    return pl.pallas_call(
        _glu_late_kernel,
        grid=(4,),
        in_specs=[by_rows(value.shape[1])] + [whole] * 6 + [by_rows(columns)] * 3,
        out_specs=[by_rows(columns)] * 3,
        out_shape=[jax.ShapeDtypeStruct(grad.shape, jnp.bfloat16)] * 3,
        compiler_params=_params(),
        cost_estimate=_cost(8),
        name="glu_late",
    )(value, *gates, *ups, *sums, grad)


def swap(value, axis, bit):
    count = lax.axis_size(axis)
    return lax.ppermute(value, axis, [(one, one ^ bit) for one in range(count)])


def gather_round(held, bit):
    other = swap(held, "seq", bit)
    return jnp.where(
        (lax.axis_index("seq") & bit) == 0,
        jnp.concatenate([held, other], axis=0),
        jnp.concatenate([other, held], axis=0),
    )


def bits_of(axis):
    return [1 << bit for bit in range(lax.axis_size(axis).bit_length() - 1)]


def own_half(value):
    rows = value.shape[0] // 2
    return lax.dynamic_slice_in_dim(value, (lax.axis_index("head") & 1) * rows, rows, 0)


def other_half(value):
    rows = value.shape[0] // 2
    return lax.dynamic_slice_in_dim(value, (1 - (lax.axis_index("head") & 1)) * rows, rows, 0)


def both_halves(value):
    other = swap(value, "head", 1)
    return jnp.where(
        (lax.axis_index("head") & 1) == 0,
        jnp.concatenate([value, other], axis=0),
        jnp.concatenate([other, value], axis=0),
    )


def summed_pair(partial_rows):
    pair = own_half(partial_rows).astype(jnp.float32) + swap(
        other_half(low(partial_rows)), "head", 1
    ).astype(jnp.float32)
    return pair


def summed_over_head(value):
    if lax.axis_size("head") == 4:
        one, two, three = (swap(value, "head", bits) for bits in (1, 2, 3))
        return (value + one) + (two + three)
    for bit in bits_of("head"):
        value = value + swap(value, "head", bit)
    return value


def asked(total):
    bits = bits_of("head")[1:]
    for bit in bits[:-1]:
        total = total + swap(low(total), "head", bit).astype(jnp.float32)
    return total, swap(low(total), "head", bits[-1])


def summed(parts):
    return parts[0] + parts[1].astype(jnp.float32)


def chunk_of(value, index):
    piece = value.shape[-1] // lax.axis_size("seq")
    return value[..., index * piece : (index + 1) * piece]


def dot(a, b):
    return jnp.dot(a, b, preferred_element_type=jnp.float32)


def dot_tn(a, b):
    return lax.dot_general(a, b, (((0,), (0,)), ((), ())), preferred_element_type=jnp.float32)


def dot_nt(a, b):
    return lax.dot_general(a, b, (((1,), (1,)), ((), ())), preferred_element_type=jnp.float32)


def after(values, others):
    return lax.optimization_barrier((values, others))[0]


def passed_along(value, steps):
    count = lax.axis_size("seq")
    leading, last = (max(0, -steps), min(count, count - steps))
    return lax.ppermute(
        value, "seq", [(source, source + steps) for source in range(leading, last)]
    )


def adam_update(master, first_m, second_m, gradient, step_rate, decay_rate):
    first_new = beta_one * first_m + (1.0 - beta_one) * gradient
    second_new = beta_two * second_m + (1.0 - beta_two) * gradient * gradient
    first_hat = first_new / (1.0 - beta_one**STEP)
    second_hat = second_new / (1.0 - beta_two**STEP)
    master_new = master - step_rate * (
        first_hat / (jnp.sqrt(second_hat) + eps_adam) + decay_rate * master
    )
    return (master_new, first_new, second_new)


def norm_back(rows, inv, gain, grad):
    weighted = grad * gain
    mean = jnp.mean(weighted * rows, axis=-1, keepdims=True)
    return inv * weighted - rows * (inv * inv * inv) * mean


def inverse_size(rows):
    return lax.rsqrt(jnp.mean(rows * rows, axis=-1, keepdims=True) + eps_norm)


def per_device(
    block_input, cotangent, lengths,
    proj_master, proj_first, proj_second,
    beta_master, beta_first, beta_second,
    conv_master, conv_first, conv_second,
    out_master, out_first, out_second,
    mlp_master, mlp_first, mlp_second,
    down_master, down_first, down_second,
    gains_master, gains_first, gains_second,
):
    bf16, f32 = jnp.bfloat16, jnp.float32
    count = lax.axis_size("seq")
    seq_index = lax.axis_index("seq")
    rows = block_input.shape[0]
    width = proj_master.shape[2]
    units = mlp_master.shape[2]
    shard = proj_master.shape[1]
    heads = width // DK
    scal = jnp.stack([lengths[0] - seq_index * rows, seq_index * rows]).astype(jnp.int32)
    flow = Flow(lengths)
    sizes = [conv_master.size, beta_master.size, gains_master.size]
    packed = low(
        jnp.concatenate(
            [conv_master.reshape(-1), beta_master.reshape(-1), gains_master.reshape(-1)]
        )
    )
    small = jnp.pad(packed, (0, -packed.size % 2048))[None]
    seq_bits = bits_of("seq")
    small = gather_round(small, seq_bits[0])
    proj_low = low(proj_master)
    ring_p = Gather(
        jnp.concatenate([proj_low[0], proj_low[1]], axis=1),
        jnp.concatenate([proj_low[2], proj_low[3]], axis=1),
    )
    flow.step(ring_p, 0)
    flow.step(ring_p, 1)
    cut = (units + width) // 2 // DK * DK
    rest = units - cut
    down_low = jnp.transpose(low(down_master))
    out_low = jnp.transpose(low(out_master))
    mlp_low = low(mlp_master)
    sources, targets = ring_sources(), ring_targets()
    x_ring = pick_columns(block_input, sources)
    dy_ring = pick_columns(cotangent, sources)
    x_rows = x_ring.astype(f32)
    x_inv = inverse_size(x_rows)
    x_ring, dy_ring, x_inv = flow.step(ring_p, 2, (x_ring, dy_ring, x_inv))
    x_rows = x_ring.astype(f32)
    small = flow.step(ring_p, 3, small)
    ring_do = Gather(
        down_low[:, :cut], jnp.concatenate([down_low[:, cut:], out_low], axis=1)
    )
    ring_m = Gather(mlp_low[0], mlp_low[1])
    small = gather_round(small, seq_bits[1])
    flow.step(ring_p, 4)
    ring_do.held[0][0], ring_do.held[1][0], ring_m.held[0][0], ring_m.held[1][0], small = flow.step(
        ring_p,
        5,
        (ring_do.held[0][0], ring_do.held[1][0], ring_m.held[0][0], ring_m.held[1][0], small),
    )
    flow.step(ring_p, 6)
    for bit in seq_bits[2:]:
        small = gather_round(small, bit)
    small = flow.step(ring_p, 7, small)
    conv_all = small[:, : sizes[0]].reshape(count, 3, CONV, -1)
    taps = jnp.transpose(conv_all, (1, 2, 0, 3)).reshape(3, CONV, width).astype(f32)
    beta_all = small[:, sizes[0] : sizes[0] + sizes[1]].reshape(D, heads)
    gains_all = small[:, sizes[0] + sizes[1] : sum(sizes)].reshape(-1)
    columns = jnp.concatenate([gains_all[: 2 * D].reshape(2, D), jnp.transpose(beta_all)], axis=0)
    columns = jnp.take(columns.reshape(2 + heads, count, -1), sources, axis=1).reshape(-1, D)
    gain_a = columns[0:1].astype(f32)
    gain_m = columns[1:2].astype(f32)
    w_beta = columns[2:]
    gain_o = gains_all[2 * D :].astype(f32)[None]
    hidden = (x_rows * x_inv * gain_a).astype(bf16)
    hidden = flow.step(ring_do, 0, hidden)
    logits = dot_nt(hidden, w_beta)
    logits = flow.step(ring_do, 1, logits)
    w_qk, w_vg = ring_p.held
    low_rows = jax.ShapeDtypeStruct((rows, width), bf16)
    (pre_q, pre_k, pre_v, gate), (w_qk, w_vg) = rows_dot(
        hidden,
        [(w_qk, 0, 2 * width), (w_vg, 0, 2 * width)],
        [(0, 0, width, 0, 0), (0, width, width, 1, 0), (1, 0, width, 2, 0), (1, width, width, 3, 0)],
        [low_rows] * 3 + [jax.ShapeDtypeStruct((rows, width), f32)],
    )
    pre = (pre_q, pre_k, pre_v)
    pre, gate = flow.step(ring_do, 2, (pre, gate))
    halo = passed_along(jnp.concatenate([one[rows - 16 :] for one in pre], axis=1), 1)
    halo = flow.step(ring_do, 3, halo)
    q, k, w, uv, t, state_add, state_map = delta_local(scal, pre, halo, taps, logits)
    state_add, state_map = flow.step(ring_do, 4, (state_add, state_map))
    hops = -(-5 * count // 8) - 1
    state_in = passed_along(low(state_add), 1)

    def hop(state):
        moved = jnp.einsum("hij,hjk->hik", state_map, state, preferred_element_type=f32)
        return passed_along(low(moved + state_add), 1)

    state_in = flow.step(ring_do, 5, state_in)
    third = (hops - 1) // 3
    for _ in range(third):
        state_in = hop(state_in)
    state_in = flow.step(ring_do, 6, state_in)
    for _ in range(third):
        state_in = hop(state_in)
    state_in = flow.step(ring_do, 7, state_in)
    for _ in range(hops - 1 - 2 * third):
        state_in = hop(state_in)
    state_in = flow.step(ring_m, 0, state_in)
    normed, out_rows, change, states = delta_apply(scal, q, k, w, uv, state_in, gate, gain_o)
    normed = flow.step(ring_m, 1, normed)
    w_do_a, w_do_b = ring_do.held
    (grad_act,), (w_down_a, w_down_b, w_out) = rows_dot(
        dy_ring,
        [(w_do_a, 0, cut), (w_do_b, 0, rest), (w_do_b, rest, width)],
        [(0, 0, cut, 0, 0), (1, 0, rest, 0, cut)],
        [jax.ShapeDtypeStruct((rows, units), f32)],
    )
    w_out, normed, grad_act = flow.step(ring_m, 2, (w_out, normed, grad_act))
    pair = summed_pair(low(dot_nt(normed, w_out)))
    pair = flow.step(ring_m, 3, pair)
    parts = asked(pair)
    flow.step(ring_m, 4)
    parts = flow.step(ring_m, 5, parts)
    x_one = own_half(x_rows) + summed(parts)
    one_inv = inverse_size(x_one)
    h_two = both_halves(low(x_one * one_inv * gain_m))
    h_two, x_one = flow.step(ring_m, 6, (h_two, x_one))
    gates, ups = ring_m.held
    half = count // 2
    *sums, w_mlp_g, w_mlp_u = glu_early(
        h_two,
        {one: piece for one, piece in gates.items() if abs(one - half) > 1},
        {one: piece for one, piece in ups.items() if abs(one - half) > 1},
    )
    sums, w_mlp_g, w_mlp_u, h_two = flow.step(ring_m, 7, (sums, w_mlp_g, w_mlp_u, h_two))
    late = (half - 1, half, half + 1)
    shard = proj_master.shape[1]
    act_low, grad_gate_u, grad_up_u = glu_late(
        h_two[:, late[0] * shard : (late[-1] + 1) * shard],
        [gates[one] for one in late],
        [ups[one] for one in late],
        sums,
        grad_act,
    )
    def rows_of(value):
        piece = value.shape[0] // count
        return lambda one: value[one * piece : (one + 1) * piece]

    back_m = Scatter(
        rows_of(low(dot_tn(h_two, grad_gate_u))), rows_of(low(dot_tn(h_two, grad_up_u)))
    )
    flow.step(back_m, 0)
    grad_gate_u, grad_up_u, act_low, w_mlp_g, w_mlp_u = flow.step(
        back_m, 1, (grad_gate_u, grad_up_u, act_low, w_mlp_g, w_mlp_u)
    )
    for one in late:
        w_mlp_g = lax.dynamic_update_slice_in_dim(w_mlp_g, gates[one], one * shard, 0)
        w_mlp_u = lax.dynamic_update_slice_in_dim(w_mlp_u, ups[one], one * shard, 0)
    part = low(dot_nt(grad_gate_u, w_mlp_g) + dot_nt(grad_up_u, w_mlp_u))
    part = flow.step(back_m, 2, part)
    pair, act_low = flow.step(back_m, 3, (summed_pair(part), act_low))
    parts = asked(pair)
    part = low(dot_nt(act_low[:, :cut], w_down_a) + dot_nt(act_low[:, cut:], w_down_b))
    part = flow.step(back_m, 4, part)
    parts, part = flow.step(back_m, 5, (parts, part))
    mlp_pair = summed_pair(part)
    grad_h_two = summed(parts)
    grad_gain_m = 0.5 * jnp.sum(grad_h_two * x_one * one_inv, axis=0, keepdims=True)
    grad_x_one = own_half(dy_ring).astype(f32) + norm_back(x_one, one_inv, gain_m, grad_h_two)
    grad_attn = both_halves(low(grad_x_one))
    grad_normed = dot(grad_attn, w_out)
    grad_normed, grad_attn, mlp_pair, act_low = flow.step(
        back_m, 6, (grad_normed, grad_attn, mlp_pair, act_low)
    )
    mlp_parts = asked(mlp_pair)
    grad_gate, grad_gain_o, grad_out, through, carry = delta_back_local(
        scal, grad_normed, gate, gain_o, out_rows, q, k, w
    )
    grad_gate, carry, grad_attn, act_low = flow.step(
        back_m, 7, (grad_gate, carry, grad_attn, act_low)
    )
    grad_do_a = low(dot_tn(dy_ring, act_low[:, :cut]))
    grad_do_b = jnp.concatenate(
        [low(dot_tn(dy_ring, act_low[:, cut:])), low(dot_tn(grad_attn, normed))], axis=1
    )
    back_do = Scatter(rows_of(grad_do_a), rows_of(grad_do_b))

    def hop_back(state):
        moved = jnp.einsum("hji,hjk->hik", state_map, state, preferred_element_type=f32)
        return passed_along(low(moved + carry), -1)

    grad_gate, carry = flow.step(back_do, 0, (grad_gate, carry))
    above = passed_along(low(carry), -1)
    above, mlp_parts = flow.step(back_do, 1, (above, mlp_parts))
    for _ in range(third):
        above = hop_back(above)
    above = flow.step(back_do, 2, above)
    for _ in range(third):
        above = hop_back(above)
    above = flow.step(back_do, 3, above)
    for _ in range(hops - 1 - 2 * third):
        above = hop_back(above)
    above, mlp_sum = flow.step(back_do, 4, (above, summed(mlp_parts)))
    grad_pre, tail, back_halo, grad_taps, grad_logits = delta_back(
        scal, pre, halo, taps, logits, q, k, w, t, change, states, grad_out, through, above
    )
    fixed = low(tail + passed_along(back_halo, -1))
    grad_logits = low(grad_logits)
    grad_pre = lax.dynamic_update_slice_in_dim(grad_pre, fixed, rows - 8, 1)
    grad_qk = jnp.concatenate([grad_pre[0], grad_pre[1]], axis=1)
    grad_vg = jnp.concatenate([grad_pre[2], grad_gate], axis=1)
    grad_w_qk = low(dot_tn(hidden, grad_qk))
    grad_w_qk, grad_qk, grad_vg, grad_logits, grad_taps = flow.step(
        back_do, 5, (grad_w_qk, grad_qk, grad_vg, grad_logits, grad_taps)
    )
    grad_beta = dot_tn(grad_logits, hidden)
    grad_conv = jnp.transpose(
        grad_taps.reshape(3, CONV, count, width // count), (2, 0, 1, 3)
    ).reshape(count, -1)
    grad_hidden = low(
        dot_nt(grad_qk, w_qk) + dot_nt(grad_vg, w_vg) + dot(grad_logits, w_beta)
    )
    grad_gain_a = jnp.sum(grad_hidden.astype(f32) * x_rows * x_inv, axis=0, keepdims=True)
    grad_hidden, grad_gain_a, grad_vg = flow.step(
        back_do, 6, (grad_hidden, grad_gain_a, grad_vg)
    )
    stacked = jnp.concatenate([grad_gain_a, grad_gain_m, grad_beta], axis=0)
    stacked = jnp.take(stacked.reshape(2 + heads, count, -1), targets, axis=1).reshape(-1, D)
    grad_gains = jnp.concatenate(
        [stacked[:2].reshape(-1), jnp.sum(grad_gain_o[:, 0], axis=0)]
    ).reshape(count, -1)
    grad_beta = jnp.transpose(stacked[2:]).reshape(count, -1)
    small = jnp.stack(
        [
            jnp.pad(low(one), ((0, 0), (0, 2 * width - one.shape[1])))
            for one in (grad_conv, grad_beta, grad_gains)
        ],
        axis=1,
    )
    small = jnp.pad(jnp.take(small, sources, axis=0), ((0, 0), (0, 13), (0, 0)))
    grad_w_vg = low(dot_tn(hidden, grad_vg)).reshape(count, -1, 2 * width)
    grad_w_vg = jnp.concatenate([grad_w_vg, small], axis=1)
    grad_w_vg = flow.step(back_do, 7, grad_w_vg)
    back_p = Scatter(rows_of(grad_w_qk), lambda one: grad_w_vg[one])
    flow.step(back_p, 0)
    flow.step(back_p, 1)
    grad_hidden, mlp_master, mlp_sum = flow.step(
        back_p, 2, (grad_hidden, mlp_master, mlp_sum)
    )
    pair = summed_pair(grad_hidden)
    result = join_columns(x_one + mlp_sum, targets)
    pair, result, down_master, out_master = flow.step(
        back_p, 3, (pair, result, down_master, out_master)
    )
    parts = asked(pair)
    mlp_g_sum, mlp_u_sum = back_m.sums()
    mlp_new, mlp_first_new, mlp_second_new = adam_update(
        mlp_master, mlp_first, mlp_second, jnp.stack([mlp_g_sum, mlp_u_sum]),
        rate_matrix, decay_matrix,
    )
    mlp_new, mlp_first_new, mlp_second_new = flow.step(
        back_p, 4, (mlp_new, mlp_first_new, mlp_second_new)
    )
    do_a_sum, do_b_sum = back_do.sums()
    summed_down = jnp.transpose(jnp.concatenate([do_a_sum, do_b_sum[:, :rest]], axis=1))
    out_sum = jnp.transpose(do_b_sum[:, rest:])
    down_new, down_first_new, down_second_new = adam_update(
        down_master, down_first, down_second, summed_down, rate_down, decay_matrix
    )
    out_new, out_first_new, out_second_new = adam_update(
        out_master, out_first, out_second, out_sum, rate_matrix, decay_matrix
    )
    parts, down_new, down_first_new, down_second_new = flow.step(
        back_p, 5, (parts, down_new, down_first_new, down_second_new)
    )
    grad_x_rest = norm_back(own_half(x_rows), own_half(x_inv), gain_a, summed(parts))
    input_half = grad_x_one + grad_x_rest
    input_half, out_new, out_first_new, out_second_new = flow.step(
        back_p, 6, (input_half, out_new, out_first_new, out_second_new)
    )
    input_grad = flow.step(back_p, 7, join_columns(input_half, targets))
    qk_sum, vg_sum = back_p.sums()
    small_sum = [vg_sum[shard + one, : sizes[one]] for one in range(3)]
    vg_sum = vg_sum[:shard]
    gains_sum = small_sum[2]
    gains_sum = summed_over_head(gains_sum)
    summed_conv = small_sum[0].reshape(conv_master.shape)
    summed_beta = small_sum[1].reshape(beta_master.shape)
    summed_proj = jnp.stack(
        [qk_sum[:, :width], qk_sum[:, width:], vg_sum[:, :width], vg_sum[:, width:]]
    )
    proj_new, proj_first_new, proj_second_new = adam_update(
        proj_master, proj_first, proj_second, summed_proj, rate_matrix, decay_matrix
    )
    beta_new, beta_first_new, beta_second_new = adam_update(
        beta_master, beta_first, beta_second, summed_beta, rate_beta, decay_matrix
    )
    conv_new, conv_first_new, conv_second_new = adam_update(
        conv_master, conv_first, conv_second, summed_conv, rate_conv, decay_matrix
    )
    gains_new, gains_first_new, gains_second_new = adam_update(
        gains_master, gains_first, gains_second, gains_sum, rate_gains, 0.0
    )
    return (
        result,
        input_grad,
        proj_new, proj_first_new, proj_second_new, proj_new.astype(bf16),
        beta_new, beta_first_new, beta_second_new, beta_new.astype(bf16),
        conv_new, conv_first_new, conv_second_new, conv_new.astype(bf16),
        out_new, out_first_new, out_second_new, out_new.astype(bf16),
        mlp_new, mlp_first_new, mlp_second_new, mlp_new.astype(bf16),
        down_new, down_first_new, down_second_new, down_new.astype(bf16),
        gains_new, gains_first_new, gains_second_new,
    )


def solution(mesh):
    rows = P("seq", None)
    proj = P(None, "seq", "head")
    tall = P("seq", "head")
    conv = P(None, None, ("head", "seq"))
    flat = P("head", "seq")
    gains = P("seq")
    return jax.shard_map(
        per_device,
        mesh=mesh,
        in_specs=(rows, rows, P())
        + (proj,) * 3
        + (tall,) * 3
        + (conv,) * 3
        + (flat,) * 3
        + (proj,) * 3
        + (flat,) * 3
        + (gains,) * 3,
        out_specs=(rows, rows)
        + (proj,) * 4
        + (tall,) * 4
        + (conv,) * 4
        + (flat,) * 4
        + (proj,) * 4
        + (flat,) * 4
        + (gains,) * 3,
        check_vma=False,
    )
```

```python
from functools import partial

import jax
import jax.numpy as jnp
from jax import lax
from jax.experimental import pallas as pl
from jax.experimental.pallas import tpu as pltpu
from jax.sharding import PartitionSpec as P

D = 2048
DK = 128
CONV = 4
SPAN = 64
STEP = 10

eps_norm = 1e-05
eps_unit = 1e-06
beta_one = 0.9
beta_two = 0.95
eps_adam = 1e-08
rate_matrix = 0.04
rate_beta = 0.12
rate_down = 0.03
rate_conv = 0.3
rate_gains = 0.4
decay_matrix = 0.1


SPANROWS = 128


def _mm(a, b):
    return jnp.dot(
        a.astype(jnp.bfloat16), b.astype(jnp.bfloat16), preferred_element_type=jnp.float32
    )


def _mm_nt(a, b):
    return lax.dot_general(
        a.astype(jnp.bfloat16),
        b.astype(jnp.bfloat16),
        (((1,), (1,)), ((), ())),
        preferred_element_type=jnp.float32,
    )


def _mm_tn(a, b):
    return lax.dot_general(
        a.astype(jnp.bfloat16),
        b.astype(jnp.bfloat16),
        (((0,), (0,)), ((), ())),
        preferred_element_type=jnp.float32,
    )


def _pair_masks():
    row = lax.broadcasted_iota(jnp.int32, (SPANROWS, SPANROWS), 0)
    col = lax.broadcasted_iota(jnp.int32, (SPANROWS, SPANROWS), 1)
    same = (row // SPAN) == (col // SPAN)
    return row, col, same


def _tap_masks(scal_ref, rows):
    edge, base = scal_ref[0], scal_ref[1]
    token = lax.broadcasted_iota(jnp.int32, (rows, DK), 0)
    after = token >= edge
    masks = [None]
    for shift in range(1, CONV):
        good = jnp.where(after, token - edge, token + base) >= shift
        masks.append(good.astype(jnp.float32))
    return masks


def _keep(scal_ref, span):
    edge, base = scal_ref[0], scal_ref[1]
    start = span * SPAN
    hit = (edge == start) | ((base + start) == 0)
    return jnp.where(hit, 0.0, 1.0).astype(jnp.float32)


def _convolved(ext_ref, pre, halo, taps, masks):
    rows = pre.shape[0]
    ext_ref[0:8] = halo[8:16].astype(jnp.float32)
    ext_ref[8 : 8 + rows] = pre.astype(jnp.float32)
    total = taps[CONV - 1 : CONV] * ext_ref[8 : 8 + rows]
    for shift in range(1, CONV):
        total = (
            total
            + taps[CONV - 1 - shift : CONV - shift]
            * ext_ref[8 - shift : 8 - shift + rows]
            * masks[shift]
        )
    return total


def _unit(act):
    return act * lax.rsqrt(jnp.sum(act * act, axis=-1, keepdims=True) + eps_unit)


def _column(table, index):
    lane = lax.broadcasted_iota(jnp.int32, table.shape, 1)
    return jnp.sum(jnp.where(lane == index, table, 0.0), axis=1, keepdims=True)


def _local_kernel(
    heads, scal_ref, pre_q, pre_k, pre_v, halo_q, halo_k, halo_v, taps_ref, logit_ref, q_ref, k_ref,
    w_ref, uv_ref, t_ref, bt_ref, pt_ref, ext_ref,
):
    pre_refs, halo_refs = (pre_q, pre_k, pre_v), (halo_q, halo_k, halo_v)
    rows = pre_q.shape[0]
    pairs = rows // SPANROWS
    masks = _tap_masks(scal_ref, rows)
    row, col, same = _pair_masks()
    strict = same & (row > col)
    eye = (row == col).astype(jnp.float32)
    levels = []
    for bit in range(6):
        inside = ((row >> (bit + 1)) == (col >> (bit + 1))) & same
        levels.append(
            (inside & (((row >> bit) & 1) == 1) & (((col >> bit) & 1) == 0)).astype(jnp.float32)
        )
    logit = logit_ref[...]
    first_head = pl.program_id(0) * heads
    keys, lowers, sides = [], [], []
    for head in range(heads):
        lanes = slice(head * DK, (head + 1) * DK)
        beta = jax.nn.sigmoid(_column(logit, first_head + head))
        acts = []
        for part in range(3):
            mixed = _convolved(
                ext_ref.at[head * 3 + part], pre_refs[part][:, lanes], halo_refs[part][:, lanes],
                taps_ref[part, :, lanes], masks,
            )
            acts.append(mixed * jax.nn.sigmoid(mixed))
        query = _unit(acts[0])
        key = _unit(acts[1])
        q_ref[:, lanes] = query.astype(jnp.bfloat16)
        key_low = key.astype(jnp.bfloat16)
        k_ref[:, lanes] = key_low
        side = jnp.concatenate([beta * key, beta * acts[2]], axis=1).astype(jnp.bfloat16)
        for pair in range(pairs):
            part = slice(pair * SPANROWS, (pair + 1) * SPANROWS)
            gram = _mm_nt(key_low[part], key_low[part])
            lowers.append(jnp.where(strict, gram * beta[part], 0.0))
            sides.append(side[part])
        keys.append(key_low)
    inverses = [eye - low * levels[0] for low in lowers]
    for bit in range(1, 6):
        middle = [_mm(low * levels[bit], inv) for low, inv in zip(lowers, inverses)]
        inverses = [inv - _mm(inv, mid) for mid, inv in zip(middle, inverses)]
    carried = []
    w_all, uv_all = [], []
    for head in range(heads):
        lanes = slice(head * DK, (head + 1) * DK)
        w_rows, uv_rows = [], []
        for pair in range(pairs):
            part = slice(pair * SPANROWS, (pair + 1) * SPANROWS)
            inv = inverses[head * pairs + pair].astype(jnp.bfloat16)
            t_ref[part, lanes] = inv
            both = _mm(inv, sides[head * pairs + pair])
            w_part = both[:, :DK].astype(jnp.bfloat16)
            w_ref[part, lanes] = w_part
            uv_ref[part, lanes] = both[:, DK:]
            w_rows.append(w_part)
            uv_rows.append(both[:, DK:])
        w_all.append(w_rows)
        uv_all.append(uv_rows)
        carried.append(jnp.concatenate([jnp.zeros((DK, DK), jnp.float32), eye], axis=1))
    for span in range(rows // SPAN):
        keep = _keep(scal_ref, span)
        pair, half = divmod(span, SPANROWS // SPAN)
        part = slice(half * SPAN, (half + 1) * SPAN)
        for head in range(heads):
            state = carried[head] * keep
            w_part = w_all[head][pair][part]
            source = jnp.concatenate(
                [uv_all[head][pair][part], jnp.zeros((SPAN, DK), jnp.float32)], axis=1
            )
            change = source - _mm(w_part, state)
            carried[head] = state + _mm_tn(
                keys[head][span * SPAN : (span + 1) * SPAN], change
            )
    for head in range(heads):
        bt_ref[head] = carried[head][:, :DK]
        pt_ref[head] = carried[head][:, DK:].astype(jnp.bfloat16)


def _apply_kernel(
    heads, scal_ref, q_ref, k_ref, w_ref, uv_ref, state_ref, gate_ref, gain_ref, n_ref, o_ref,
    u_ref, s_ref,
):
    rows = q_ref.shape[0]
    pairs = rows // SPANROWS
    row, col, same = _pair_masks()
    lower = same & (row >= col)
    states = [state_ref[head].astype(jnp.float32) for head in range(heads)]
    moved = [[] for _ in range(heads)]
    crossed = [[] for _ in range(heads)]
    for span in range(rows // SPAN):
        keep = _keep(scal_ref, span)
        part = slice(span * SPAN, (span + 1) * SPAN)
        for head in range(heads):
            lanes = slice(head * DK, (head + 1) * DK)
            state = states[head] * keep
            state_low = state.astype(jnp.bfloat16)
            s_ref[head, span] = state_low
            both = _mm(
                jnp.concatenate([w_ref[part, lanes], q_ref[part, lanes]], axis=0), state_low
            )
            change = (uv_ref[part, lanes] - both[:SPAN]).astype(jnp.bfloat16)
            crossed[head].append(both[SPAN:])
            moved[head].append(change)
            states[head] = state + _mm_tn(k_ref[part, lanes], change)
    for head in range(heads):
        lanes = slice(head * DK, (head + 1) * DK)
        for pair in range(pairs):
            part = slice(pair * SPANROWS, (pair + 1) * SPANROWS)
            change = jnp.concatenate([moved[head][2 * pair], moved[head][2 * pair + 1]], axis=0)
            cross = jnp.concatenate([crossed[head][2 * pair], crossed[head][2 * pair + 1]], axis=0)
            u_ref[part, lanes] = change
            scores = jnp.where(lower, _mm_nt(q_ref[part, lanes], k_ref[part, lanes]), 0.0)
            out = cross + _mm(scores, change)
            o_ref[part, lanes] = out
            scaled = out * lax.rsqrt(jnp.mean(out * out, axis=-1, keepdims=True) + eps_norm)
            gate = gate_ref[part, lanes]
            n_ref[part, lanes] = (
                scaled * gain_ref[...] * (gate * jax.nn.sigmoid(gate))
            ).astype(jnp.bfloat16)


def _back_local_kernel(
    heads, scal_ref, dn_ref, gate_ref, gain_ref, o_ref, q_ref, k_ref, w_ref, dg_ref, dgo_ref,
    do_ref, p_ref, carry_ref,
):
    rows = q_ref.shape[0]
    pairs = rows // SPANROWS
    row, col, same = _pair_masks()
    lower = same & (row >= col)
    gain = gain_ref[...]
    grad_outs = [[] for _ in range(heads)]
    passed = [[] for _ in range(heads)]
    for head in range(heads):
        lanes = slice(head * DK, (head + 1) * DK)
        gain_sum = jnp.zeros((1, DK), jnp.float32)
        for pair in range(pairs):
            part = slice(pair * SPANROWS, (pair + 1) * SPANROWS)
            out = o_ref[part, lanes]
            gate = gate_ref[part, lanes]
            grad_n = dn_ref[part, lanes]
            inv = lax.rsqrt(jnp.mean(out * out, axis=-1, keepdims=True) + eps_norm)
            sig = jax.nn.sigmoid(gate)
            act = gate * sig
            scaled = out * inv
            with_gain = grad_n * gain
            dg_ref[part, lanes] = (
                with_gain * scaled * (sig * (1.0 + gate * (1.0 - sig)))
            ).astype(jnp.bfloat16)
            gain_sum = gain_sum + jnp.sum(grad_n * scaled * act, axis=0, keepdims=True)
            inner = with_gain * act
            grad_out = (
                inv * inner
                - out * (inv * inv * inv) * jnp.mean(inner * out, axis=-1, keepdims=True)
            ).astype(jnp.bfloat16)
            do_ref[part, lanes] = grad_out
            scores = jnp.where(lower, _mm_nt(q_ref[part, lanes], k_ref[part, lanes]), 0.0)
            through = _mm_tn(scores, grad_out)
            p_ref[part, lanes] = through
            grad_outs[head].append(grad_out)
            passed[head].append(through)
        dgo_ref[head] = jnp.broadcast_to(gain_sum, (8, DK))
    carried = [jnp.zeros((DK, DK), jnp.float32) for _ in range(heads)]
    for span in reversed(range(rows // SPAN)):
        keep = _keep(scal_ref, span)
        rows_in = slice(span * SPAN, (span + 1) * SPAN)
        pair, half = divmod(span, SPANROWS // SPAN)
        part = slice(half * SPAN, (half + 1) * SPAN)
        for head in range(heads):
            lanes = slice(head * DK, (head + 1) * DK)
            change = passed[head][pair][part] + _mm(k_ref[rows_in, lanes], carried[head])
            carried[head] = keep * (
                carried[head]
                + _mm_tn(q_ref[rows_in, lanes], grad_outs[head][pair][part])
                - _mm_tn(w_ref[rows_in, lanes], change)
            )
    for head in range(heads):
        carry_ref[head] = carried[head]


def _back_kernel(
    heads, scal_ref, pre_q, pre_k, pre_v, halo_q, halo_k, halo_v, taps_ref, logit_ref, q_ref, k_ref,
    w_ref, t_ref, u_ref, s_ref, do_ref, p_ref, above_ref, dpre_ref, tail_ref, dhalo_ref, dtaps_ref,
    dlogit_ref, ext_ref, pad_ref,
):
    pre_refs, halo_refs = (pre_q, pre_k, pre_v), (halo_q, halo_k, halo_v)
    rows = q_ref.shape[0]
    pairs = rows // SPANROWS
    masks = _tap_masks(scal_ref, rows)
    row, col, same = _pair_masks()
    lower = same & (row >= col)
    strict = same & (row > col)
    edge, base = scal_ref[0], scal_ref[1]
    token = lax.broadcasted_iota(jnp.int32, (rows + 8, DK), 0) - 8
    back_masks = []
    for shift in range(CONV):
        good = jnp.where(token + shift >= edge, token - edge, token + base) >= 0
        back_masks.append(good.astype(jnp.float32))
    logit = logit_ref[...]
    first_head = pl.program_id(0) * heads
    carried = [above_ref[head].astype(jnp.float32) for head in range(heads)]
    changes = [[None] * (rows // SPAN) for _ in range(heads)]
    crossed = [[None] * (rows // SPAN) for _ in range(heads)]
    for span in reversed(range(rows // SPAN)):
        keep = _keep(scal_ref, span)
        part = slice(span * SPAN, (span + 1) * SPAN)
        for head in range(heads):
            lanes = slice(head * DK, (head + 1) * DK)
            above = carried[head].astype(jnp.bfloat16)
            change = (p_ref[part, lanes] + _mm(k_ref[part, lanes], above)).astype(jnp.bfloat16)
            changes[head][span] = change
            crossed[head][span] = _mm_nt(u_ref[part, lanes], above)
            carried[head] = keep * (
                carried[head]
                + _mm_tn(q_ref[part, lanes], do_ref[part, lanes])
                - _mm_tn(w_ref[part, lanes], change)
            )
    lane_index = lax.broadcasted_iota(jnp.int32, logit.shape, 1)
    grad_logit = jnp.zeros(logit.shape, jnp.float32)
    for head in range(heads):
        lanes = slice(head * DK, (head + 1) * DK)
        taps = taps_ref[:, :, lanes]
        beta = jax.nn.sigmoid(_column(logit, first_head + head))
        acts, slopes = [], []
        for which in range(3):
            mixed = _convolved(
                ext_ref.at[head * 3 + which], pre_refs[which][:, lanes], halo_refs[which][:, lanes],
                taps[which], masks,
            )
            sig = jax.nn.sigmoid(mixed)
            acts.append(mixed * sig)
            slopes.append(sig * (1.0 + mixed * (1.0 - sig)))
        query_inv = lax.rsqrt(jnp.sum(acts[0] * acts[0], axis=-1, keepdims=True) + eps_unit)
        key_inv = lax.rsqrt(jnp.sum(acts[1] * acts[1], axis=-1, keepdims=True) + eps_unit)
        query = acts[0] * query_inv
        key = acts[1] * key_inv
        value = acts[2]
        grad_q, grad_k, grad_v, grad_b = [], [], [], []
        for pair in range(pairs):
            part = slice(pair * SPANROWS, (pair + 1) * SPANROWS)
            spans = (2 * pair, 2 * pair + 1)
            q_low, k_low = q_ref[part, lanes], k_ref[part, lanes]
            u_low, do_low = u_ref[part, lanes], do_ref[part, lanes]
            change = jnp.concatenate([changes[head][span] for span in spans], axis=0)
            solved = _mm_tn(t_ref[part, lanes], change)
            solved_low = solved.astype(jnp.bfloat16)
            both = [
                _mm_nt(
                    jnp.concatenate(
                        [
                            do_low[half * SPAN : (half + 1) * SPAN],
                            solved_low[half * SPAN : (half + 1) * SPAN],
                        ],
                        axis=0,
                    ),
                    s_ref[head, span],
                )
                for half, span in enumerate(spans)
            ]
            out_state = jnp.concatenate([both[0][:SPAN], both[1][:SPAN]], axis=0)
            solved_state = jnp.concatenate([both[0][SPAN:], both[1][SPAN:]], axis=0)
            weights = jnp.where(lower, _mm_nt(do_low, u_low), 0.0).astype(jnp.bfloat16)
            grad_q.append(out_state + _mm(weights, k_low))
            grad_low = jnp.where(strict, -_mm_nt(solved_low, u_low), 0.0)
            gram = _mm_nt(k_low, k_low)
            beta_part = beta[part]
            grad_gram = (grad_low * beta_part).astype(jnp.bfloat16)
            grad_k.append(
                _mm_tn(weights, q_low)
                + jnp.concatenate([crossed[head][span] for span in spans], axis=0)
                - beta_part * solved_state
                + _mm(grad_gram, k_low)
                + _mm_tn(grad_gram, k_low)
            )
            grad_v.append(beta_part * solved)
            grad_b.append(
                jnp.sum(grad_low * gram, axis=1, keepdims=True)
                + jnp.sum(solved * value[part] - solved_state * key[part], axis=1, keepdims=True)
            )
        grad_query = jnp.concatenate(grad_q, axis=0)
        grad_key = jnp.concatenate(grad_k, axis=0)
        grad_beta = jnp.concatenate(grad_b, axis=0)
        grad_logit = grad_logit + jnp.where(
            lane_index == first_head + head, grad_beta * beta * (1.0 - beta), 0.0
        )
        grad_acts = [
            (grad_query - query * jnp.sum(query * grad_query, axis=-1, keepdims=True)) * query_inv,
            (grad_key - key * jnp.sum(key * grad_key, axis=-1, keepdims=True)) * key_inv,
            jnp.concatenate(grad_v, axis=0),
        ]
        for which in range(3):
            grad_mixed = grad_acts[which] * slopes[which]
            pad = pad_ref.at[head * 3 + which]
            ext = ext_ref.at[head * 3 + which]
            pad[0:8] = jnp.zeros((8, DK), jnp.float32)
            pad[8 : 8 + rows] = grad_mixed
            pad[8 + rows : 16 + rows] = jnp.zeros((8, DK), jnp.float32)
            total = jnp.zeros((rows + 8, DK), jnp.float32)
            for shift in range(CONV):
                tap = CONV - 1 - shift
                shifted = pad[shift : shift + rows + 8] * back_masks[shift]
                total = total + taps[which, tap : tap + 1] * shifted
                dtaps_ref[which, tap : tap + 1, lanes] = jnp.sum(
                    shifted * ext[0 : rows + 8], axis=0, keepdims=True
                )
            dhalo_ref[which, :, lanes] = total[:8]
            dpre_ref[which, :, lanes] = total[8:].astype(jnp.bfloat16)
            tail_ref[which, :, lanes] = total[rows:]

    @pl.when(pl.program_id(0) == 0)
    def _():
        dlogit_ref[...] = grad_logit

    @pl.when(pl.program_id(0) > 0)
    def _():
        dlogit_ref[...] += grad_logit


HEADS_AT_ONCE = 4


def _specs(heads, rows):
    wide = heads * DK
    return dict(
        scal=pl.BlockSpec(memory_space=pltpu.SMEM),
        flat=pl.BlockSpec((rows, wide), lambda h: (0, h)),
        three=pl.BlockSpec((3, rows, wide), lambda h: (0, 0, h)),
        edge=pl.BlockSpec((3, 8, wide), lambda h: (0, 0, h)),
        taps=pl.BlockSpec((3, CONV, wide), lambda h: (0, 0, h)),
        square=pl.BlockSpec((heads, DK, DK), lambda h: (h, 0, 0)),
        spans=pl.BlockSpec((heads, rows // SPAN, DK, DK), lambda h: (h, 0, 0, 0)),
        gain=pl.BlockSpec((1, DK), lambda h: (0, 0)),
        small=pl.BlockSpec((heads, 8, DK), lambda h: (h, 0, 0)),
    )


def _three_specs(heads, rows, total):
    def one(tall, part):
        return pl.BlockSpec((tall, heads * DK), lambda h: (0, part * (total // heads) + h))

    return [one(rows, 0)] * 3 + [one(16, part) for part in range(3)]


def _cost(microseconds):
    return pl.CostEstimate(
        flops=microseconds * 11 * 10**8,
        bytes_accessed=microseconds * 36 * 10**5,
        transcendentals=0,
    )


def _params(mebibytes=48):
    return pltpu.CompilerParams(
        dimension_semantics=("arbitrary",), vmem_limit_bytes=mebibytes * 1024 * 1024
    )


def delta_local(scal, pre, halo, taps, logits):
    rows, width = pre[0].shape
    total = width // DK
    heads = min(HEADS_AT_ONCE, total)
    sp = _specs(heads, rows)
    table = pl.BlockSpec((rows, total), lambda h: (0, 0))
    low = jax.ShapeDtypeStruct((rows, width), jnp.bfloat16)
    return pl.pallas_call(
        partial(_local_kernel, heads),
        grid=(total // heads,),
        in_specs=[sp["scal"]] + _three_specs(heads, rows, total) + [sp["taps"], table],
        out_specs=[sp["flat"]] * 5 + [sp["square"]] * 2,
        out_shape=[
            low,
            low,
            low,
            jax.ShapeDtypeStruct((rows, width), jnp.float32),
            low,
            jax.ShapeDtypeStruct((total, DK, DK), jnp.float32),
            jax.ShapeDtypeStruct((total, DK, DK), jnp.bfloat16),
        ],
        scratch_shapes=[pltpu.VMEM((3 * heads, rows + 8, DK), jnp.float32)],
        compiler_params=_params(60),
        cost_estimate=_cost(8),
        name="delta_local",
    )(scal, *pre, halo, halo, halo, taps, logits)


def delta_apply(scal, q, k, w, uv, state_in, gate, gain):
    rows, width = q.shape
    total = width // DK
    heads = min(HEADS_AT_ONCE, total)
    sp = _specs(heads, rows)
    low = jax.ShapeDtypeStruct((rows, width), jnp.bfloat16)
    return pl.pallas_call(
        partial(_apply_kernel, heads),
        grid=(total // heads,),
        in_specs=[sp["scal"]] + [sp["flat"]] * 4 + [sp["square"], sp["flat"], sp["gain"]],
        out_specs=[sp["flat"]] * 3 + [sp["spans"]],
        out_shape=[
            low,
            jax.ShapeDtypeStruct((rows, width), jnp.float32),
            low,
            jax.ShapeDtypeStruct((total, rows // SPAN, DK, DK), jnp.bfloat16),
        ],
        compiler_params=_params(60),
        cost_estimate=_cost(5),
        name="delta_apply",
    )(scal, q, k, w, uv, state_in, gate, gain)


def delta_back_local(scal, dn, gate, gain, o, q, k, w):
    rows, width = q.shape
    total = width // DK
    heads = min(HEADS_AT_ONCE, total)
    sp = _specs(heads, rows)
    low = jax.ShapeDtypeStruct((rows, width), jnp.bfloat16)
    return pl.pallas_call(
        partial(_back_local_kernel, heads),
        grid=(total // heads,),
        in_specs=[sp["scal"], sp["flat"], sp["flat"], sp["gain"]] + [sp["flat"]] * 4,
        out_specs=[sp["flat"], sp["small"], sp["flat"], sp["flat"], sp["square"]],
        out_shape=[
            low,
            jax.ShapeDtypeStruct((total, 8, DK), jnp.float32),
            low,
            jax.ShapeDtypeStruct((rows, width), jnp.float32),
            jax.ShapeDtypeStruct((total, DK, DK), jnp.float32),
        ],
        compiler_params=_params(),
        cost_estimate=_cost(8),
        name="delta_back_local",
    )(scal, dn, gate, gain, o, q, k, w)


def delta_back(scal, pre, halo, taps, logits, q, k, w, t, u, s, do, p, above):
    rows, width = pre[0].shape
    total = width // DK
    heads = min(HEADS_AT_ONCE, total)
    sp = _specs(heads, rows)
    table = pl.BlockSpec((rows, total), lambda h: (0, 0))
    edge = jax.ShapeDtypeStruct((3, 8, width), jnp.float32)
    return pl.pallas_call(
        partial(_back_kernel, heads),
        grid=(total // heads,),
        in_specs=[sp["scal"]]
        + _three_specs(heads, rows, total)
        + [sp["taps"], table]
        + [sp["flat"]] * 5
        + [sp["spans"], sp["flat"], sp["flat"], sp["square"]],
        out_specs=[sp["three"], sp["edge"], sp["edge"], sp["taps"], table],
        out_shape=[
            jax.ShapeDtypeStruct((3, rows, width), jnp.bfloat16),
            edge,
            edge,
            jax.ShapeDtypeStruct((3, CONV, width), jnp.float32),
            jax.ShapeDtypeStruct((rows, total), jnp.float32),
        ],
        scratch_shapes=[
            pltpu.VMEM((3 * heads, rows + 8, DK), jnp.float32),
            pltpu.VMEM((3 * heads, rows + 16, DK), jnp.float32),
        ],
        compiler_params=_params(),
        cost_estimate=_cost(15),
        name="delta_back",
    )(
        scal, *pre, halo, halo, halo, taps, logits, q, k, w, t, u, s, do, p, above
    )


def ring_order(count):
    return list(range(0, count, 2)) + list(range(count - 1, 0, -2))


def ring_pairs(count):
    order = ring_order(count)
    return [(order[place], order[(place + 1) % count]) for place in range(count)]


def send_up(value):
    return lax.ppermute(value, "seq", ring_pairs(lax.axis_size("seq")))


def send_down(value):
    return lax.ppermute(value, "seq", [(b, a) for a, b in ring_pairs(lax.axis_size("seq"))])


def ring_place():
    count = lax.axis_size("seq")
    index = lax.axis_index("seq")
    return jnp.where(index % 2 == 0, index // 2, count - (index + 1) // 2)


def ring_sources():
    count = lax.axis_size("seq")
    order = jnp.asarray(ring_order(count), jnp.int32)
    return jnp.take(order, (ring_place() + jnp.arange(count, dtype=jnp.int32)) % count)


def ring_targets():
    count = lax.axis_size("seq")
    order = ring_order(count)
    places = jnp.asarray([order.index(one) for one in range(count)], jnp.int32)
    return (places + count - ring_place()) % count


def _pick_kernel(pieces, index_ref, value_ref, out_ref):
    piece = out_ref.shape[1] // pieces
    for one in range(pieces):
        start = pl.multiple_of(index_ref[one] * piece, DK)
        out_ref[:, one * piece : (one + 1) * piece] = value_ref[:, pl.ds(start, piece)]


def _join_kernel(pieces, index_ref, own_ref, other_ref, out_ref):
    piece = out_ref.shape[1] // pieces
    own = (pl.program_id(0) >= pl.num_programs(0) // 2) == (index_ref[pieces] == 1)
    for one in range(pieces):
        start = pl.multiple_of(index_ref[one] * piece, DK)
        out_ref[:, one * piece : (one + 1) * piece] = jnp.where(
            own, own_ref[:, pl.ds(start, piece)], other_ref[:, pl.ds(start, piece)]
        )


def pick_columns(value, index):
    count = index.shape[0]
    rows, wide = value.shape
    piece = wide // count
    if piece % DK:
        return jnp.take(value.reshape(rows, count, piece), index, axis=1).reshape(rows, wide)
    tall = rows // 4
    return pl.pallas_call(
        partial(_pick_kernel, count),
        grid=(4,),
        in_specs=[
            pl.BlockSpec(memory_space=pltpu.SMEM),
            pl.BlockSpec((tall, wide), lambda i: (i, 0)),
        ],
        out_specs=pl.BlockSpec((tall, wide), lambda i: (i, 0)),
        out_shape=jax.ShapeDtypeStruct(value.shape, value.dtype),
        compiler_params=_params(),
        cost_estimate=_cost(3),
        name="pick_columns",
    )(index, value)


def join_columns(own, index):
    other = swap(own, "head", 1)
    bit = lax.axis_index("head") & 1
    count = index.shape[0]
    rows, wide = own.shape
    if (wide // count) % DK:
        both = jnp.where(
            bit == 0,
            jnp.concatenate([own, other], axis=0),
            jnp.concatenate([other, own], axis=0),
        )
        return pick_columns(both, index)
    tall = rows // 2
    half = pl.BlockSpec((tall, wide), lambda i: (i % 2, 0))
    return pl.pallas_call(
        partial(_join_kernel, count),
        grid=(4,),
        in_specs=[pl.BlockSpec(memory_space=pltpu.SMEM), half, half],
        out_specs=pl.BlockSpec((tall, wide), lambda i: (i, 0)),
        out_shape=jax.ShapeDtypeStruct((2 * rows, wide), own.dtype),
        compiler_params=_params(),
        cost_estimate=_cost(4),
        name="join_columns",
    )(jnp.concatenate([index, bit[None].astype(jnp.int32)]), own, other)


def low(value):
    return value.astype(jnp.bfloat16)


class Gather:
    def __init__(self, first, second):
        self.count = lax.axis_size("seq")
        self.half = self.count // 2
        self.held = ({0: first}, {0: second})

    def fresh(self, slot):
        return [self.held[slot]] if slot < 2 else []

    def send(self, slot):
        step, second = slot // 2 + 1, slot % 2
        held = self.held[second]
        back, forth = (self.count - step) % self.count, step
        keys = []
        if step < self.half or not second:
            held[back] = send_up(held[(back + 1) % self.count])
            keys.append((held, back))
        if step < self.half or second:
            held[forth] = send_down(held[forth - 1])
            keys.append((held, forth))
        return keys


class Scatter:
    def __init__(self, first, second):
        self.count = lax.axis_size("seq")
        self.half = self.count // 2
        self.terms = (first, second)
        self.got = ({}, {})

    def places(self, slot):
        step, second = slot // 2, slot % 2
        up = self.half - step - (1 if second else 0)
        down = self.half + step + (0 if second else 1)
        return up, down

    def fresh(self, slot):
        if slot > 1:
            return []
        self.first = {0: dict(zip(("up", "down"), map(self.terms[slot], self.places(slot))))}
        return [self.first]

    def send(self, slot):
        got = self.got[slot % 2]
        keys = []
        for way, send, place in zip(("up", "down"), (send_up, send_down), self.places(slot)):
            if 0 < place < self.count:
                if way in got:
                    term = self.terms[slot % 2](place)
                    term = low(term.astype(jnp.float32) + got[way].astype(jnp.float32))
                else:
                    term = self.first[0][way]
                got[way] = send(term)
                keys.append((got, way))
        return keys

    def sums(self):
        return [
            terms(0).astype(jnp.float32) + got["up"].astype(jnp.float32) + got["down"].astype(jnp.float32)
            for terms, got in zip(self.terms, self.got)
        ]


class Flow:
    def __init__(self, token):
        self.flying = []
        self.token = token

    def wait(self, values):
        keys = [one for _, _, sent in self.flying for one in sent]
        self.flying = []
        arrived, values, self.token = lax.optimization_barrier(
            ([held[key] for held, key in keys], values, self.token)
        )
        for (held, key), value in zip(keys, arrived):
            held[key] = value
        return values

    def step(self, ring, stage, values=(), most=4):
        each = lax.axis_size("seq") // 8
        for slot in range(stage * each, (stage + 1) * each):
            fresh = ring.fresh(slot)
            new = 1 if slot // 2 == ring.half - 1 else 2
            keys = []
            while self.flying and (
                sum(len(sent) for _, _, sent in self.flying) + new > most
                or any(other is ring and was <= slot - 2 for other, was, _ in self.flying)
            ):
                keys += self.flying.pop(0)[2]
            arrived, first, values, self.token = lax.optimization_barrier(
                (
                    [held[key] for held, key in keys],
                    [held[0] for held in fresh],
                    values,
                    self.token,
                )
            )
            for held, value in zip(fresh, first):
                held[0] = value
            for (held, key), value in zip(keys, arrived):
                held[key] = value
            self.flying.append((ring, slot, ring.send(slot)))
        return values


def _rows_dot_kernel(count, operands, outs, *refs):
    size = len(operands)
    value_ref = refs[0]
    weights = [refs[1 + one * count : 1 + (one + 1) * count] for one in range(size)]
    out_refs = refs[1 + size * count : -1 - size]
    held = refs[-1 - size : -1]
    sems = refs[-1]

    def copy(one, place):
        first, columns = operands[one]
        piece = weights[one][place].shape[0]
        return pltpu.make_async_copy(
            weights[one][place].at[:, pl.ds(first, columns)],
            held[one].at[pl.ds(place * piece, piece)],
            sems.at[one, place],
        )

    for one in range(size):
        for place in range(count):
            copy(one, place).start()
    for one in range(size):
        for place in range(count):
            copy(one, place).wait()
        for source, start, columns, out, at in outs:
            if source == one:
                out_refs[out][:, at : at + columns] = jnp.dot(
                    value_ref[...],
                    held[one][:, start : start + columns],
                    preferred_element_type=jnp.float32,
                ).astype(out_refs[out].dtype)


def rows_dot(value, operands, outs, shapes):
    count = len(operands[0][0])
    vmem = pl.BlockSpec(memory_space=pltpu.VMEM)
    ranges = [(first, columns) for _, first, columns in operands]
    whole = [
        jax.ShapeDtypeStruct((value.shape[1], columns), jnp.bfloat16) for _, columns in ranges
    ]
    results = pl.pallas_call(
        partial(_rows_dot_kernel, count, ranges, outs),
        in_specs=[vmem] + [pl.BlockSpec(memory_space=pl.ANY)] * (len(operands) * count),
        out_specs=[vmem] * (len(shapes) + len(whole)),
        out_shape=list(shapes) + whole,
        scratch_shapes=[pltpu.SemaphoreType.DMA((len(operands), count))],
        compiler_params=pltpu.CompilerParams(vmem_limit_bytes=60 * 1024 * 1024),
        cost_estimate=_cost(12),
        name="rows_dot",
    )(value, *[pieces[place] for pieces, _, _ in operands for place in range(count)])
    return results[: len(shapes)], results[len(shapes) :]


def _glu_early_kernel(count, *refs):
    half = count // 2
    late = (half - 1, half, half + 1)
    value_ref = refs[0]
    weights = (refs[1 : 1 + count], refs[1 + count : 1 + 2 * count])
    outs = refs[1 + 2 * count : 3 + 2 * count]
    held = refs[3 + 2 * count : 5 + 2 * count]
    sems = refs[-1]
    piece = weights[0][0].shape[0]
    places = [place for place in range(count) if place not in late]

    def copy(one, place):
        return pltpu.make_async_copy(
            weights[one][place], held[one].at[pl.ds(place * piece, piece)], sems.at[one, place]
        )

    for one in range(2):
        for place in places:
            copy(one, place).start()
    stop, again = (half - 1) * piece, (half + 2) * piece
    for one in range(2):
        held[one][stop:again] = jnp.zeros((3 * piece, held[one].shape[1]), jnp.bfloat16)
    for one in range(2):
        for place in places:
            copy(one, place).wait()
        outs[one][...] = jnp.dot(
            value_ref[:, :stop], held[one][:stop], preferred_element_type=jnp.float32
        ) + jnp.dot(value_ref[:, again:], held[one][again:], preferred_element_type=jnp.float32)


def glu_early(value, gates, ups):
    count = lax.axis_size("seq")
    vmem = pl.BlockSpec(memory_space=pltpu.VMEM)
    columns = gates[0].shape[1]
    return pl.pallas_call(
        partial(_glu_early_kernel, count),
        in_specs=[vmem] + [pl.BlockSpec(memory_space=pl.ANY)] * (2 * count),
        out_specs=[vmem] * 4,
        out_shape=[jax.ShapeDtypeStruct((value.shape[0], columns), jnp.float32)] * 2
        + [jax.ShapeDtypeStruct((value.shape[1], columns), jnp.bfloat16)] * 2,
        scratch_shapes=[pltpu.SemaphoreType.DMA((2, count))],
        compiler_params=pltpu.CompilerParams(vmem_limit_bytes=60 * 1024 * 1024),
        cost_estimate=_cost(14),
        name="glu_early",
    )(
        value,
        *[gates.get(place, gates[0]) for place in range(count)],
        *[ups.get(place, ups[0]) for place in range(count)],
    )


def _glu_late_kernel(value_ref, *refs):
    gates_refs, ups_refs = refs[:3], refs[3:6]
    gate_ref, up_ref, grad_ref, act_ref, dgate_ref, dup_ref = refs[6:]
    columns = grad_ref.shape[1]
    piece = gates_refs[0].shape[0]
    wide = 256
    for start in range(0, columns, wide):
        part = slice(start, min(start + wide, columns))
        gate, up = gate_ref[:, part], up_ref[:, part]
        for one in range(3):
            value = value_ref[:, one * piece : (one + 1) * piece]
            gate = gate + jnp.dot(
                value, gates_refs[one][:, part], preferred_element_type=jnp.float32
            )
            up = up + jnp.dot(value, ups_refs[one][:, part], preferred_element_type=jnp.float32)
        grad = grad_ref[:, part]
        sig = jax.nn.sigmoid(gate)
        act = gate * sig
        act_ref[:, part] = low(act * up)
        dgate_ref[:, part] = low(grad * up * (sig * (1.0 + gate * (1.0 - sig))))
        dup_ref[:, part] = low(grad * act)


def glu_late(value, gates, ups, sums, grad):
    rows, columns = grad.shape
    tall = rows // 4

    def by_rows(wide):
        return pl.BlockSpec((tall, wide), lambda i: (i, 0))

    whole = pl.BlockSpec(gates[0].shape, lambda i: (0, 0))
    return pl.pallas_call(
        _glu_late_kernel,
        grid=(4,),
        in_specs=[by_rows(value.shape[1])] + [whole] * 6 + [by_rows(columns)] * 3,
        out_specs=[by_rows(columns)] * 3,
        out_shape=[jax.ShapeDtypeStruct(grad.shape, jnp.bfloat16)] * 3,
        compiler_params=_params(),
        cost_estimate=_cost(8),
        name="glu_late",
    )(value, *gates, *ups, *sums, grad)


def swap(value, axis, bit):
    count = lax.axis_size(axis)
    return lax.ppermute(value, axis, [(one, one ^ bit) for one in range(count)])


def gather_round(held, bit):
    other = swap(held, "seq", bit)
    return jnp.where(
        (lax.axis_index("seq") & bit) == 0,
        jnp.concatenate([held, other], axis=0),
        jnp.concatenate([other, held], axis=0),
    )


def bits_of(axis):
    return [1 << bit for bit in range(lax.axis_size(axis).bit_length() - 1)]


def own_half(value):
    rows = value.shape[0] // 2
    return lax.dynamic_slice_in_dim(value, (lax.axis_index("head") & 1) * rows, rows, 0)


def other_half(value):
    rows = value.shape[0] // 2
    return lax.dynamic_slice_in_dim(value, (1 - (lax.axis_index("head") & 1)) * rows, rows, 0)


def both_halves(value):
    other = swap(value, "head", 1)
    return jnp.where(
        (lax.axis_index("head") & 1) == 0,
        jnp.concatenate([value, other], axis=0),
        jnp.concatenate([other, value], axis=0),
    )


def summed_pair(partial_rows):
    pair = own_half(partial_rows).astype(jnp.float32) + swap(
        other_half(low(partial_rows)), "head", 1
    ).astype(jnp.float32)
    return pair


def summed_over_head(value):
    if lax.axis_size("head") == 4:
        one, two, three = (swap(value, "head", bits) for bits in (1, 2, 3))
        return (value + one) + (two + three)
    for bit in bits_of("head"):
        value = value + swap(value, "head", bit)
    return value


def asked(total):
    bits = bits_of("head")[1:]
    for bit in bits[:-1]:
        total = total + swap(low(total), "head", bit).astype(jnp.float32)
    return total, swap(low(total), "head", bits[-1])


def summed(parts):
    return parts[0] + parts[1].astype(jnp.float32)


def chunk_of(value, index):
    piece = value.shape[-1] // lax.axis_size("seq")
    return value[..., index * piece : (index + 1) * piece]


def dot(a, b):
    return jnp.dot(a, b, preferred_element_type=jnp.float32)


def dot_tn(a, b):
    return lax.dot_general(a, b, (((0,), (0,)), ((), ())), preferred_element_type=jnp.float32)


def dot_nt(a, b):
    return lax.dot_general(a, b, (((1,), (1,)), ((), ())), preferred_element_type=jnp.float32)


def after(values, others):
    return lax.optimization_barrier((values, others))[0]


def passed_along(value, steps):
    count = lax.axis_size("seq")
    leading, last = (max(0, -steps), min(count, count - steps))
    return lax.ppermute(
        value, "seq", [(source, source + steps) for source in range(leading, last)]
    )


def adam_update(master, first_m, second_m, gradient, step_rate, decay_rate):
    first_new = beta_one * first_m + (1.0 - beta_one) * gradient
    second_new = beta_two * second_m + (1.0 - beta_two) * gradient * gradient
    first_hat = first_new / (1.0 - beta_one**STEP)
    second_hat = second_new / (1.0 - beta_two**STEP)
    master_new = master - step_rate * (
        first_hat / (jnp.sqrt(second_hat) + eps_adam) + decay_rate * master
    )
    return (master_new, first_new, second_new)


def norm_back(rows, inv, gain, grad):
    weighted = grad * gain
    mean = jnp.mean(weighted * rows, axis=-1, keepdims=True)
    return inv * weighted - rows * (inv * inv * inv) * mean


def inverse_size(rows):
    return lax.rsqrt(jnp.mean(rows * rows, axis=-1, keepdims=True) + eps_norm)


def per_device(
    block_input, cotangent, lengths,
    proj_master, proj_first, proj_second,
    beta_master, beta_first, beta_second,
    conv_master, conv_first, conv_second,
    out_master, out_first, out_second,
    mlp_master, mlp_first, mlp_second,
    down_master, down_first, down_second,
    gains_master, gains_first, gains_second,
):
    bf16, f32 = jnp.bfloat16, jnp.float32
    count = lax.axis_size("seq")
    seq_index = lax.axis_index("seq")
    rows = block_input.shape[0]
    width = proj_master.shape[2]
    units = mlp_master.shape[2]
    shard = proj_master.shape[1]
    heads = width // DK
    scal = jnp.stack([lengths[0] - seq_index * rows, seq_index * rows]).astype(jnp.int32)
    flow = Flow(lengths)
    sizes = [conv_master.size, beta_master.size, gains_master.size]
    packed = low(
        jnp.concatenate(
            [conv_master.reshape(-1), beta_master.reshape(-1), gains_master.reshape(-1)]
        )
    )
    small = jnp.pad(packed, (0, -packed.size % 2048))[None]
    seq_bits = bits_of("seq")
    small = gather_round(small, seq_bits[0])
    proj_low = low(proj_master)
    ring_p = Gather(
        jnp.concatenate([proj_low[0], proj_low[1]], axis=1),
        jnp.concatenate([proj_low[2], proj_low[3]], axis=1),
    )
    flow.step(ring_p, 0)
    flow.step(ring_p, 1)
    cut = (units + width) // 2 // DK * DK
    rest = units - cut
    down_low = jnp.transpose(low(down_master))
    out_low = jnp.transpose(low(out_master))
    mlp_low = low(mlp_master)
    sources, targets = ring_sources(), ring_targets()
    x_ring = pick_columns(block_input, sources)
    dy_ring = pick_columns(cotangent, sources)
    x_rows = x_ring.astype(f32)
    x_inv = inverse_size(x_rows)
    x_ring, dy_ring, x_inv = flow.step(ring_p, 2, (x_ring, dy_ring, x_inv))
    x_rows = x_ring.astype(f32)
    small = flow.step(ring_p, 3, small)
    ring_do = Gather(
        down_low[:, :cut], jnp.concatenate([down_low[:, cut:], out_low], axis=1)
    )
    ring_m = Gather(mlp_low[0], mlp_low[1])
    small = gather_round(small, seq_bits[1])
    flow.step(ring_p, 4)
    ring_do.held[0][0], ring_do.held[1][0], ring_m.held[0][0], ring_m.held[1][0], small = flow.step(
        ring_p,
        5,
        (ring_do.held[0][0], ring_do.held[1][0], ring_m.held[0][0], ring_m.held[1][0], small),
    )
    flow.step(ring_p, 6)
    for bit in seq_bits[2:]:
        small = gather_round(small, bit)
    small = flow.step(ring_p, 7, small)
    conv_all = small[:, : sizes[0]].reshape(count, 3, CONV, -1)
    taps = jnp.transpose(conv_all, (1, 2, 0, 3)).reshape(3, CONV, width).astype(f32)
    beta_all = small[:, sizes[0] : sizes[0] + sizes[1]].reshape(D, heads)
    gains_all = small[:, sizes[0] + sizes[1] : sum(sizes)].reshape(-1)
    columns = jnp.concatenate([gains_all[: 2 * D].reshape(2, D), jnp.transpose(beta_all)], axis=0)
    columns = jnp.take(columns.reshape(2 + heads, count, -1), sources, axis=1).reshape(-1, D)
    gain_a = columns[0:1].astype(f32)
    gain_m = columns[1:2].astype(f32)
    w_beta = columns[2:]
    gain_o = gains_all[2 * D :].astype(f32)[None]
    hidden = (x_rows * x_inv * gain_a).astype(bf16)
    hidden = flow.step(ring_do, 0, hidden)
    logits = dot_nt(hidden, w_beta)
    logits = flow.step(ring_do, 1, logits)
    w_qk, w_vg = ring_p.held
    low_rows = jax.ShapeDtypeStruct((rows, width), bf16)
    (pre_q, pre_k, pre_v, gate), (w_qk, w_vg) = rows_dot(
        hidden,
        [(w_qk, 0, 2 * width), (w_vg, 0, 2 * width)],
        [(0, 0, width, 0, 0), (0, width, width, 1, 0), (1, 0, width, 2, 0), (1, width, width, 3, 0)],
        [low_rows] * 3 + [jax.ShapeDtypeStruct((rows, width), f32)],
    )
    pre = (pre_q, pre_k, pre_v)
    pre, gate = flow.step(ring_do, 2, (pre, gate))
    halo = passed_along(jnp.concatenate([one[rows - 16 :] for one in pre], axis=1), 1)
    halo = flow.step(ring_do, 3, halo)
    q, k, w, uv, t, state_add, state_map = delta_local(scal, pre, halo, taps, logits)
    state_add, state_map = flow.step(ring_do, 4, (state_add, state_map))
    hops = -(-5 * count // 8) - 1
    state_in = passed_along(low(state_add), 1)

    def hop(state):
        moved = jnp.einsum("hij,hjk->hik", state_map, state, preferred_element_type=f32)
        return passed_along(low(moved + state_add), 1)

    state_in = flow.step(ring_do, 5, state_in)
    third = (hops - 1) // 3
    for _ in range(third):
        state_in = hop(state_in)
    state_in = flow.step(ring_do, 6, state_in)
    for _ in range(third):
        state_in = hop(state_in)
    state_in = flow.step(ring_do, 7, state_in)
    for _ in range(hops - 1 - 2 * third):
        state_in = hop(state_in)
    state_in = flow.step(ring_m, 0, state_in)
    normed, out_rows, change, states = delta_apply(scal, q, k, w, uv, state_in, gate, gain_o)
    normed = flow.step(ring_m, 1, normed)
    w_do_a, w_do_b = ring_do.held
    (grad_act,), (w_down_a, w_down_b, w_out) = rows_dot(
        dy_ring,
        [(w_do_a, 0, cut), (w_do_b, 0, rest), (w_do_b, rest, width)],
        [(0, 0, cut, 0, 0), (1, 0, rest, 0, cut)],
        [jax.ShapeDtypeStruct((rows, units), f32)],
    )
    w_out, normed, grad_act = flow.step(ring_m, 2, (w_out, normed, grad_act), most=2)
    pair = summed_pair(low(dot_nt(normed, w_out)))
    pair = flow.step(ring_m, 3, pair)
    parts = asked(pair)
    flow.step(ring_m, 4)
    parts = flow.step(ring_m, 5, parts)
    x_one = own_half(x_rows) + summed(parts)
    one_inv = inverse_size(x_one)
    h_two = both_halves(low(x_one * one_inv * gain_m))
    h_two, x_one = flow.step(ring_m, 6, (h_two, x_one))
    gates, ups = ring_m.held
    half = count // 2
    *sums, w_mlp_g, w_mlp_u = glu_early(
        h_two,
        {one: piece for one, piece in gates.items() if abs(one - half) > 1},
        {one: piece for one, piece in ups.items() if abs(one - half) > 1},
    )
    sums, w_mlp_g, w_mlp_u, h_two = flow.step(ring_m, 7, (sums, w_mlp_g, w_mlp_u, h_two))
    late = (half - 1, half, half + 1)
    shard = proj_master.shape[1]
    act_low, grad_gate_u, grad_up_u = glu_late(
        h_two[:, late[0] * shard : (late[-1] + 1) * shard],
        [gates[one] for one in late],
        [ups[one] for one in late],
        sums,
        grad_act,
    )
    def rows_of(value):
        piece = value.shape[0] // count
        return lambda one: value[one * piece : (one + 1) * piece]

    back_m = Scatter(
        rows_of(low(dot_tn(h_two, grad_gate_u))), rows_of(low(dot_tn(h_two, grad_up_u)))
    )
    flow.step(back_m, 0)
    grad_gate_u, grad_up_u, act_low, w_mlp_g, w_mlp_u = flow.step(
        back_m, 1, (grad_gate_u, grad_up_u, act_low, w_mlp_g, w_mlp_u)
    )
    for one in late:
        w_mlp_g = lax.dynamic_update_slice_in_dim(w_mlp_g, gates[one], one * shard, 0)
        w_mlp_u = lax.dynamic_update_slice_in_dim(w_mlp_u, ups[one], one * shard, 0)
    part = low(dot_nt(grad_gate_u, w_mlp_g) + dot_nt(grad_up_u, w_mlp_u))
    part = flow.step(back_m, 2, part)
    pair, act_low = flow.step(back_m, 3, (summed_pair(part), act_low))
    parts = asked(pair)
    part = low(dot_nt(act_low[:, :cut], w_down_a) + dot_nt(act_low[:, cut:], w_down_b))
    part = flow.step(back_m, 4, part)
    parts, part = flow.step(back_m, 5, (parts, part))
    mlp_pair = summed_pair(part)
    grad_h_two = summed(parts)
    grad_gain_m = 0.5 * jnp.sum(grad_h_two * x_one * one_inv, axis=0, keepdims=True)
    grad_x_one = own_half(dy_ring).astype(f32) + norm_back(x_one, one_inv, gain_m, grad_h_two)
    grad_attn = both_halves(low(grad_x_one))
    grad_normed = dot(grad_attn, w_out)
    grad_normed, grad_attn, mlp_pair, act_low = flow.step(
        back_m, 6, (grad_normed, grad_attn, mlp_pair, act_low)
    )
    mlp_parts = asked(mlp_pair)
    grad_gate, grad_gain_o, grad_out, through, carry = delta_back_local(
        scal, grad_normed, gate, gain_o, out_rows, q, k, w
    )
    grad_gate, carry, grad_attn, act_low = flow.step(
        back_m, 7, (grad_gate, carry, grad_attn, act_low)
    )
    grad_do_a = low(dot_tn(dy_ring, act_low[:, :cut]))
    grad_do_b = jnp.concatenate(
        [low(dot_tn(dy_ring, act_low[:, cut:])), low(dot_tn(grad_attn, normed))], axis=1
    )
    back_do = Scatter(rows_of(grad_do_a), rows_of(grad_do_b))

    def hop_back(state):
        moved = jnp.einsum("hji,hjk->hik", state_map, state, preferred_element_type=f32)
        return passed_along(low(moved + carry), -1)

    grad_gate, carry = flow.step(back_do, 0, (grad_gate, carry))
    above = passed_along(low(carry), -1)
    above, mlp_parts = flow.step(back_do, 1, (above, mlp_parts))
    for _ in range(third):
        above = hop_back(above)
    above = flow.step(back_do, 2, above)
    for _ in range(third):
        above = hop_back(above)
    above = flow.step(back_do, 3, above)
    for _ in range(hops - 1 - 2 * third):
        above = hop_back(above)
    above, mlp_sum = flow.step(back_do, 4, (above, summed(mlp_parts)))
    grad_pre, tail, back_halo, grad_taps, grad_logits = delta_back(
        scal, pre, halo, taps, logits, q, k, w, t, change, states, grad_out, through, above
    )
    grad_pre, tail, back_halo, grad_taps, grad_logits = flow.wait(
        (grad_pre, tail, back_halo, grad_taps, grad_logits)
    )
    flow.step(back_do, 5)
    flow.step(back_do, 6)
    fixed = low(tail + passed_along(back_halo, -1))
    grad_logits = low(grad_logits)
    grad_pre = lax.dynamic_update_slice_in_dim(grad_pre, fixed, rows - 8, 1)
    grad_qk = jnp.concatenate([grad_pre[0], grad_pre[1]], axis=1)
    grad_vg = jnp.concatenate([grad_pre[2], grad_gate], axis=1)
    grad_w_qk = low(dot_tn(hidden, grad_qk))
    grad_w_qk, grad_qk, grad_vg, grad_logits, grad_taps = flow.step(
        back_do, 7, (grad_w_qk, grad_qk, grad_vg, grad_logits, grad_taps)
    )
    grad_beta = dot_tn(grad_logits, hidden)
    grad_conv = jnp.transpose(
        grad_taps.reshape(3, CONV, count, width // count), (2, 0, 1, 3)
    ).reshape(count, -1)
    grad_hidden = low(
        dot_nt(grad_qk, w_qk) + dot_nt(grad_vg, w_vg) + dot(grad_logits, w_beta)
    )
    grad_gain_a = jnp.sum(grad_hidden.astype(f32) * x_rows * x_inv, axis=0, keepdims=True)
    stacked = jnp.concatenate([grad_gain_a, grad_gain_m, grad_beta], axis=0)
    stacked = jnp.take(stacked.reshape(2 + heads, count, -1), targets, axis=1).reshape(-1, D)
    grad_gains = jnp.concatenate(
        [stacked[:2].reshape(-1), jnp.sum(grad_gain_o[:, 0], axis=0)]
    ).reshape(count, -1)
    grad_beta = jnp.transpose(stacked[2:]).reshape(count, -1)
    small = jnp.stack(
        [
            jnp.pad(low(one), ((0, 0), (0, 2 * width - one.shape[1])))
            for one in (grad_conv, grad_beta, grad_gains)
        ],
        axis=1,
    )
    small = jnp.pad(jnp.take(small, sources, axis=0), ((0, 0), (0, 13), (0, 0)))
    grad_w_vg = low(dot_tn(hidden, grad_vg)).reshape(count, -1, 2 * width)
    grad_w_vg = jnp.concatenate([grad_w_vg, small], axis=1)
    back_p = Scatter(rows_of(grad_w_qk), lambda one: grad_w_vg[one])
    flow.step(back_p, 0)
    flow.step(back_p, 1)
    grad_hidden, mlp_master = flow.step(back_p, 2, (grad_hidden, mlp_master))
    pair = summed_pair(grad_hidden)
    pair, down_master, out_master = flow.step(back_p, 3, (pair, down_master, out_master))
    parts = asked(pair)
    mlp_g_sum, mlp_u_sum = back_m.sums()
    mlp_new, mlp_first_new, mlp_second_new = adam_update(
        mlp_master, mlp_first, mlp_second, jnp.stack([mlp_g_sum, mlp_u_sum]),
        rate_matrix, decay_matrix,
    )
    mlp_new, mlp_first_new, mlp_second_new = flow.step(
        back_p, 4, (mlp_new, mlp_first_new, mlp_second_new)
    )
    do_a_sum, do_b_sum = back_do.sums()
    summed_down = jnp.transpose(jnp.concatenate([do_a_sum, do_b_sum[:, :rest]], axis=1))
    out_sum = jnp.transpose(do_b_sum[:, rest:])
    down_new, down_first_new, down_second_new = adam_update(
        down_master, down_first, down_second, summed_down, rate_down, decay_matrix
    )
    out_new, out_first_new, out_second_new = adam_update(
        out_master, out_first, out_second, out_sum, rate_matrix, decay_matrix
    )
    mlp_sum, down_new, down_first_new, down_second_new = flow.step(
        back_p, 5, (mlp_sum, down_new, down_first_new, down_second_new)
    )
    result = join_columns(x_one + mlp_sum, targets)
    parts, result, out_new, out_first_new, out_second_new = flow.step(
        back_p, 6, (parts, result, out_new, out_first_new, out_second_new)
    )
    grad_x_rest = norm_back(own_half(x_rows), own_half(x_inv), gain_a, summed(parts))
    input_half = grad_x_one + grad_x_rest
    input_grad = flow.step(back_p, 7, join_columns(input_half, targets))
    qk_sum, vg_sum = back_p.sums()
    small_sum = [vg_sum[shard + one, : sizes[one]] for one in range(3)]
    vg_sum = vg_sum[:shard]
    gains_sum = small_sum[2]
    gains_sum = summed_over_head(gains_sum)
    summed_conv = small_sum[0].reshape(conv_master.shape)
    summed_beta = small_sum[1].reshape(beta_master.shape)
    summed_proj = jnp.stack(
        [qk_sum[:, :width], qk_sum[:, width:], vg_sum[:, :width], vg_sum[:, width:]]
    )
    proj_new, proj_first_new, proj_second_new = adam_update(
        proj_master, proj_first, proj_second, summed_proj, rate_matrix, decay_matrix
    )
    beta_new, beta_first_new, beta_second_new = adam_update(
        beta_master, beta_first, beta_second, summed_beta, rate_beta, decay_matrix
    )
    conv_new, conv_first_new, conv_second_new = adam_update(
        conv_master, conv_first, conv_second, summed_conv, rate_conv, decay_matrix
    )
    gains_new, gains_first_new, gains_second_new = adam_update(
        gains_master, gains_first, gains_second, gains_sum, rate_gains, 0.0
    )
    return (
        result,
        input_grad,
        proj_new, proj_first_new, proj_second_new, proj_new.astype(bf16),
        beta_new, beta_first_new, beta_second_new, beta_new.astype(bf16),
        conv_new, conv_first_new, conv_second_new, conv_new.astype(bf16),
        out_new, out_first_new, out_second_new, out_new.astype(bf16),
        mlp_new, mlp_first_new, mlp_second_new, mlp_new.astype(bf16),
        down_new, down_first_new, down_second_new, down_new.astype(bf16),
        gains_new, gains_first_new, gains_second_new,
    )


def solution(mesh):
    rows = P("seq", None)
    proj = P(None, "seq", "head")
    tall = P("seq", "head")
    conv = P(None, None, ("head", "seq"))
    flat = P("head", "seq")
    gains = P("seq")
    return jax.shard_map(
        per_device,
        mesh=mesh,
        in_specs=(rows, rows, P())
        + (proj,) * 3
        + (tall,) * 3
        + (conv,) * 3
        + (flat,) * 3
        + (proj,) * 3
        + (flat,) * 3
        + (gains,) * 3,
        out_specs=(rows, rows)
        + (proj,) * 4
        + (tall,) * 4
        + (conv,) * 4
        + (flat,) * 4
        + (proj,) * 4
        + (flat,) * 4
        + (gains,) * 3,
        check_vma=False,
    )
```
